128 devices in a mesh: ctx: 16 (over x, y_lo, core), tp: 8 (over y_hi, z).
Axes of the slice: x: 4, y: 4 (y_hi: 2, y_lo: 2; y = y_hi * 2 + y_lo), z: 4, core: 2. Of those that a mesh axis runs over, the one named last changes fastest.
Arguments:
- frames: bfloat16 [3072, 4096], P('ctx'), may hold values from -6 to 6
- frame_pos: int32 [3072], replicated, may hold values from 0 to 3071, as said below
- codes: int32 [3072, 8], P('ctx'), may hold values from 0 to 2047
- loss_grad: float32 [3072, 8], P('ctx'), may hold values from -6 to 6
- w_query: bfloat16 [4096, 2048], P(None, 'tp'), may hold values from -0.15625 to 0.15625
- w_key: bfloat16 [4096, 2048], P(None, 'tp'), may hold values from -0.15625 to 0.15625
- w_value: bfloat16 [4096, 2048], P(None, 'tp'), may hold values from -0.09375 to 0.09375
- w_out: bfloat16 [2048, 4096], P('tp'), may hold values from -0.125 to 0.125
- w_depth_in: bfloat16 [4096, 1024], P('tp'), may hold values from -0.09375 to 0.09375
- code_embed: bfloat16 [7, 2048, 1024], P(None, 'tp'), may hold values from -8 to 8
- code_head: bfloat16 [8, 1024, 2048], P(None, None, 'tp'), may hold values from -0.6 to 0.6
Outputs:
- token_loss: float32 [3072, 8], P('ctx')
- grad_query: float32 [4096, 2048], P('ctx', 'tp')
- grad_key: float32 [4096, 2048], P('ctx', 'tp')
- grad_value: float32 [4096, 2048], P('ctx', 'tp')
- grad_out: float32 [2048, 4096], P('tp', 'ctx')
- grad_depth_in: float32 [4096, 1024], P('tp', 'ctx')
- grad_head: float32 [8, 1024, 2048], P(None, 'ctx', 'tp')
The draws below stay inside these ranges and needn't reach their ends.
Inputs may be any that keep to these rules, and one draw needn't show every extreme that they name: frame_pos holds each of 0 to 3071 once; every aligned run of 96 entries holds consecutive increasing positions.
All inputs are finite; a program needn't handle non-finite values.
Results may differ from the reference program's by a relative error of at most 0.035.
Values may be sent and summed in bfloat16 or wider, within the bound.
No kernel may reach another device: no remote copies, remote signals or barrier semaphores. Data moves between devices by JAX's collectives and lax.ppermute only.
A program may use at most 128 MiB of HBM per device.

```python
import math
import jax
import jax.numpy as jnp
from jax import lax

D = 4096
HEADS = 16
HD = 128
HQ = 2048
DD = 1024
V = 2048
CB = 8
FR_DEV = 192
BLK = 96
FRAMES = 3072
N_CTX = 16
N_TP = 8


def drawn_weight(key):
    return jnp.clip(jax.random.normal(key, (D, HQ), jnp.float32), -6.0, 6.0) * D ** (-0.5)


def draw_frame_pos(key, part):
    key = jax.random.fold_in(key, 7)
    block_total = FRAMES // BLK
    block_order = jax.random.permutation(key, block_total).astype(jnp.int32)
    within = jnp.arange(FRAMES, dtype=jnp.int32)
    return block_order[within // BLK] * BLK + within % BLK


def draw_frames(key, part):
    key = jax.random.fold_in(key, 11)
    return jnp.clip(jax.random.normal(key, (FRAMES, D), jnp.float32), -6.0, 6.0).astype(jnp.bfloat16)


def draw_w_query(key, part):
    key = jax.random.fold_in(key, 13)
    return drawn_weight(key).astype(jnp.bfloat16)


def draw_w_key(key, part):
    key = jax.random.fold_in(key, 17)
    return drawn_weight(key).astype(jnp.bfloat16)


def draw_code_embed(key, part):
    key = jax.random.fold_in(key, 19)
    return jnp.clip(jax.random.normal(key, (CB - 1, V, DD), jnp.float32), -6.0, 6.0).astype(jnp.bfloat16)


def draw_code_head(key, part):
    key = jax.random.fold_in(key, 23)
    return jnp.clip(0.1 * jax.random.normal(key, (CB, DD, V), jnp.float32), -0.6, 0.6).astype(jnp.bfloat16)


def with_ends(array, stream_key, low, top_value):
    index_at = [jax.random.randint(jax.random.fold_in(stream_key, axis), (), 0, length) for axis, length in enumerate(array.shape)]
    main_axis = array.shape.index(max(array.shape))
    neighbour = index_at[:main_axis] + [(index_at[main_axis] + 1) % array.shape[main_axis]] + index_at[main_axis + 1:]
    return array.at[tuple(index_at)].set(low).at[tuple(neighbour)].set(top_value)


def block_levels(key, dims, cuts, least, top_value):
    level, own = 1.0, jax.random.fold_in(key, 6)
    for axis_at, parts in cuts:
        heights = jnp.exp(jax.random.uniform(jax.random.fold_in(own, axis_at), (parts,), jnp.float32, least / len(cuts), top_value / len(cuts)))
        level = level * jnp.repeat(heights, dims[axis_at] // parts).reshape([-1 if axis == axis_at else 1 for axis in range(len(dims))])
    return level


def bell_draw(stream_key, extent, scale, reach, cuts=(), kind=jnp.bfloat16):
    loudness = block_levels(stream_key, extent, cuts, -0.22, 0.18) if cuts else 1.0
    entries = jax.random.normal(stream_key, extent, jnp.float32) * scale * loudness
    return jnp.minimum(jnp.maximum(entries, -reach), reach).astype(kind)


def setup_inputs(seed: int = 0) -> dict:
    key_list = jax.random.split(jax.random.key(seed), 12)
    frames = draw_frames(jax.random.fold_in(key_list[11], 71), 0)
    frame_pos = draw_frame_pos(jax.random.fold_in(key_list[11], 71), 0)
    codes = with_ends(jax.random.randint(key_list[2], (FRAMES, CB), 0, V), jax.random.fold_in(key_list[2], 1), 0, V - 1).astype(jnp.int32)
    loss_grad = bell_draw(key_list[3], (FRAMES, CB), 1.0, 6.0, ((0, 16),), jnp.float32)
    w_query = draw_w_query(jax.random.fold_in(key_list[11], 71), 0)
    w_key = draw_w_key(jax.random.fold_in(key_list[11], 71), 0)
    w_value = bell_draw(key_list[6], (D, HQ), D ** -0.5, 0.09375, ((1, 8),))
    w_out = bell_draw(key_list[7], (HQ, D), HQ ** -0.5, 0.125, ((0, 8),))
    w_depth_in = bell_draw(key_list[8], (D, DD), D ** -0.5, 0.09375, ((0, 8),))
    code_embed = draw_code_embed(jax.random.fold_in(key_list[11], 71), 0)
    code_head = draw_code_head(jax.random.fold_in(key_list[11], 71), 0)
    return dict(frames=frames, frame_pos=frame_pos, codes=codes, loss_grad=loss_grad, w_query=w_query, w_key=w_key, w_value=w_value, w_out=w_out, w_depth_in=w_depth_in, code_embed=code_embed, code_head=code_head)


EPS = 1e-05
NEG = -1e+30

def rms_rows(values):
    return values * lax.rsqrt(lax.optimization_barrier(jnp.mean(values * values, axis=-1, keepdims=True)) + EPS)

def rounded(values):
    return lax.optimization_barrier(values.astype(jnp.bfloat16)).astype(jnp.float32)

def probabilities(query_h, key_h, allowed):
    scores = jnp.dot(query_h, key_h.T, preferred_element_type=jnp.float32) * (1.0 / math.sqrt(HD))
    scores = jnp.where(allowed, scores, NEG)
    weights = jnp.exp(scores - lax.optimization_barrier(jnp.max(scores, axis=-1, keepdims=True)))
    return (weights / lax.optimization_barrier(jnp.sum(weights, axis=-1, keepdims=True))).astype(jnp.bfloat16)

def block_sums(left, right):
    running_sum = jnp.zeros((left.shape[1], right.shape[1]), jnp.float32)
    for block_index in range(N_CTX):
        first_row = block_index * FR_DEV
        running_sum = running_sum + rounded(jnp.dot(left[first_row:first_row + FR_DEV].T, right[first_row:first_row + FR_DEV], preferred_element_type=jnp.float32))
    return running_sum

def reference(frames, frame_pos, codes, loss_grad, w_query, w_key, w_value, w_out, w_depth_in, code_embed, code_head):
    normed = rms_rows(frames.astype(jnp.float32)).astype(jnp.bfloat16)
    queries = jnp.dot(normed, w_query, preferred_element_type=jnp.float32).astype(jnp.bfloat16)
    key_rows = jnp.dot(normed, w_key, preferred_element_type=jnp.float32).astype(jnp.bfloat16)
    value_rows = jnp.dot(normed, w_value, preferred_element_type=jnp.float32).astype(jnp.bfloat16)
    allowed = frame_pos[None, :] <= frame_pos[:, None]

    def heads_first(matrix):
        return matrix.reshape(FRAMES, HEADS, HD).transpose(1, 0, 2)

    def heads_last(stacked):
        return stacked.transpose(1, 0, 2).reshape(FRAMES, HQ)

    def head_forward(operands):
        query_h, key_h, value_h = operands
        return jnp.dot(probabilities(query_h, key_h, allowed), value_h, preferred_element_type=jnp.float32).astype(jnp.bfloat16)
    attended = heads_last(lax.map(head_forward, (heads_first(queries), heads_first(key_rows), heads_first(value_rows))))
    head_cols = HQ // N_TP
    feat_cols = D // N_TP
    vocab_cols = V // N_TP
    context = jnp.zeros((FRAMES, D), jnp.float32)
    for shard_index in range(N_TP):
        first_col = shard_index * head_cols
        context = context + rounded(jnp.dot(attended[:, first_col:first_col + head_cols], w_out[first_col:first_col + head_cols], preferred_element_type=jnp.float32))
    context = context.astype(jnp.bfloat16)
    embedded = jnp.stack([code_embed[level_index][codes[:, level_index]] for level_index in range(CB - 1)], axis=1).astype(jnp.float32)
    owners = codes[:, :CB - 1] // vocab_cols
    depth_in = jnp.zeros((FRAMES, CB, DD), jnp.float32)
    for shard_index in range(N_TP):
        first_col = shard_index * feat_cols
        base_term = jnp.dot(context[:, first_col:first_col + feat_cols], w_depth_in[first_col:first_col + feat_cols], preferred_element_type=jnp.float32)
        picked = jnp.where((owners == shard_index)[:, :, None], embedded, jnp.zeros_like(embedded))
        depth_in = depth_in + rounded(jnp.concatenate([base_term[:, None], base_term[:, None] + picked], axis=1))
    inverse_rms = lax.rsqrt(lax.optimization_barrier(jnp.mean(depth_in * depth_in, axis=-1, keepdims=True)) + EPS)
    scaled = depth_in * inverse_rms
    unit_rows = scaled.astype(jnp.bfloat16)
    vocab_ids = jnp.arange(V, dtype=jnp.int32)

    def codebook(operands):
        level_units, level_head, level_target, level_cotangent = operands
        logits = jnp.dot(level_units, level_head, preferred_element_type=jnp.float32)
        peak_value = lax.optimization_barrier(jnp.max(logits, axis=-1, keepdims=True))
        exp_terms = jnp.exp(logits - peak_value)
        denominator = lax.optimization_barrier(jnp.sum(exp_terms, axis=-1, keepdims=True))
        is_target = level_target[:, None] == vocab_ids[None, :]
        target_logit = lax.optimization_barrier(jnp.sum(jnp.where(is_target, logits, jnp.zeros_like(logits)), axis=-1))
        level_loss = jnp.log(denominator[:, 0]) + peak_value[:, 0] - target_logit
        dlogits = (level_cotangent[:, None] * (exp_terms / denominator - is_target.astype(jnp.float32))).astype(jnp.bfloat16)
        level_grad = block_sums(level_units, dlogits)
        unit_grad = jnp.zeros((FRAMES, DD), jnp.float32)
        for shard_index in range(N_TP):
            first_col = shard_index * vocab_cols
            unit_grad = unit_grad + rounded(jnp.dot(dlogits[:, first_col:first_col + vocab_cols], level_head[:, first_col:first_col + vocab_cols].T, preferred_element_type=jnp.float32))
        return (level_loss, level_grad, unit_grad)
    losses, grad_head, unit_grads = lax.map(codebook, (unit_rows.transpose(1, 0, 2), code_head, codes.T, loss_grad.T))
    token_loss = losses.T
    unit_grad = unit_grads.transpose(1, 0, 2)
    depth_grad = inverse_rms * (unit_grad - scaled * lax.optimization_barrier(jnp.mean(unit_grad * scaled, axis=-1, keepdims=True)))
    summed_grad = lax.optimization_barrier(jnp.sum(depth_grad, axis=1)).astype(jnp.bfloat16)
    grad_depth_in = block_sums(context, summed_grad)
    context_grad = jnp.dot(summed_grad, w_depth_in.T, preferred_element_type=jnp.float32).astype(jnp.bfloat16)
    attended_grad = jnp.dot(context_grad, w_out.T, preferred_element_type=jnp.float32).astype(jnp.bfloat16)

    def head_backward(operands):
        query_h, key_h, value_h, grad_h = operands
        prob_weights = probabilities(query_h, key_h, allowed)
        prob_grad = jnp.dot(grad_h, value_h.T, preferred_element_type=jnp.float32)
        centre = lax.optimization_barrier(jnp.sum(prob_weights.astype(jnp.float32) * prob_grad, axis=-1, keepdims=True))
        score_grad = (prob_weights.astype(jnp.float32) * (prob_grad - centre) * (1.0 / math.sqrt(HD))).astype(jnp.bfloat16)
        query_grad = jnp.dot(score_grad, key_h, preferred_element_type=jnp.float32).astype(jnp.bfloat16)
        key_grad = block_sums(score_grad, query_h).astype(jnp.bfloat16)
        value_grad = block_sums(prob_weights, grad_h).astype(jnp.bfloat16)
        return (query_grad, key_grad, value_grad)
    backward_heads = lax.map(head_backward, (heads_first(queries), heads_first(key_rows), heads_first(value_rows), heads_first(attended_grad)))
    query_grad, key_grad, value_grad = [heads_last(stacked_grad) for stacked_grad in backward_heads]
    grad_query = jnp.dot(normed.T, query_grad, preferred_element_type=jnp.float32)
    grad_key = jnp.dot(normed.T, key_grad, preferred_element_type=jnp.float32)
    grad_value = jnp.dot(normed.T, value_grad, preferred_element_type=jnp.float32)
    grad_out = jnp.dot(attended.T, context_grad, preferred_element_type=jnp.float32)
    return (token_loss, grad_query, grad_key, grad_value, grad_out, grad_depth_in, grad_head)
```

```python
import math

import jax
import jax.numpy as jnp
from jax import lax
from jax.sharding import Mesh
from jax.sharding import PartitionSpec as P

HD = 128
EPS = 1e-05
NEG = -1e30
CTX = ("x", "yl", "core")
CHIPS = ("x", "yl")
TP = ("yh", "z")
ALL = CTX + TP
BF = jnp.bfloat16
F32 = jnp.float32


def rms_rows(values):
    return values * lax.rsqrt(jnp.mean(values * values, axis=-1, keepdims=True) + EPS)


def dot(left, right, dims):
    return lax.dot_general(left, right, (dims, ((), ())), preferred_element_type=F32)


def exchange(parts, axes):
    return lax.all_to_all(parts, axes, 0, 0, tiled=True)


def spread(block, axes, count):
    return exchange(jnp.broadcast_to(block[None], (count,) + block.shape), axes)


def total(parts):
    return jnp.sum(parts.astype(F32), axis=0)


def swap_core(block):
    return lax.ppermute(block, "core", [(0, 1), (1, 0)])


def all_sum_tp(part):
    rows, cols = part.shape
    pieces = exchange(part.reshape(8, rows // 8, cols), TP)
    own = total(pieces).astype(BF)
    return spread(own, TP, 8).reshape(rows, cols)


def per_device(
    frames,
    frame_pos,
    codes,
    loss_grad,
    w_query,
    w_key,
    w_value,
    w_out,
    w_depth_in,
    code_embed,
    code_head,
):
    rows = frames.shape[0]
    core = lax.axis_index("core")
    ctx = lax.axis_index(CTX)
    tp = lax.axis_index(TP)
    scale = 1.0 / math.sqrt(HD)
    first = core == 0

    depth_cols = lax.dynamic_slice_in_dim(w_depth_in, ctx * 64, 64, 1).T
    depth_cols = lax.all_gather(depth_cols, TP, axis=1, tiled=True)
    fold_cols = dot(depth_cols, w_out, ((1,), (1,))).astype(BF)
    fold = lax.all_gather(fold_cols, CTX, axis=0, tiled=True)
    depth_half = lax.dynamic_slice_in_dim(w_depth_in, core * 256, 256, 0)
    moves = [
        (c * 8 + t, (2 * t + c % 2) * 8 + c // 2) for c in range(16) for t in range(8)
    ]
    depth_rows = lax.ppermute(depth_half, ALL, moves)

    head_own = exchange(lax.dynamic_slice_in_dim(code_head, core * 512, 512, 1), TP)
    head_other = swap_core(head_own)
    embed_half = lax.dynamic_slice_in_dim(code_embed, core * 128, 128, 1)
    embed_half = jnp.concatenate([jnp.zeros_like(embed_half[:1]), embed_half], axis=0)
    embed_own = exchange(embed_half, TP)
    embed_other = swap_core(embed_own)

    normed = rms_rows(frames.astype(F32)).astype(BF)
    normed_pair = jnp.concatenate([normed, swap_core(normed)], axis=0)
    query = dot(normed, w_query, ((1,), (0,))).astype(BF)
    key = dot(normed, w_key, ((1,), (0,))).astype(BF)
    value = dot(normed, w_value, ((1,), (0,))).astype(BF)

    key_value = jnp.stack(
        [jnp.concatenate([key[:, :HD], value[:, :HD]], 1),
         jnp.concatenate([key[:, HD:], value[:, HD:]], 1)]
    )
    key_value = exchange(
        jnp.broadcast_to(key_value[None], (8, 2, rows, 2 * HD)).reshape(16, rows, 2 * HD), CTX
    ).reshape(16 * rows, 2 * HD)
    keys, values = key_value[:, :HD], key_value[:, HD:]

    def to_head(block):
        return exchange(jnp.stack([block[:, :HD], block[:, HD:]]), "core").reshape(2 * rows, HD)

    def to_frames(block):
        parts = exchange(block.reshape(2, rows, HD), "core")
        return jnp.concatenate([parts[0], parts[1]], axis=1)

    queries = to_head(query)
    query_pos = lax.dynamic_slice_in_dim(frame_pos, (ctx - core) * rows, 2 * rows, 0)
    allowed = frame_pos[None, :] <= query_pos[:, None]
    scores = dot(queries, keys, ((1,), (1,))) * scale
    scores = jnp.where(allowed, scores, NEG)
    weights = jnp.exp(scores - jnp.max(scores, axis=-1, keepdims=True))
    probs = (weights / jnp.sum(weights, axis=-1, keepdims=True)).astype(BF)
    attended = to_frames(dot(probs, values, ((1,), (0,))).astype(BF))

    base = all_sum_tp(dot(attended, fold, ((1,), (1,))).astype(BF)).astype(F32)

    level_onehot = (jnp.arange(8, dtype=jnp.int32) == tp)
    target = jnp.sum(jnp.where(level_onehot[None, :], codes, 0), axis=1)
    cotangent = jnp.sum(jnp.where(level_onehot[None, :], loss_grad, 0.0), axis=1)
    before_onehot = (jnp.arange(8, dtype=jnp.int32) + 1 == tp)
    previous = jnp.sum(jnp.where(before_onehot[None, :], codes, 0), axis=1)
    shard_start = jnp.arange(8, dtype=jnp.int32)[:, None] * 256
    half_ids = (shard_start + jnp.arange(128, dtype=jnp.int32)[None, :]).reshape(1, 1024)
    pick_own = (previous[:, None] == half_ids + core * 128).astype(BF)
    pick_other = (previous[:, None] == half_ids + (1 - core) * 128).astype(BF)
    embedded = dot(pick_own, embed_own.reshape(1024, 1024), ((1,), (0,))) + dot(
        pick_other, embed_other.reshape(1024, 1024), ((1,), (0,))
    )
    depth_in = base + embedded
    inverse_rms = lax.rsqrt(jnp.mean(depth_in * depth_in, axis=-1, keepdims=True) + EPS)
    scaled = depth_in * inverse_rms
    unit = scaled.astype(BF)
    unit_own = jnp.where(first, unit[:, :512], unit[:, 512:])
    unit_other = jnp.where(first, unit[:, 512:], unit[:, :512])
    logits = (
        dot(unit_own, head_own, ((1,), (1,))) + dot(unit_other, head_other, ((1,), (1,)))
    ).reshape(rows, 2048)
    ids = jnp.arange(2048, dtype=jnp.int32)
    is_target = target[:, None] == ids[None, :]
    peak = jnp.max(logits, axis=-1, keepdims=True)
    exp_terms = jnp.exp(logits - peak)
    denominator = jnp.sum(exp_terms, axis=-1, keepdims=True)
    target_logit = jnp.sum(jnp.where(is_target, logits, 0.0), axis=-1)
    loss = jnp.log(denominator[:, 0]) + peak[:, 0] - target_logit
    dlogits = (
        cotangent[:, None] * (exp_terms / denominator - is_target.astype(F32))
    ).astype(BF)
    token_loss = lax.all_gather(loss, TP, axis=0, tiled=False).T

    head_part = dot(unit, dlogits, ((0,), (0,))).astype(BF)
    head_sum = lax.psum_scatter(head_part, CTX, scatter_dimension=0, tiled=True)
    grad_head = exchange(head_sum.reshape(64, 8, 256).transpose(1, 0, 2), TP).astype(F32)

    dlogits_s = dlogits.reshape(rows, 8, 256)
    grad_own = dot(dlogits_s, head_own, ((1, 2), (0, 2)))
    grad_other = dot(dlogits_s, head_other, ((1, 2), (0, 2)))
    unit_grad = jnp.concatenate(
        [jnp.where(first, grad_own, grad_other), jnp.where(first, grad_other, grad_own)], axis=1
    )
    depth_grad = inverse_rms * (
        unit_grad - scaled * jnp.mean(unit_grad * scaled, axis=-1, keepdims=True)
    )
    summed = all_sum_tp(depth_grad.astype(BF))

    attended_grad = to_head(dot(summed, fold, ((1,), (0,))).astype(BF))
    prob_grad = dot(attended_grad, values, ((1,), (1,)))
    prob_float = probs.astype(F32)
    centre = jnp.sum(prob_float * prob_grad, axis=-1, keepdims=True)
    score_grad = (prob_float * (prob_grad - centre) * scale).astype(BF)
    query_grad = dot(score_grad, keys, ((1,), (0,))).astype(BF)
    key_part = dot(score_grad, queries, ((0,), (0,))).astype(BF)
    value_part = dot(probs, attended_grad, ((0,), (0,))).astype(BF)
    key_value_grad = total(
        exchange(jnp.concatenate([key_part, value_part], 1).reshape(8, 2 * rows, 2 * HD), CHIPS)
    ).astype(BF)
    grads = jnp.concatenate([query_grad, key_value_grad], axis=1)
    grads = jnp.where(first, grads, jnp.concatenate([grads[rows:], grads[:rows]], axis=0))
    weight_part = dot(normed_pair, grads, ((0,), (0,))).astype(BF)
    weight_sum = total(exchange(weight_part.reshape(8, 512, 3 * HD), CHIPS)).astype(BF)
    weight_sum = exchange(weight_sum.reshape(2, 256, 3 * HD), "core").astype(F32)
    grad_query, grad_key, grad_value = (
        jnp.concatenate([weight_sum[0, :, s], weight_sum[1, :, s]], axis=1)
        for s in (slice(0, HD), slice(HD, 2 * HD), slice(2 * HD, 3 * HD))
    )

    outer = dot(attended, summed, ((0,), (0,))).astype(BF)
    outer = total(exchange(outer.reshape(16, 16, 1024), CTX)).astype(BF)
    outer = lax.all_gather(outer, CTX, axis=0, tiled=True)
    grad_out = dot(outer, depth_rows, ((1,), (1,)))
    outer_cols = lax.dynamic_slice_in_dim(outer, ctx * 64, 64, 1)
    depth_part = dot(outer_cols, w_out, ((0,), (0,))).astype(BF)
    grad_depth_in = total(
        exchange(depth_part.reshape(64, 8, 512).transpose(1, 0, 2), TP)
    ).T
    return (token_loss, grad_query, grad_key, grad_value, grad_out, grad_depth_in, grad_head)


def solution(mesh):
    fine = Mesh(mesh.devices.reshape(4, 2, 2, 2, 4), ALL)
    in_specs = (
        P(CTX, None),
        P(),
        P(CTX, None),
        P(CTX, None),
        P(None, TP),
        P(None, TP),
        P(None, TP),
        P(TP, None),
        P(TP, None),
        P(None, TP, None),
        P(None, None, TP),
    )
    out_specs = (
        P(CTX, None),
        P(CTX, TP),
        P(CTX, TP),
        P(CTX, TP),
        P(TP, CTX),
        P(TP, CTX),
        P(None, CTX, TP),
    )
    return jax.shard_map(
        per_device, mesh=fine, in_specs=in_specs, out_specs=out_specs, check_vma=False
    )
```

```python
import math

import jax
import jax.numpy as jnp
from jax import lax
from jax.experimental import pallas as pl
from jax.experimental.pallas import tpu as pltpu
from jax.sharding import Mesh
from jax.sharding import PartitionSpec as P

HD = 128
EPS = 1e-05
NEG = -1e30
SCALE = 1.0 / math.sqrt(HD)
CTX = ("x", "yl", "core")
CHIPS = ("x", "yl")
TP = ("yh", "z")
ALL = CTX + TP
BF = jnp.bfloat16
F32 = jnp.float32
RUN = 96
QB = 256
KB = 512


def rms_rows(values):
    return values * lax.rsqrt(jnp.mean(values * values, axis=-1, keepdims=True) + EPS)


def dot(left, right, dims):
    return lax.dot_general(left, right, (dims, ((), ())), preferred_element_type=F32)


def exchange(parts, axes):
    return lax.all_to_all(parts, axes, 0, 0, tiled=True)


def spread(block, axes, count):
    return exchange(jnp.broadcast_to(block[None], (count,) + block.shape), axes)


def total(parts):
    return jnp.sum(parts.astype(F32), axis=0)


def swap_core(block):
    return lax.ppermute(block, "core", [(0, 1), (1, 0)])


def after(value, *earlier):
    return lax.optimization_barrier((value,) + earlier)[0]


def thirds(values):
    high = lax.reduce_precision(values, 8, 7)
    rest = values - high
    middle = lax.reduce_precision(rest, 8, 7)
    return jnp.stack([high, middle, rest - middle]).astype(BF)


def kernel_call(body, out_shape, scratch, flops, byte_count, smem_first, count):
    specs = [pl.BlockSpec(memory_space=pltpu.VMEM)] * count
    if smem_first:
        specs[0] = pl.BlockSpec(memory_space=pltpu.SMEM)
    return pl.pallas_call(
        body,
        out_shape=out_shape,
        in_specs=specs,
        out_specs=jax.tree.map(lambda _: pl.BlockSpec(memory_space=pltpu.VMEM), out_shape),
        scratch_shapes=scratch,
        compiler_params=pltpu.CompilerParams(vmem_limit_bytes=48 << 20),
        cost_estimate=pl.CostEstimate(
            flops=flops, bytes_accessed=byte_count, transcendentals=0
        ),
    )


def forward_body(q_ref, kv_ref, key_pos_ref, query_pos_ref, out_ref, lse_ref):
    for part in range(q_ref.shape[0] // 128):
        rows = slice(part * 128, part * 128 + 128)
        scores = dot(kv_ref[:, :HD], q_ref[rows, :], ((1,), (1,))) * SCALE
        allowed = key_pos_ref[...] <= query_pos_ref[:, rows]
        scores = jnp.where(allowed, scores, NEG)
        peak = jnp.max(scores, axis=0, keepdims=True)
        weights = jnp.exp(scores - peak)
        denominator = jnp.sum(weights, axis=0, keepdims=True)
        probs = (weights * (1.0 / denominator)).astype(BF)
        out_ref[rows, :] = dot(probs, kv_ref[:, HD:], ((0,), (0,))).astype(BF)
        lse_ref[:, rows] = peak + jnp.log(denominator)


def backward_body(pos_ref, q_ref, kv_ref, g_ref, out_ref, qs, ks, vs, gs, dq, dk, dv):
    total_rows = q_ref.shape[0]
    runs = total_rows // RUN

    @pl.loop(0, runs)
    def _(run):
        src = pl.ds(pl.multiple_of(run * RUN, RUN), RUN)
        dst = pl.ds(pl.multiple_of(pos_ref[run], 32), RUN)
        qs[dst, :] = q_ref[src, :]
        gs[dst, :] = g_ref[src, :]
        ks[dst, :HD] = kv_ref[src, :HD]
        vs[dst, :HD] = kv_ref[src, HD:]

    ks[:, HD:] = jnp.ones((total_rows, HD), BF)
    vs[:, HD:] = jnp.ones((total_rows, HD), BF)
    dk[...] = jnp.zeros_like(dk)
    dv[...] = jnp.zeros_like(dv)

    @pl.loop(0, total_rows // QB)
    def _(block):
        q_rows = pl.ds(pl.multiple_of(block * QB, QB), QB)
        q = qs[q_rows, :]
        g = gs[q_rows, :]

        def step(chunk, running, masked):
            rows = pl.ds(pl.multiple_of(chunk * KB, KB), KB)
            k = ks[rows, :]
            v = vs[rows, :]
            shifted = dot(k, q, ((1,), (1,)))
            if masked:
                key_at = lax.broadcasted_iota(jnp.int32, (KB, QB), 0) + chunk * KB
                query_at = lax.broadcasted_iota(jnp.int32, (KB, QB), 1) + block * QB
                shifted = jnp.where(key_at <= query_at, shifted, NEG)
            probs = jnp.exp(shifted * SCALE)
            score_grad = (probs * dot(v, g, ((1,), (1,)))).astype(BF)
            dv[rows, :] += dot(probs.astype(BF), g[:, :HD], ((1,), (0,)))
            dk[rows, :] += dot(score_grad, q[:, :HD], ((1,), (0,)))
            return running + dot(score_grad, k[:, :HD], ((0,), (0,)))

        last = block // (KB // QB)
        running = lax.fori_loop(
            0, last, lambda chunk, acc: step(chunk, acc, False), jnp.zeros((QB, HD), F32)
        )
        dq[q_rows, :] = step(last, running, True)

    @pl.loop(0, runs)
    def _(run):
        src = pl.ds(pl.multiple_of(run * RUN, RUN), RUN)
        dst = pl.ds(pl.multiple_of(pos_ref[run], 32), RUN)
        out_ref[src, :HD] = (dq[dst, :] * SCALE).astype(BF)
        out_ref[src, HD : 2 * HD] = (dk[dst, :] * SCALE).astype(BF)
        out_ref[src, 2 * HD :] = dv[dst, :].astype(BF)


def embed_body(place_ref, ids_ref, *refs):
    out_ref = refs[-1]
    core, tp = place_ref[0], place_ref[1]
    rows = ids_ref.shape[0]
    lane = lax.broadcasted_iota(jnp.int32, (rows, 128), 1)
    sums = [jnp.zeros((rows, 256), F32) for _ in range(4)]
    for slot in range(8):
        shard = lax.rem(tp + 8 - slot, 8)
        for side in range(2):
            half = core if side == 0 else 1 - core
            pick = (ids_ref[...] == lane + (shard * 256 + half * 128)).astype(F32).astype(BF)
            for quarter in range(4):
                table = refs[side * 8 + slot][512 + quarter * 128 : 640 + quarter * 128, :]
                sums[quarter] += dot(pick, table, ((1,), (0,)))
    for quarter in range(4):
        out_ref[:, quarter * 256 : quarter * 256 + 256] = sums[quarter].astype(BF)


def head_body(place_ref, base_ref, embed_ref, target_ref, cot_ref, *refs):
    tables, (unit_ref, dlogits_ref, grad_ref, loss_ref, logits_ref) = refs[:16], refs[16:]
    core, tp = place_ref[0], place_ref[1]
    rows = base_ref.shape[0]
    keep = jnp.where(tp > 0, 1.0, 0.0)
    depth_in = base_ref[...].astype(F32) + embed_ref[...].astype(F32) * keep
    inverse_rms = lax.rsqrt(jnp.mean(depth_in * depth_in, axis=-1, keepdims=True) + EPS)
    scaled = depth_in * inverse_rms
    unit = scaled.astype(BF)
    unit_ref[...] = unit
    low_first = core == 0
    sides = (
        jnp.where(low_first, unit[:, :512], unit[:, 512:]),
        jnp.where(low_first, unit[:, 512:], unit[:, :512]),
    )
    lane = lax.broadcasted_iota(jnp.int32, (rows, 256), 1)
    peak = jnp.full((rows, 1), NEG, F32)
    for slot in range(8):
        cols = slice(slot * 256, slot * 256 + 256)
        logits = dot(sides[0], tables[slot][:512, :], ((1,), (0,))) + dot(
            sides[1], tables[8 + slot][:512, :], ((1,), (0,))
        )
        logits_ref[:, cols] = logits
        peak = jnp.maximum(peak, jnp.max(logits, axis=-1, keepdims=True))
    denominator = jnp.zeros((rows, 1), F32)
    chosen = jnp.zeros((rows, 1), F32)
    for slot in range(8):
        cols = slice(slot * 256, slot * 256 + 256)
        shard = lax.rem(tp + 8 - slot, 8)
        logits = logits_ref[:, cols]
        is_target = target_ref[...] == lane + shard * 256
        chosen += jnp.sum(jnp.where(is_target, logits, 0.0), axis=-1, keepdims=True)
        terms = jnp.exp(logits - peak)
        denominator += jnp.sum(terms, axis=-1, keepdims=True)
        logits_ref[:, cols] = terms
    loss_ref[...] = jnp.log(denominator) + peak - chosen
    inverse = 1.0 / denominator
    cot = cot_ref[...]
    sums = [jnp.zeros((rows, 512), F32), jnp.zeros((rows, 512), F32)]
    for slot in range(8):
        cols = slice(slot * 256, slot * 256 + 256)
        shard = lax.rem(tp + 8 - slot, 8)
        hit = jnp.where(target_ref[...] == lane + shard * 256, 1.0, 0.0)
        dlogits = (cot * (logits_ref[:, cols] * inverse - hit)).astype(BF)
        dlogits_ref[:, pl.ds(pl.multiple_of(shard * 256, 256), 256)] = dlogits
        for side in range(2):
            sums[side] += dot(dlogits, tables[side * 8 + slot][:512, :], ((1,), (1,)))
    unit_grad = jnp.concatenate(
        [jnp.where(low_first, sums[0], sums[1]), jnp.where(low_first, sums[1], sums[0])], axis=1
    )
    centre = jnp.mean(unit_grad * scaled, axis=-1, keepdims=True)
    grad_ref[...] = (inverse_rms * (unit_grad - scaled * centre)).astype(BF)


def all_sum_tp(part):
    rows, cols = part.shape
    pieces = exchange(part.reshape(8, rows // 8, cols), TP)
    own = total(pieces).astype(BF)
    return spread(own, TP, 8).reshape(rows, cols)


def per_device(
    frames,
    frame_pos,
    codes,
    loss_grad,
    w_query,
    w_key,
    w_value,
    w_out,
    w_depth_in,
    code_embed,
    code_head,
):
    rows = frames.shape[0]
    frame_total = frame_pos.shape[0]
    core = lax.axis_index("core")
    ctx = lax.axis_index(CTX)
    tp = lax.axis_index(TP)
    first = core == 0
    place = jnp.stack([core, tp]).astype(jnp.int32)

    depth_cols = lax.dynamic_slice_in_dim(w_depth_in, ctx * 64, 64, 1).T
    depth_cols = spread(depth_cols, TP, 8)
    fold_cols = lax.dot_general(
        depth_cols, w_out.reshape(256, 8, 512), (((0, 2), (1, 2)), ((), ())),
        preferred_element_type=F32,
    ).astype(BF)

    normed = rms_rows(frames.astype(F32)).astype(BF)
    key = dot(normed, w_key, ((1,), (0,))).astype(BF)
    value = dot(normed, w_value, ((1,), (0,))).astype(BF)
    query = dot(normed, w_query, ((1,), (0,))).astype(BF)

    key_value = jnp.stack(
        [jnp.concatenate([key[:, :HD], value[:, :HD]], 1),
         jnp.concatenate([key[:, HD:], value[:, HD:]], 1)]
    )
    key_value = exchange(
        after(
            jnp.broadcast_to(key_value[None], (8, 2, rows, 2 * HD)).reshape(16, rows, 2 * HD),
            depth_cols,
        ),
        CTX,
    ).reshape(frame_total, 2 * HD)

    def to_head(block):
        keep = jnp.where(first, block[:, :HD], block[:, HD:])
        come = swap_core(jnp.where(first, block[:, HD:], block[:, :HD]))
        return jnp.where(
            first, jnp.concatenate([keep, come], 0), jnp.concatenate([come, keep], 0)
        )

    def to_frames(block):
        keep = jnp.where(first, block[:rows], block[rows:])
        come = swap_core(jnp.where(first, block[rows:], block[:rows]))
        return jnp.where(
            first, jnp.concatenate([keep, come], 1), jnp.concatenate([come, keep], 1)
        )

    queries = to_head(query)

    def chunk(level):
        head = lax.dynamic_slice(code_head, (level, core * 512, 0), (1, 512, 256))[0]
        table = lax.dynamic_slice(
            code_embed, (jnp.maximum(level - 1, 0), core * 128, 0), (1, 128, 1024)
        )[0]
        table = table.reshape(128, 4, 256).transpose(1, 0, 2).reshape(512, 256)
        return jnp.concatenate([head, table], axis=0)

    own_chunks = [chunk(tp)]
    for shift in range(1, 8):
        own_chunks.append(
            lax.ppermute(
                chunk(lax.rem(tp + shift, 8)), TP, [(i, (i + shift) % 8) for i in range(8)]
            )
        )
    other_chunks = [swap_core(block) for block in own_chunks]
    chunks = own_chunks + other_chunks

    query_pos = lax.dynamic_slice_in_dim(frame_pos, (ctx - core) * rows, 2 * rows, 0)
    attended_head, lse = kernel_call(
        forward_body,
        (jax.ShapeDtypeStruct((2 * rows, HD), BF), jax.ShapeDtypeStruct((1, 2 * rows), F32)),
        [], 2_000_000_000, 20_000_000, False, 4,
    )(queries, key_value, frame_pos[:, None], query_pos[None, :])
    fold = spread(after(fold_cols, key_value), CTX, 16).reshape(1024, 2 * HD)
    attended = to_frames(attended_head)

    base = all_sum_tp(dot(attended, fold, ((1,), (1,))).astype(BF))

    level_ids = jnp.arange(8, dtype=jnp.int32)[None, :]
    target = jnp.sum(jnp.where(level_ids == tp, codes, 0), axis=1, keepdims=True)
    cotangent = jnp.sum(jnp.where(level_ids == tp, loss_grad, 0.0), axis=1, keepdims=True)
    previous = jnp.sum(jnp.where(level_ids + 1 == tp, codes, 0), axis=1, keepdims=True)
    embedded = kernel_call(
        embed_body, jax.ShapeDtypeStruct((rows, 1024), BF), [], 800_000_000, 9_000_000, True, 18
    )(place, previous, *chunks)
    unit, dlogits, depth_grad, loss = kernel_call(
        head_body,
        (
            jax.ShapeDtypeStruct((rows, 1024), BF),
            jax.ShapeDtypeStruct((rows, 2048), BF),
            jax.ShapeDtypeStruct((rows, 1024), BF),
            jax.ShapeDtypeStruct((rows, 1), F32),
        ),
        [pltpu.VMEM((rows, 2048), F32)],
        4_000_000_000, 30_000_000, True, 21,
    )(place, base, embedded, target, cotangent, *chunks)

    def with_parts(block, values):
        parts = thirds(values).reshape(3 * 3, 128)
        return jnp.concatenate([block, jnp.pad(parts, ((0, 7), (0, 0)))], axis=0)

    def gathered(blocks):
        parts = blocks[:, 2 * rows : 2 * rows + 9].reshape(8, 3, 2 * rows)
        parts = parts.transpose(0, 2, 1).reshape(frame_total, 3)
        return jnp.concatenate(
            [blocks[:, : 2 * rows].reshape(frame_total, HD), jnp.pad(parts, ((0, 0), (0, 125)))],
            axis=1,
        )

    query_send = with_parts(queries, -lse[0] * (1.0 / SCALE))
    query_all = gathered(spread(after(query_send, base), CHIPS, 8))

    summed = all_sum_tp(after(depth_grad, query_all))

    unit_blocks = unit.reshape(rows, 8, 2, 64)
    unit_keep = lax.dynamic_index_in_dim(unit_blocks, core, 2, False).reshape(rows, 512)
    unit_send = lax.dynamic_index_in_dim(unit_blocks, 1 - core, 2, False).reshape(rows, 512)
    head_come = swap_core(dot(unit_send, dlogits, ((0,), (0,))).astype(BF))
    head_part = (dot(unit_keep, dlogits, ((0,), (0,))) + head_come.astype(F32)).astype(BF)
    head_sum = lax.psum_scatter(head_part, CHIPS, scatter_dimension=0, tiled=True)

    grad_head_cols = to_head(dot(summed, fold, ((1,), (0,))).astype(BF))
    centre = jnp.sum(grad_head_cols.astype(F32) * attended_head.astype(F32), axis=-1)
    grad_all_raw = spread(with_parts(grad_head_cols, -centre), CHIPS, 8)
    grad_all = gathered(grad_all_raw)

    grads = kernel_call(
        backward_body,
        jax.ShapeDtypeStruct((frame_total, 3 * HD), BF),
        [pltpu.VMEM((frame_total, 2 * HD), BF)] * 4 + [pltpu.VMEM((frame_total, HD), F32)] * 3,
        25_000_000_000, 20_000_000, True, 4,
    )(frame_pos[::RUN], query_all, key_value, grad_all)

    normed_own = exchange(
        after(normed.reshape(rows, 8, 512).transpose(1, 0, 2), grad_all_raw), CHIPS
    )
    normed_other = swap_core(normed_own)
    normed_all = jnp.where(
        first,
        jnp.stack([normed_own, normed_other], axis=1),
        jnp.stack([normed_other, normed_own], axis=1),
    ).reshape(frame_total, 512)

    outer = dot(attended, summed, ((0,), (0,))).astype(BF)
    outer = total(exchange(after(outer.reshape(16, 16, 1024), grad_all_raw), CTX)).astype(BF)
    outer = spread(outer, CTX, 16).reshape(256, 1024)
    depth_half = lax.dynamic_slice_in_dim(w_depth_in, core * 256, 256, 0)
    moves = [
        (c * 8 + t, (2 * t + c % 2) * 8 + c // 2) for c in range(16) for t in range(8)
    ]
    depth_rows = lax.ppermute(depth_half, ALL, moves)
    grad_out = dot(outer, depth_rows, ((1,), (1,)))
    outer_cols = lax.dynamic_slice_in_dim(outer, ctx * 64, 64, 1)
    depth_part = dot(outer_cols, w_out, ((0,), (0,))).astype(BF)
    loss_row = jnp.pad(thirds(loss[:, 0]).reshape(1, 576), ((0, 15), (0, 192)))
    tail = jnp.concatenate(
        [
            jnp.concatenate(
                [depth_part.reshape(64, 8, 512), head_sum.reshape(64, 8, 256)], axis=2
            ).transpose(1, 0, 2),
            jnp.broadcast_to(loss_row[None], (8, 16, 768)),
        ],
        axis=1,
    )
    tail = exchange(tail, TP)
    grad_depth_in = total(tail[:, :64, :512]).T
    grad_head = tail[:, :64, 512:].astype(F32)
    token_loss = total(tail[:, 64, :576].reshape(8, 3, rows).transpose(1, 2, 0))

    weights = dot(normed_all, grads, ((0,), (0,)))
    weights_keep = jnp.where(first, weights[:256], weights[256:])
    weights_come = swap_core(jnp.where(first, weights[256:], weights[:256]))

    def paired(cols):
        keep, come = weights_keep[:, cols], weights_come[:, cols]
        return jnp.where(
            first, jnp.concatenate([keep, come], 1), jnp.concatenate([come, keep], 1)
        )

    grad_query = paired(slice(0, HD))
    grad_key = paired(slice(HD, 2 * HD))
    grad_value = paired(slice(2 * HD, 3 * HD))
    return (token_loss, grad_query, grad_key, grad_value, grad_out, grad_depth_in, grad_head)


def solution(mesh):
    fine = Mesh(mesh.devices.reshape(4, 2, 2, 2, 4), ALL)
    in_specs = (
        P(CTX, None),
        P(),
        P(CTX, None),
        P(CTX, None),
        P(None, TP),
        P(None, TP),
        P(None, TP),
        P(TP, None),
        P(TP, None),
        P(None, TP, None),
        P(None, None, TP),
    )
    out_specs = (
        P(CTX, None),
        P(CTX, TP),
        P(CTX, TP),
        P(CTX, TP),
        P(TP, CTX),
        P(TP, CTX),
        P(None, CTX, TP),
    )
    return jax.shard_map(
        per_device, mesh=fine, in_specs=in_specs, out_specs=out_specs, check_vma=False
    )
```

```python
import math

import jax
import jax.numpy as jnp
from jax import lax
from jax.experimental import pallas as pl
from jax.experimental.pallas import tpu as pltpu
from jax.sharding import Mesh
from jax.sharding import PartitionSpec as P

HD = 128
EPS = 1e-05
NEG = -1e30
SCALE = 1.0 / math.sqrt(HD)
CTX = ("x", "yl", "core")
CHIPS = ("x", "yl")
TP = ("yh", "z")
ALL = CTX + TP
BF = jnp.bfloat16
F32 = jnp.float32
RUN = 96
QB = 256
KB = 512


def rms_rows(values):
    return values * lax.rsqrt(jnp.mean(values * values, axis=-1, keepdims=True) + EPS)


def dot(left, right, dims):
    return lax.dot_general(left, right, (dims, ((), ())), preferred_element_type=F32)


def exchange(parts, axes):
    return lax.all_to_all(parts, axes, 0, 0, tiled=True)


def spread(block, axes, count):
    return exchange(jnp.broadcast_to(block[None], (count,) + block.shape), axes)


def total(parts):
    return jnp.sum(parts.astype(F32), axis=0)


def swap_core(block):
    return lax.ppermute(block, "core", [(0, 1), (1, 0)])


def after(value, *earlier):
    return lax.optimization_barrier((value,) + earlier)[0]


def thirds(values):
    high = lax.reduce_precision(values, 8, 7)
    rest = values - high
    middle = lax.reduce_precision(rest, 8, 7)
    return jnp.stack([high, middle, rest - middle]).astype(BF)


def kernel_call(body, out_shape, scratch, flops, byte_count, count):
    return pl.pallas_call(
        body,
        out_shape=out_shape,
        in_specs=[pl.BlockSpec(memory_space=pltpu.SMEM)]
        + [pl.BlockSpec(memory_space=pltpu.VMEM)] * (count - 1),
        out_specs=jax.tree.map(lambda _: pl.BlockSpec(memory_space=pltpu.VMEM), out_shape),
        scratch_shapes=scratch,
        compiler_params=pltpu.CompilerParams(vmem_limit_bytes=48 << 20),
        cost_estimate=pl.CostEstimate(
            flops=flops, bytes_accessed=byte_count, transcendentals=0
        ),
    )


CORE, CTX_AT, TP_AT, SHARDS = 32, 33, 34, 35


def forward_body(
    meta_ref, q_ref, q_come_ref, kv_ref, own_ref, other_ref, lse_ref, qs, key_pos
):
    first = meta_ref[CORE] == 0
    ctx = meta_ref[CTX_AT]
    qs[...] = jnp.zeros_like(qs)
    for run in range(2):
        rows = slice(run * RUN, run * RUN + RUN)
        qs[run * 128 : run * 128 + RUN, :] = jnp.where(
            first, q_ref[rows, :HD], q_ref[rows, HD:]
        )
        qs[256 + run * 128 : 256 + run * 128 + RUN, :] = q_come_ref[rows, :]
    down = lax.broadcasted_iota(jnp.int32, (RUN, 128), 0)
    for run in range(key_pos.shape[0] // RUN):
        key_pos[run * RUN : run * RUN + RUN, :] = down + meta_ref[run]
    lse_ref[...] = jnp.zeros_like(lse_ref)
    across = lax.broadcasted_iota(jnp.int32, (1, 128), 1)
    for part in range(4):
        owner = ctx if part < 2 else ctx + 1 - 2 * meta_ref[CORE]
        query_pos = across + meta_ref[2 * owner + part % 2]
        scores = dot(kv_ref[:, :HD], qs[part * 128 : part * 128 + 128, :], ((1,), (1,))) * SCALE
        scores = jnp.where(key_pos[...] <= query_pos, scores, NEG)
        peak = jnp.max(scores, axis=0, keepdims=True)
        weights = jnp.exp(scores - peak)
        denominator = jnp.sum(weights, axis=0, keepdims=True)
        probs = (weights * (1.0 / denominator)).astype(BF)
        result = dot(probs, kv_ref[:, HD:], ((0,), (0,))).astype(BF)
        rows = slice(part % 2 * RUN, part % 2 * RUN + RUN)
        (own_ref if part < 2 else other_ref)[rows, :] = result[:RUN, :]
        lse_ref[part : part + 1, :] = peak + jnp.log(denominator)


def embed_body(meta_ref, ids_ref, *refs):
    out_ref = refs[-1]
    rows = ids_ref.shape[0]
    lane = lax.broadcasted_iota(jnp.int32, (rows, 256), 1)
    sums = jnp.zeros((rows, 1024), F32)
    for block in range(8):
        pick = (ids_ref[...] == lane + meta_ref[SHARDS + block] * 256).astype(F32).astype(BF)
        sums += dot(pick, refs[block][...], ((1,), (0,)))
    out_ref[...] = sums.astype(BF)


def head_body(meta_ref, base_ref, embed_ref, target_ref, cot_ref, *refs):
    tables, (unit_ref, dlogits_ref, grad_ref, loss_ref, logits_ref) = refs[:8], refs[8:]
    rows = base_ref.shape[0]
    keep = jnp.where(meta_ref[TP_AT] > 0, 1.0, 0.0)
    depth_in = base_ref[...].astype(F32) + embed_ref[...].astype(F32) * keep
    inverse_rms = lax.rsqrt(jnp.mean(depth_in * depth_in, axis=-1, keepdims=True) + EPS)
    scaled = depth_in * inverse_rms
    unit = scaled.astype(BF)
    unit_ref[...] = unit
    lane = lax.broadcasted_iota(jnp.int32, (rows, 256), 1)
    peak = jnp.full((rows, 1), NEG, F32)
    for block in range(8):
        cols = slice(block * 256, block * 256 + 256)
        logits = dot(unit, tables[block][...], ((1,), (0,)))
        logits_ref[:, cols] = logits
        peak = jnp.maximum(peak, jnp.max(logits, axis=-1, keepdims=True))
    denominator = jnp.zeros((rows, 1), F32)
    chosen = jnp.zeros((rows, 1), F32)
    for block in range(8):
        cols = slice(block * 256, block * 256 + 256)
        logits = logits_ref[:, cols]
        is_target = target_ref[...] == lane + meta_ref[SHARDS + block] * 256
        chosen += jnp.sum(jnp.where(is_target, logits, 0.0), axis=-1, keepdims=True)
        terms = jnp.exp(logits - peak)
        denominator += jnp.sum(terms, axis=-1, keepdims=True)
        logits_ref[:, cols] = terms
    loss_ref[...] = jnp.log(denominator) + peak - chosen
    inverse = 1.0 / denominator
    cot = cot_ref[...]
    unit_grad = jnp.zeros((rows, 1024), F32)
    for block in range(8):
        cols = slice(block * 256, block * 256 + 256)
        start = meta_ref[SHARDS + block] * 256
        hit = jnp.where(target_ref[...] == lane + start, 1.0, 0.0)
        dlogits = (cot * (logits_ref[:, cols] * inverse - hit)).astype(BF)
        dlogits_ref[:, pl.ds(pl.multiple_of(start, 256), 256)] = dlogits
        unit_grad += dot(dlogits, tables[block][...], ((1,), (1,)))
    centre = jnp.mean(unit_grad * scaled, axis=-1, keepdims=True)
    grad_ref[...] = (inverse_rms * (unit_grad - scaled * centre)).astype(BF)


STAT_AT, OUTER_AT, SEND = 192, 224, 352


def send_body(
    meta_ref, summed_ref, fold_ref, attended_ref, lse_ref, lse_come_ref, out_ref, stat, product
):
    first = meta_ref[CORE] == 0
    summed = summed_ref[...]
    attended = attended_ref[...]
    grad = dot(summed, fold_ref[...], ((1,), (0,))).astype(BF)
    outer = dot(attended, summed, ((0,), (0,))).astype(BF)
    for block in range(16):
        for piece in range(8):
            at = OUTER_AT + piece * 16
            out_ref[block, at : at + 16, :] = outer[
                block * 16 : block * 16 + 16, piece * 128 : piece * 128 + 128
            ]
    ones = jnp.ones((8, 128), F32)
    for head in range(2):
        cols = slice(head * HD, head * HD + HD)
        stat[...] = jnp.zeros_like(stat)
        product[...] = jnp.zeros_like(product)
        for run in range(2):
            rows = slice(run * RUN, run * RUN + RUN)
            product[:RUN, :] = grad[rows, cols].astype(F32) * attended[rows, cols].astype(F32)
            centre = lax.dot_general(
                ones, product[...], (((1,), (1,)), ((), ())),
                preferred_element_type=F32, precision=lax.Precision.HIGHEST,
            )[:1, :]
            mine = lse_ref[run : run + 1, :]
            come = lse_come_ref[2 + run : 3 + run, :]
            lse = jnp.where(first, mine, come) if head == 0 else jnp.where(first, come, mine)
            for at, value in ((0, lse * (-1.0 / SCALE)), (3, -centre)):
                for term in range(3):
                    part = value.astype(BF).astype(F32)
                    row = run * 16 + at + term
                    stat[row : row + 1, :] = part
                    value = value - part
        packed = stat[...].astype(BF)
        for block in range(head, 16, 2):
            out_ref[block, :STAT_AT, :] = grad[:, cols]
            out_ref[block, STAT_AT:OUTER_AT, :] = packed


def backward_body(
    meta_ref, q_ref, kv_ref, come_ref, normed_ref, normed_other_ref, keep_ref, send_ref,
    qs, ks, vs, gs, dq, dk, dv, grads,
):
    core = meta_ref[CORE]
    first = core == 0
    total_rows = q_ref.shape[0]
    runs = total_rows // RUN
    stat_row = lax.broadcasted_iota(jnp.int32, (16, 128), 0)
    stat_lane = lax.broadcasted_iota(jnp.int32, (16, 128), 1)
    place_lse = jnp.where((stat_row == stat_lane) & (stat_lane < 3), 1.0, 0.0).astype(BF)
    place_centre = jnp.where((stat_row == stat_lane + 3) & (stat_lane < 3), 1.0, 0.0).astype(BF)
    for run in range(runs):
        src = slice(run * RUN, run * RUN + RUN)
        dst = pl.ds(pl.multiple_of(meta_ref[run], 32), RUN)
        half = slice(run % 2 * RUN, run % 2 * RUN + RUN)
        stats = come_ref[run // 2, STAT_AT + run % 2 * 16 : STAT_AT + run % 2 * 16 + 16, :]
        qs[dst, :HD] = jnp.where(first, q_ref[src, :HD], q_ref[src, HD:])
        qs[dst, HD:] = dot(stats, place_lse, ((0,), (0,))).astype(BF)[:RUN, :]
        gs[dst, :HD] = come_ref[run // 2, half, :]
        gs[dst, HD:] = dot(stats, place_centre, ((0,), (0,))).astype(BF)[:RUN, :]
        ks[dst, :HD] = kv_ref[src, :HD]
        vs[dst, :HD] = kv_ref[src, HD:]

    ks[:, HD:] = jnp.ones((total_rows, HD), BF)
    vs[:, HD:] = jnp.ones((total_rows, HD), BF)
    dk[...] = jnp.zeros_like(dk)
    dv[...] = jnp.zeros_like(dv)

    @pl.loop(0, total_rows // QB)
    def _(block):
        q_rows = pl.ds(pl.multiple_of(block * QB, QB), QB)
        q = qs[q_rows, :]
        g = gs[q_rows, :]

        def step(chunk, running, masked):
            rows = pl.ds(pl.multiple_of(chunk * KB, KB), KB)
            k = ks[rows, :]
            v = vs[rows, :]
            shifted = dot(k, q, ((1,), (1,)))
            if masked:
                key_at = lax.broadcasted_iota(jnp.int32, (KB, QB), 0) + chunk * KB
                query_at = lax.broadcasted_iota(jnp.int32, (KB, QB), 1) + block * QB
                shifted = jnp.where(key_at <= query_at, shifted, NEG)
            probs = jnp.exp(shifted * SCALE)
            score_grad = (probs * dot(v, g, ((1,), (1,)))).astype(BF)
            dv[rows, :] += dot(probs.astype(BF), g[:, :HD], ((1,), (0,)))
            dk[rows, :] += dot(score_grad, q[:, :HD], ((1,), (0,)))
            return running + dot(score_grad, k[:, :HD], ((0,), (0,)))

        last = block // (KB // QB)
        running = lax.fori_loop(
            0, last, lambda chunk, acc: step(chunk, acc, False), jnp.zeros((QB, HD), F32)
        )
        dq[q_rows, :] = step(last, running, True)

    for run in range(runs):
        src = slice(run * RUN, run * RUN + RUN)
        dst = pl.ds(pl.multiple_of(meta_ref[run], 32), RUN)
        grads[src, :HD] = (dq[dst, :] * SCALE).astype(BF)
        grads[src, HD : 2 * HD] = (dk[dst, :] * SCALE).astype(BF)
        grads[src, 2 * HD :] = dv[dst, :].astype(BF)

    sums = jnp.zeros((512, 3 * HD), F32)
    for hop in range(8):
        from_x = lax.rem(lax.div(meta_ref[CTX_AT], 4) + 4 - hop // 2, 4)
        from_yl = lax.rem(lax.div(meta_ref[CTX_AT], 2) + 2 - hop % 2, 2)
        for side in range(2):
            from_core = core if side == 0 else 1 - core
            start = (from_x * 2 + from_yl) * 384 + from_core * 192
            rows = pl.ds(pl.multiple_of(start, 192), 192)
            block = (normed_ref if side == 0 else normed_other_ref)[hop]
            sums += dot(block, grads[rows, :], ((0,), (0,)))
    keep_ref[...] = jnp.where(first, sums[:256], sums[256:])
    send_ref[...] = jnp.where(first, sums[256:], sums[:256])


def join_body(meta_ref, keep_ref, come_ref, *out_refs):
    first = meta_ref[CORE] == 0
    for at, out_ref in enumerate(out_refs):
        cols = slice(at * HD, at * HD + HD)
        keep, come = keep_ref[:, cols], come_ref[:, cols]
        out_ref[:, :HD] = jnp.where(first, keep, come)
        out_ref[:, HD:] = jnp.where(first, come, keep)


def all_sum_tp(part):
    rows, cols = part.shape
    pieces = exchange(part.reshape(8, rows // 8, cols), TP)
    own = total(pieces).astype(BF)
    return spread(own, TP, 8).reshape(rows, cols)


def per_device(
    frames,
    frame_pos,
    codes,
    loss_grad,
    w_query,
    w_key,
    w_value,
    w_out,
    w_depth_in,
    code_embed,
    code_head,
):
    rows = frames.shape[0]
    frame_total = frame_pos.shape[0]
    x, yl, core = lax.axis_index("x"), lax.axis_index("yl"), lax.axis_index("core")
    yh, z = lax.axis_index("yh"), lax.axis_index("z")
    ctx = lax.axis_index(CTX)
    tp = lax.axis_index(TP)
    first = core == 0

    shards, head_blocks, embed_blocks = [], [], []
    for block in range(4):
        far, near = block // 2, block % 2 * 2
        level = (yh + far) % 2 * 4 + (z + near + core) % 4
        head_blocks.append(lax.dynamic_index_in_dim(code_head, level, 0, False))
        embed_blocks.append(
            lax.dynamic_index_in_dim(code_embed, jnp.maximum(level - 1, 0), 0, False)
        )
    frames, *blocks = lax.optimization_barrier((frames, *head_blocks, *embed_blocks))
    for side in range(2):
        for block in range(4):
            far, near = block // 2, block % 2 * 2
            turn = near + (core if side == 0 else 1 - core)
            shards.append((yh + far) % 2 * 4 + (z + 4 - turn) % 4)
    own_blocks = []
    for at, operand in enumerate(blocks):
        far, near = at % 4 // 2, at % 2 * 2
        moves = []
        for a in range(2):
            for k in range(2):
                for h in range(2):
                    for d in range(4):
                        to = ((a + far) % 2, k, (h + far) % 2, (d + near + k) % 4)
                        moves.append(
                            (((a * 2 + k) * 2 + h) * 4 + d, ((to[0] * 2 + to[1]) * 2 + to[2]) * 4 + to[3])
                        )
        own_blocks.append(lax.ppermute(operand, ("yl", "core", "yh", "z"), moves))
    other_blocks = [swap_core(block) for block in own_blocks]
    head_tables = own_blocks[:4] + other_blocks[:4]
    embed_tables = own_blocks[4:] + other_blocks[4:]
    meta = jnp.concatenate(
        [frame_pos[::RUN], jnp.stack([core, ctx, tp] + shards).astype(jnp.int32)]
    )

    depth_cols = lax.dynamic_slice_in_dim(w_depth_in, ctx * 64, 64, 1).T
    depth_cols = spread(depth_cols, TP, 8)
    fold_cols = lax.dot_general(
        depth_cols, w_out.reshape(256, 8, 512), (((0, 2), (1, 2)), ((), ())),
        preferred_element_type=F32,
    ).astype(BF)

    normed = rms_rows(frames.astype(F32)).astype(BF)
    key = dot(normed, w_key, ((1,), (0,))).astype(BF)
    value = dot(normed, w_value, ((1,), (0,))).astype(BF)
    query = dot(normed, w_query, ((1,), (0,))).astype(BF)

    key_value = jnp.stack(
        [jnp.concatenate([key[:, :HD], value[:, :HD]], 1),
         jnp.concatenate([key[:, HD:], value[:, HD:]], 1)]
    )
    key_value = exchange(
        after(
            jnp.broadcast_to(key_value[None], (8, 2, rows, 2 * HD)).reshape(16, rows, 2 * HD),
            depth_cols,
        ),
        CTX,
    ).reshape(frame_total, 2 * HD)
    query_all = lax.all_gather(query, CTX, axis=0, tiled=True)
    query_come = swap_core(jnp.where(first, query[:, HD:], query[:, :HD]))

    own_part, other_part, lse = kernel_call(
        forward_body,
        (
            jax.ShapeDtypeStruct((rows, HD), BF),
            jax.ShapeDtypeStruct((rows, HD), BF),
            jax.ShapeDtypeStruct((8, 128), F32),
        ),
        [pltpu.VMEM((512, HD), BF), pltpu.VMEM((frame_total, 128), jnp.int32)],
        2_000_000_000, 4_000_000, 4,
    )(meta, query, query_come, key_value)
    come_part = swap_core(other_part)
    lse_come = swap_core(lse)
    attended = jnp.where(
        first,
        jnp.concatenate([own_part, come_part], 1),
        jnp.concatenate([come_part, own_part], 1),
    )
    fold = spread(after(fold_cols, key_value), CTX, 16).reshape(1024, 2 * HD)

    base = all_sum_tp(dot(attended, fold, ((1,), (1,))).astype(BF))

    normed_blocks = after(normed, key_value).reshape(rows, 8, 512)
    chip = x * 2 + yl
    pieces = []
    for hop in range(8):
        to = (x + hop // 2) % 4 * 2 + (yl + hop % 2) % 2
        piece = lax.dynamic_index_in_dim(normed_blocks, to, 1, False)
        if hop:
            moves = [
                (a * 2 + b, (a + hop // 2) % 4 * 2 + (b + hop % 2) % 2)
                for a in range(4) for b in range(2)
            ]
            piece = lax.ppermute(piece, CHIPS, moves)
        pieces.append(piece)
    normed_own = jnp.stack(pieces)
    normed_other = swap_core(normed_own)

    level_ids = jnp.arange(8, dtype=jnp.int32)[None, :]
    target = jnp.sum(jnp.where(level_ids == tp, codes, 0), axis=1, keepdims=True)
    cotangent = jnp.sum(jnp.where(level_ids == tp, loss_grad, 0.0), axis=1, keepdims=True)
    previous = jnp.sum(jnp.where(level_ids + 1 == tp, codes, 0), axis=1, keepdims=True)
    embedded = kernel_call(
        embed_body, jax.ShapeDtypeStruct((rows, 1024), BF), [], 800_000_000, 5_000_000, 10
    )(meta, previous, *embed_tables)
    unit, dlogits, depth_grad, loss = kernel_call(
        head_body,
        (
            jax.ShapeDtypeStruct((rows, 1024), BF),
            jax.ShapeDtypeStruct((rows, 2048), BF),
            jax.ShapeDtypeStruct((rows, 1024), BF),
            jax.ShapeDtypeStruct((rows, 1), F32),
        ),
        [pltpu.VMEM((rows, 2048), F32)],
        2_000_000_000, 6_000_000, 13,
    )(meta, base, embedded, target, cotangent, *head_tables)

    summed = all_sum_tp(depth_grad)

    unit_blocks = unit.reshape(rows, 8, 2, 64)
    unit_keep = lax.dynamic_index_in_dim(unit_blocks, core, 2, False).reshape(rows, 512)
    unit_send = lax.dynamic_index_in_dim(unit_blocks, 1 - core, 2, False).reshape(rows, 512)
    head_come = swap_core(dot(unit_send, dlogits, ((0,), (0,))).astype(BF))
    head_part = (dot(unit_keep, dlogits, ((0,), (0,))) + head_come.astype(F32)).astype(BF)
    head_sum = lax.psum_scatter(head_part, CHIPS, scatter_dimension=0, tiled=True)

    send = kernel_call(
        send_body,
        jax.ShapeDtypeStruct((16, SEND, 128), BF),
        [pltpu.VMEM((32, 128), F32), pltpu.VMEM((128, 128), F32)],
        400_000_000, 3_000_000, 6,
    )(meta, after(summed, head_part), fold, attended, lse, lse_come)
    come = exchange(send, CTX)

    outer_own = total(come[:, OUTER_AT:]).astype(BF)
    outer = spread(outer_own, CTX, 16).reshape(16, 8, 16, 128)
    outer = outer.transpose(0, 2, 1, 3).reshape(256, 1024)

    weights_keep, weights_send = kernel_call(
        backward_body,
        (jax.ShapeDtypeStruct((256, 3 * HD), F32), jax.ShapeDtypeStruct((256, 3 * HD), F32)),
        [pltpu.VMEM((frame_total, 2 * HD), BF)] * 4
        + [pltpu.VMEM((frame_total, HD), F32)] * 3
        + [pltpu.VMEM((frame_total, 3 * HD), BF)],
        25_000_000_000, 8_000_000, 6,
    )(meta, query_all, key_value, come, normed_own, normed_other)
    weights_come = swap_core(weights_send)
    grad_query, grad_key, grad_value = kernel_call(
        join_body, (jax.ShapeDtypeStruct((256, 2 * HD), F32),) * 3, [], 0, 2_000_000, 3
    )(meta, weights_keep, weights_come)

    depth_half = lax.dynamic_slice_in_dim(w_depth_in, core * 256, 256, 0)
    moves = [
        (c * 8 + t, (2 * t + c % 2) * 8 + c // 2) for c in range(16) for t in range(8)
    ]
    depth_rows = lax.ppermute(after(depth_half, base), ALL, moves)
    grad_out = dot(outer, depth_rows, ((1,), (1,)))
    outer_cols = lax.dynamic_slice_in_dim(outer, ctx * 64, 64, 1)
    depth_part = dot(outer_cols, w_out, ((0,), (0,))).astype(BF)
    loss_row = jnp.pad(thirds(loss[:, 0]).reshape(1, 576), ((0, 15), (0, 192)))
    tail = jnp.concatenate(
        [
            jnp.concatenate(
                [depth_part.reshape(64, 8, 512), head_sum.reshape(64, 8, 256)], axis=2
            ).transpose(1, 0, 2),
            jnp.broadcast_to(loss_row[None], (8, 16, 768)),
        ],
        axis=1,
    )
    tail = exchange(tail, TP)
    grad_depth_in = total(tail[:, :64, :512]).T
    grad_head = tail[:, :64, 512:].astype(F32)
    token_loss = total(tail[:, 64, :576].reshape(8, 3, rows).transpose(1, 2, 0))
    return (token_loss, grad_query, grad_key, grad_value, grad_out, grad_depth_in, grad_head)


def solution(mesh):
    fine = Mesh(mesh.devices.reshape(4, 2, 2, 2, 4), ALL)
    in_specs = (
        P(CTX, None),
        P(),
        P(CTX, None),
        P(CTX, None),
        P(None, TP),
        P(None, TP),
        P(None, TP),
        P(TP, None),
        P(TP, None),
        P(None, TP, None),
        P(None, None, TP),
    )
    out_specs = (
        P(CTX, None),
        P(CTX, TP),
        P(CTX, TP),
        P(CTX, TP),
        P(TP, CTX),
        P(TP, CTX),
        P(None, CTX, TP),
    )
    return jax.shard_map(
        per_device, mesh=fine, in_specs=in_specs, out_specs=out_specs, check_vma=False
    )
```

```python
import math

import jax
import jax.numpy as jnp
from jax import lax
from jax.experimental import pallas as pl
from jax.experimental.pallas import tpu as pltpu
from jax.sharding import Mesh
from jax.sharding import PartitionSpec as P

HD = 128
EPS = 1e-05
NEG = -1e30
SCALE = 1.0 / math.sqrt(HD)
CTX = ("x", "yl", "core")
CHIPS = ("x", "yl")
TP = ("yh", "z")
ALL = CTX + TP
BF = jnp.bfloat16
F32 = jnp.float32
RUN = 96
QB = 256
KB = 512


def rms_rows(values):
    return values * lax.rsqrt(jnp.mean(values * values, axis=-1, keepdims=True) + EPS)


def dot(left, right, dims):
    return lax.dot_general(left, right, (dims, ((), ())), preferred_element_type=F32)


def exchange(parts, axes):
    return lax.all_to_all(parts, axes, 0, 0, tiled=True)


def spread(block, axes, count):
    return exchange(jnp.broadcast_to(block[None], (count,) + block.shape), axes)


def total(parts):
    return jnp.sum(parts.astype(F32), axis=0)


def swap_core(block):
    return lax.ppermute(block, "core", [(0, 1), (1, 0)])


def after(value, *earlier):
    return lax.optimization_barrier((value,) + earlier)[0]


def thirds(values):
    high = lax.reduce_precision(values, 8, 7)
    rest = values - high
    middle = lax.reduce_precision(rest, 8, 7)
    return jnp.stack([high, middle, rest - middle]).astype(BF)


def kernel_call(body, out_shape, scratch, flops, byte_count, count):
    return pl.pallas_call(
        body,
        out_shape=out_shape,
        in_specs=[pl.BlockSpec(memory_space=pltpu.SMEM)]
        + [pl.BlockSpec(memory_space=pltpu.VMEM)] * (count - 1),
        out_specs=jax.tree.map(lambda _: pl.BlockSpec(memory_space=pltpu.VMEM), out_shape),
        scratch_shapes=scratch,
        compiler_params=pltpu.CompilerParams(vmem_limit_bytes=48 << 20),
        cost_estimate=pl.CostEstimate(
            flops=flops, bytes_accessed=byte_count, transcendentals=0
        ),
    )


CORE, CTX_AT, TP_AT, SHARDS = 32, 33, 34, 35


def forward_body(
    meta_ref, q_ref, q_come_ref, kv_ref, own_ref, other_ref, lse_ref, qs, key_pos
):
    first = meta_ref[CORE] == 0
    ctx = meta_ref[CTX_AT]
    qs[...] = jnp.zeros_like(qs)
    for run in range(2):
        rows = slice(run * RUN, run * RUN + RUN)
        qs[run * 128 : run * 128 + RUN, :] = jnp.where(
            first, q_ref[rows, :HD], q_ref[rows, HD:]
        )
        qs[256 + run * 128 : 256 + run * 128 + RUN, :] = q_come_ref[rows, :]
    down = lax.broadcasted_iota(jnp.int32, (RUN, 128), 0)
    for run in range(key_pos.shape[0] // RUN):
        key_pos[run * RUN : run * RUN + RUN, :] = down + meta_ref[run]
    lse_ref[...] = jnp.zeros_like(lse_ref)
    across = lax.broadcasted_iota(jnp.int32, (1, 128), 1)
    for part in range(4):
        owner = ctx if part < 2 else ctx + 1 - 2 * meta_ref[CORE]
        query_pos = across + meta_ref[2 * owner + part % 2]
        scores = dot(kv_ref[:, :HD], qs[part * 128 : part * 128 + 128, :], ((1,), (1,))) * SCALE
        scores = jnp.where(key_pos[...] <= query_pos, scores, NEG)
        peak = jnp.max(scores, axis=0, keepdims=True)
        weights = jnp.exp(scores - peak)
        denominator = jnp.sum(weights, axis=0, keepdims=True)
        probs = (weights * (1.0 / denominator)).astype(BF)
        result = dot(probs, kv_ref[:, HD:], ((0,), (0,))).astype(BF)
        rows = slice(part % 2 * RUN, part % 2 * RUN + RUN)
        (own_ref if part < 2 else other_ref)[rows, :] = result[:RUN, :]
        lse_ref[part : part + 1, :] = peak + jnp.log(denominator)


def embed_body(meta_ref, ids_ref, *refs):
    out_ref = refs[-1]
    rows = ids_ref.shape[0]
    lane = lax.broadcasted_iota(jnp.int32, (rows, 256), 1)
    sums = jnp.zeros((rows, 1024), F32)
    for block in range(8):
        pick = (ids_ref[...] == lane + meta_ref[SHARDS + block] * 256).astype(F32).astype(BF)
        sums += dot(pick, refs[block][...], ((1,), (0,)))
    out_ref[...] = sums.astype(BF)


def head_body(meta_ref, base_ref, embed_ref, target_ref, cot_ref, *refs):
    tables, (unit_ref, dlogits_ref, grad_ref, loss_ref, logits_ref) = refs[:8], refs[8:]
    rows = base_ref.shape[0]
    keep = jnp.where(meta_ref[TP_AT] > 0, 1.0, 0.0)
    depth_in = base_ref[...].astype(F32) + embed_ref[...].astype(F32) * keep
    inverse_rms = lax.rsqrt(jnp.mean(depth_in * depth_in, axis=-1, keepdims=True) + EPS)
    scaled = depth_in * inverse_rms
    unit = scaled.astype(BF)
    unit_ref[...] = unit
    lane = lax.broadcasted_iota(jnp.int32, (rows, 256), 1)
    peak = jnp.full((rows, 1), NEG, F32)
    for block in range(8):
        cols = slice(block * 256, block * 256 + 256)
        logits = dot(unit, tables[block][...], ((1,), (0,)))
        logits_ref[:, cols] = logits
        peak = jnp.maximum(peak, jnp.max(logits, axis=-1, keepdims=True))
    denominator = jnp.zeros((rows, 1), F32)
    chosen = jnp.zeros((rows, 1), F32)
    for block in range(8):
        cols = slice(block * 256, block * 256 + 256)
        logits = logits_ref[:, cols]
        is_target = target_ref[...] == lane + meta_ref[SHARDS + block] * 256
        chosen += jnp.sum(jnp.where(is_target, logits, 0.0), axis=-1, keepdims=True)
        terms = jnp.exp(logits - peak)
        denominator += jnp.sum(terms, axis=-1, keepdims=True)
        logits_ref[:, cols] = terms
    loss_ref[...] = jnp.log(denominator) + peak - chosen
    inverse = 1.0 / denominator
    cot = cot_ref[...]
    unit_grad = jnp.zeros((rows, 1024), F32)
    for block in range(8):
        cols = slice(block * 256, block * 256 + 256)
        start = meta_ref[SHARDS + block] * 256
        hit = jnp.where(target_ref[...] == lane + start, 1.0, 0.0)
        dlogits = (cot * (logits_ref[:, cols] * inverse - hit)).astype(BF)
        dlogits_ref[:, pl.ds(pl.multiple_of(start, 256), 256)] = dlogits
        unit_grad += dot(dlogits, tables[block][...], ((1,), (1,)))
    centre = jnp.mean(unit_grad * scaled, axis=-1, keepdims=True)
    grad_ref[...] = (inverse_rms * (unit_grad - scaled * centre)).astype(BF)


STAT_AT, OUTER_AT, SEND = 192, 224, 352


def send_body(
    meta_ref, summed_ref, fold_ref, attended_ref, lse_ref, lse_come_ref, out_ref, stat, product
):
    first = meta_ref[CORE] == 0
    summed = summed_ref[...]
    attended = attended_ref[...]
    grad = dot(summed, fold_ref[...], ((1,), (0,))).astype(BF)
    outer = dot(summed, attended, ((0,), (0,))).astype(BF)
    for block in range(16):
        out_ref[block, OUTER_AT : OUTER_AT + 64, :] = outer[block * 64 : block * 64 + 64, :HD]
        out_ref[block, OUTER_AT + 64 :, :] = outer[block * 64 : block * 64 + 64, HD:]
    ones = jnp.ones((8, 128), F32)
    for head in range(2):
        cols = slice(head * HD, head * HD + HD)
        stat[...] = jnp.zeros_like(stat)
        product[...] = jnp.zeros_like(product)
        for run in range(2):
            rows = slice(run * RUN, run * RUN + RUN)
            product[:RUN, :] = grad[rows, cols].astype(F32) * attended[rows, cols].astype(F32)
            centre = lax.dot_general(
                ones, product[...], (((1,), (1,)), ((), ())),
                preferred_element_type=F32, precision=lax.Precision.HIGHEST,
            )[:1, :]
            mine = lse_ref[run : run + 1, :]
            come = lse_come_ref[2 + run : 3 + run, :]
            lse = jnp.where(first, mine, come) if head == 0 else jnp.where(first, come, mine)
            for at, value in ((0, lse * (-1.0 / SCALE)), (3, -centre)):
                for term in range(3):
                    part = value.astype(BF).astype(F32)
                    row = run * 16 + at + term
                    stat[row : row + 1, :] = part
                    value = value - part
        packed = stat[...].astype(BF)
        for block in range(head, 16, 2):
            out_ref[block, :STAT_AT, :] = grad[:, cols]
            out_ref[block, STAT_AT:OUTER_AT, :] = packed


def backward_body(
    meta_ref, q_ref, kv_ref, come_ref, *refs
):
    normed_refs, refs = refs[:16], refs[16:]
    keep_ref, send_ref, qs, ks, vs, gs, dq, dk, dv, grads = refs
    core = meta_ref[CORE]
    first = core == 0
    total_rows = q_ref.shape[0]
    runs = total_rows // RUN
    stat_row = lax.broadcasted_iota(jnp.int32, (16, 128), 0)
    stat_lane = lax.broadcasted_iota(jnp.int32, (16, 128), 1)
    place_lse = jnp.where((stat_row == stat_lane) & (stat_lane < 3), 1.0, 0.0).astype(BF)
    place_centre = jnp.where((stat_row == stat_lane + 3) & (stat_lane < 3), 1.0, 0.0).astype(BF)
    for run in range(runs):
        src = slice(run * RUN, run * RUN + RUN)
        dst = pl.ds(pl.multiple_of(meta_ref[run], 32), RUN)
        half = slice(run % 2 * RUN, run % 2 * RUN + RUN)
        stats = come_ref[run // 2, STAT_AT + run % 2 * 16 : STAT_AT + run % 2 * 16 + 16, :]
        qs[dst, :HD] = jnp.where(first, q_ref[src, :HD], q_ref[src, HD:])
        qs[dst, HD:] = dot(stats, place_lse, ((0,), (0,))).astype(BF)[:RUN, :]
        gs[dst, :HD] = come_ref[run // 2, half, :]
        gs[dst, HD:] = dot(stats, place_centre, ((0,), (0,))).astype(BF)[:RUN, :]
        ks[dst, :HD] = kv_ref[src, :HD]
        vs[dst, :HD] = kv_ref[src, HD:]

    ks[:, HD:] = jnp.ones((total_rows, HD), BF)
    vs[:, HD:] = jnp.ones((total_rows, HD), BF)
    dk[...] = jnp.zeros_like(dk)
    dv[...] = jnp.zeros_like(dv)

    @pl.loop(0, total_rows // QB)
    def _(block):
        q_rows = pl.ds(pl.multiple_of(block * QB, QB), QB)
        q = qs[q_rows, :]
        g = gs[q_rows, :]

        def step(chunk, running, masked):
            rows = pl.ds(pl.multiple_of(chunk * KB, KB), KB)
            k = ks[rows, :]
            v = vs[rows, :]
            shifted = dot(k, q, ((1,), (1,)))
            if masked:
                key_at = lax.broadcasted_iota(jnp.int32, (KB, QB), 0) + chunk * KB
                query_at = lax.broadcasted_iota(jnp.int32, (KB, QB), 1) + block * QB
                shifted = jnp.where(key_at <= query_at, shifted, NEG)
            probs = jnp.exp(shifted * SCALE)
            score_grad = (probs * dot(v, g, ((1,), (1,)))).astype(BF)
            dv[rows, :] += dot(probs.astype(BF), g[:, :HD], ((1,), (0,)))
            dk[rows, :] += dot(score_grad, q[:, :HD], ((1,), (0,)))
            return running + dot(score_grad, k[:, :HD], ((0,), (0,)))

        last = block // (KB // QB)
        running = lax.fori_loop(
            0, last, lambda chunk, acc: step(chunk, acc, False), jnp.zeros((QB, HD), F32)
        )
        dq[q_rows, :] = step(last, running, True)

    for run in range(runs):
        src = slice(run * RUN, run * RUN + RUN)
        dst = pl.ds(pl.multiple_of(meta_ref[run], 32), RUN)
        grads[src, :HD] = (dq[dst, :] * SCALE).astype(BF)
        grads[src, HD : 2 * HD] = (dk[dst, :] * SCALE).astype(BF)
        grads[src, 2 * HD :] = dv[dst, :].astype(BF)

    sums = jnp.zeros((512, 3 * HD), F32)
    for hop in range(8):
        from_x = lax.rem(lax.div(meta_ref[CTX_AT], 4) + 4 - hop // 2, 4)
        from_yl = lax.rem(lax.div(meta_ref[CTX_AT], 2) + 2 - hop % 2, 2)
        for side in range(2):
            from_core = core if side == 0 else 1 - core
            start = (from_x * 2 + from_yl) * 384 + from_core * 192
            rows = pl.ds(pl.multiple_of(start, 192), 192)
            sums += dot(normed_refs[side * 8 + hop][...], grads[rows, :], ((0,), (0,)))
    keep_ref[...] = jnp.where(first, sums[:256], sums[256:])
    send_ref[...] = jnp.where(first, sums[256:], sums[:256])


def cut_body(meta_ref, normed_ref, *out_refs):
    at_x = lax.div(meta_ref[CTX_AT], 4)
    at_yl = lax.rem(lax.div(meta_ref[CTX_AT], 2), 2)
    for hop, out_ref in enumerate(out_refs):
        chip = lax.rem(at_x + hop // 2, 4) * 2 + lax.rem(at_yl + hop % 2, 2)
        out_ref[...] = normed_ref[:, pl.ds(pl.multiple_of(chip * 512, 512), 512)]


def widen_body(meta_ref, in_ref, out_ref):
    out_ref[...] = in_ref[...].astype(F32)


def fold_body(meta_ref, depth_ref, out_weight_ref, out_ref):
    sums = jnp.zeros((64, 2 * HD), F32)
    for shard in range(8):
        sums += dot(
            depth_ref[shard * 64 : shard * 64 + 64, :].astype(BF),
            out_weight_ref[:, shard * 512 : shard * 512 + 512],
            ((1,), (1,)),
        )
    out_ref[...] = sums.astype(BF)


def grad_out_body(meta_ref, outer_ref, depth_ref, out_ref):
    out_ref[...] = dot(outer_ref[...].astype(BF), depth_ref[...], ((0,), (1,)))


def join_body(meta_ref, keep_ref, come_ref, *out_refs):
    first = meta_ref[CORE] == 0
    for at, out_ref in enumerate(out_refs):
        cols = slice(at * HD, at * HD + HD)
        keep, come = keep_ref[:, cols], come_ref[:, cols]
        out_ref[:, :HD] = jnp.where(first, keep, come)
        out_ref[:, HD:] = jnp.where(first, come, keep)


def sum_piece_tp(part):
    rows, cols = part.shape
    return total(exchange(part.reshape(8, rows // 8, cols), TP)).astype(BF)


def gather_wide(block, axes):
    return lax.all_gather(block, axes, axis=0, tiled=True)


def per_device(
    frames,
    frame_pos,
    codes,
    loss_grad,
    w_query,
    w_key,
    w_value,
    w_out,
    w_depth_in,
    code_embed,
    code_head,
):
    rows = frames.shape[0]
    frame_total = frame_pos.shape[0]
    x, yl, core = lax.axis_index("x"), lax.axis_index("yl"), lax.axis_index("core")
    yh, z = lax.axis_index("yh"), lax.axis_index("z")
    ctx = lax.axis_index(CTX)
    tp = lax.axis_index(TP)
    first = core == 0

    shards, head_blocks, embed_blocks = [], [], []
    for block in range(4):
        far, near = block // 2, block % 2 * 2
        level = (yh + far) % 2 * 4 + (z + near + core) % 4
        head_blocks.append(lax.dynamic_index_in_dim(code_head, level, 0, False))
        embed_blocks.append(
            lax.dynamic_index_in_dim(code_embed, jnp.maximum(level - 1, 0), 0, False)
        )
    frames, *blocks = lax.optimization_barrier((frames, *head_blocks, *embed_blocks))
    for side in range(2):
        for block in range(4):
            far, near = block // 2, block % 2 * 2
            turn = near + (core if side == 0 else 1 - core)
            shards.append((yh + far) % 2 * 4 + (z + 4 - turn) % 4)
    own_blocks = []
    for at, operand in enumerate(blocks):
        far, near = at % 4 // 2, at % 2 * 2
        moves = []
        for a in range(2):
            for k in range(2):
                for h in range(2):
                    for d in range(4):
                        to = ((a + far) % 2, k, (h + far) % 2, (d + near + k) % 4)
                        moves.append(
                            (((a * 2 + k) * 2 + h) * 4 + d, ((to[0] * 2 + to[1]) * 2 + to[2]) * 4 + to[3])
                        )
        own_blocks.append(lax.ppermute(operand, ("yl", "core", "yh", "z"), moves))
    other_blocks = [swap_core(block) for block in own_blocks]
    head_tables = own_blocks[:4] + other_blocks[:4]
    embed_tables = own_blocks[4:] + other_blocks[4:]
    meta = jnp.concatenate(
        [frame_pos[::RUN], jnp.stack([core, ctx, tp] + shards).astype(jnp.int32)]
    )

    depth_cols = lax.dynamic_slice_in_dim(w_depth_in, ctx * 64, 64, 1).T
    depth_cols = kernel_call(
        widen_body, jax.ShapeDtypeStruct((64, 512), F32), [], 0, 200_000, 2
    )(meta, depth_cols)
    depth_cols = gather_wide(depth_cols, TP)
    fold_cols = kernel_call(
        fold_body, jax.ShapeDtypeStruct((64, 2 * HD), BF), [], 100_000_000, 3_000_000, 3
    )(meta, depth_cols, w_out)

    normed = rms_rows(frames.astype(F32)).astype(BF)
    key = dot(normed, w_key, ((1,), (0,))).astype(BF)
    value = dot(normed, w_value, ((1,), (0,))).astype(BF)
    query = dot(normed, w_query, ((1,), (0,))).astype(BF)

    key_value = jnp.stack(
        [jnp.concatenate([key[:, :HD], value[:, :HD]], 1),
         jnp.concatenate([key[:, HD:], value[:, HD:]], 1)]
    )
    key_value = exchange(
        jnp.broadcast_to(key_value[None], (8, 2, rows, 2 * HD)).reshape(16, rows, 2 * HD), CTX
    ).reshape(frame_total, 2 * HD)
    query_all = lax.all_gather(query, CTX, axis=0, tiled=True)
    query_come = swap_core(jnp.where(first, query[:, HD:], query[:, :HD]))

    own_part, other_part, lse = kernel_call(
        forward_body,
        (
            jax.ShapeDtypeStruct((rows, HD), BF),
            jax.ShapeDtypeStruct((rows, HD), BF),
            jax.ShapeDtypeStruct((8, 128), F32),
        ),
        [pltpu.VMEM((512, HD), BF), pltpu.VMEM((frame_total, 128), jnp.int32)],
        2_000_000_000, 4_000_000, 4,
    )(meta, query, query_come, after(key_value, *own_blocks[4:]))
    come_part = swap_core(other_part)
    lse_come = swap_core(lse)
    attended = jnp.where(
        first,
        jnp.concatenate([own_part, come_part], 1),
        jnp.concatenate([come_part, own_part], 1),
    )
    fold = spread(after(fold_cols, key_value), CTX, 16).reshape(1024, 2 * HD)

    pieces = kernel_call(
        cut_body, (jax.ShapeDtypeStruct((rows, 512), BF),) * 8, [], 0, 3_000_000, 2
    )(meta, after(normed, key_value))
    normed_own = []
    for hop, piece in enumerate(pieces):
        moves = [
            (a * 2 + b, (a + hop // 2) % 4 * 2 + (b + hop % 2) % 2)
            for a in range(4) for b in range(2)
        ]
        normed_own.append(lax.ppermute(piece, CHIPS, moves) if hop else piece)
    normed_other = [swap_core(piece) for piece in normed_own]

    base = sum_piece_tp(dot(attended, fold, ((1,), (1,))).astype(BF))
    base = spread(after(base, query_all, *own_blocks), TP, 8).reshape(rows, 1024)

    level_ids = jnp.arange(8, dtype=jnp.int32)[None, :]
    target = jnp.sum(jnp.where(level_ids == tp, codes, 0), axis=1, keepdims=True)
    cotangent = jnp.sum(jnp.where(level_ids == tp, loss_grad, 0.0), axis=1, keepdims=True)
    previous = jnp.sum(jnp.where(level_ids + 1 == tp, codes, 0), axis=1, keepdims=True)
    embedded = kernel_call(
        embed_body, jax.ShapeDtypeStruct((rows, 1024), BF), [], 800_000_000, 5_000_000, 10
    )(meta, previous, *embed_tables)
    unit, dlogits, depth_grad, loss = kernel_call(
        head_body,
        (
            jax.ShapeDtypeStruct((rows, 1024), BF),
            jax.ShapeDtypeStruct((rows, 2048), BF),
            jax.ShapeDtypeStruct((rows, 1024), BF),
            jax.ShapeDtypeStruct((rows, 1), F32),
        ),
        [pltpu.VMEM((rows, 2048), F32)],
        2_000_000_000, 6_000_000, 13,
    )(meta, base, after(embedded, *normed_own), target, cotangent, *head_tables)

    summed = sum_piece_tp(depth_grad)
    unit, dlogits = after(unit, summed), after(dlogits, summed)
    summed = spread(summed, TP, 8).reshape(rows, 1024)

    unit_blocks = unit.reshape(rows, 8, 2, 64)
    unit_keep = lax.dynamic_index_in_dim(unit_blocks, core, 2, False).reshape(rows, 512)
    unit_send = lax.dynamic_index_in_dim(unit_blocks, 1 - core, 2, False).reshape(rows, 512)
    head_come = swap_core(dot(unit_send, dlogits, ((0,), (0,))).astype(BF))
    head_part = (dot(unit_keep, dlogits, ((0,), (0,))) + head_come.astype(F32)).astype(BF)
    head_sum = lax.psum_scatter(head_part, CHIPS, scatter_dimension=0, tiled=True)

    send = kernel_call(
        send_body,
        jax.ShapeDtypeStruct((16, SEND, 128), BF),
        [pltpu.VMEM((32, 128), F32), pltpu.VMEM((128, 128), F32)],
        400_000_000, 3_000_000, 6,
    )(meta, after(summed, head_part, *normed_other), fold, attended, lse, lse_come)
    come = exchange(send, CTX)

    outer_own = total(come[:, OUTER_AT:])
    outer_own = jnp.concatenate([outer_own[:64], outer_own[64:]], axis=1)
    outer = gather_wide(outer_own, CTX)

    weights_keep, weights_send = kernel_call(
        backward_body,
        (jax.ShapeDtypeStruct((256, 3 * HD), F32), jax.ShapeDtypeStruct((256, 3 * HD), F32)),
        [pltpu.VMEM((frame_total, 2 * HD), BF)] * 4
        + [pltpu.VMEM((frame_total, HD), F32)] * 3
        + [pltpu.VMEM((frame_total, 3 * HD), BF)],
        25_000_000_000, 8_000_000, 20,
    )(meta, query_all, key_value, come, *normed_own, *normed_other)
    weights_come = swap_core(weights_send)
    grad_query, grad_key, grad_value = kernel_call(
        join_body, (jax.ShapeDtypeStruct((256, 2 * HD), F32),) * 3, [], 0, 2_000_000, 3
    )(meta, weights_keep, weights_come)

    depth_half = lax.dynamic_slice_in_dim(w_depth_in, core * 256, 256, 0)
    moves = [
        (c * 8 + t, (2 * t + c % 2) * 8 + c // 2) for c in range(16) for t in range(8)
    ]
    depth_rows = lax.ppermute(after(depth_half, base), ALL, moves)
    grad_out = kernel_call(
        grad_out_body, jax.ShapeDtypeStruct((2 * HD, 256), F32), [], 100_000_000, 2_000_000, 3
    )(meta, outer, depth_rows)
    depth_part = dot(outer_own.astype(BF), w_out, ((1,), (0,))).astype(BF)
    loss_row = jnp.pad(thirds(loss[:, 0]).reshape(1, 576), ((0, 15), (0, 448)))
    tail = jnp.concatenate(
        [
            depth_part.reshape(64, 8, 512).transpose(1, 0, 2),
            jnp.broadcast_to(loss_row.reshape(1, 32, 512), (8, 32, 512)),
        ],
        axis=1,
    )
    tail = exchange(tail, TP)
    grad_depth_in = total(tail[:, :64]).T
    losses = tail[:, 64:].reshape(8, 16, 1024)[:, 0, :576].reshape(8, 3, rows)
    token_loss = total(losses.transpose(1, 2, 0))
    head_sum = after(head_sum, tail).reshape(64, 8, 256).transpose(1, 0, 2)
    grad_head = exchange(head_sum, TP).astype(F32)
    return (token_loss, grad_query, grad_key, grad_value, grad_out, grad_depth_in, grad_head)


def solution(mesh):
    fine = Mesh(mesh.devices.reshape(4, 2, 2, 2, 4), ALL)
    in_specs = (
        P(CTX, None),
        P(),
        P(CTX, None),
        P(CTX, None),
        P(None, TP),
        P(None, TP),
        P(None, TP),
        P(TP, None),
        P(TP, None),
        P(None, TP, None),
        P(None, None, TP),
    )
    out_specs = (
        P(CTX, None),
        P(CTX, TP),
        P(CTX, TP),
        P(CTX, TP),
        P(TP, CTX),
        P(TP, CTX),
        P(None, CTX, TP),
    )
    return jax.shard_map(
        per_device, mesh=fine, in_specs=in_specs, out_specs=out_specs, check_vma=False
    )
```

```python
import math

import jax
import jax.numpy as jnp
from jax import lax
from jax.experimental import pallas as pl
from jax.experimental.pallas import tpu as pltpu
from jax.sharding import Mesh
from jax.sharding import PartitionSpec as P

HD = 128
EPS = 1e-05
NEG = -1e30
SCALE = 1.0 / math.sqrt(HD)
CTX = ("x", "yl", "core")
CHIPS = ("x", "yl")
TP = ("yh", "z")
ALL = CTX + TP
BF = jnp.bfloat16
F32 = jnp.float32
RUN = 96
QB = 256
KB = 512


def rms_rows(values):
    return values * lax.rsqrt(jnp.mean(values * values, axis=-1, keepdims=True) + EPS)


def dot(left, right, dims):
    return lax.dot_general(left, right, (dims, ((), ())), preferred_element_type=F32)


def exchange(parts, axes):
    return lax.all_to_all(parts, axes, 0, 0, tiled=True)


def spread(block, axes, count):
    return exchange(jnp.broadcast_to(block[None], (count,) + block.shape), axes)


def total(parts):
    return jnp.sum(parts.astype(F32), axis=0)


def swap_core(block):
    return lax.ppermute(block, "core", [(0, 1), (1, 0)])


def after(value, *earlier):
    return lax.optimization_barrier((value,) + earlier)[0]


def thirds(values):
    high = lax.reduce_precision(values, 8, 7)
    rest = values - high
    middle = lax.reduce_precision(rest, 8, 7)
    return jnp.stack([high, middle, rest - middle]).astype(BF)


def kernel_call(body, out_shape, scratch, flops, byte_count, count, far_in=0):
    near, far = pl.BlockSpec(memory_space=pltpu.VMEM), pl.BlockSpec(memory_space=pl.ANY)
    return pl.pallas_call(
        body,
        out_shape=out_shape,
        in_specs=[pl.BlockSpec(memory_space=pltpu.SMEM)]
        + [near] * (count - 1 - far_in)
        + [far] * far_in,
        out_specs=jax.tree.map(lambda _: near, out_shape),
        scratch_shapes=scratch,
        compiler_params=pltpu.CompilerParams(vmem_limit_bytes=48 << 20),
        cost_estimate=pl.CostEstimate(
            flops=flops, bytes_accessed=byte_count, transcendentals=0
        ),
    )


CORE, CTX_AT, TP_AT, SHARDS, LEVELS = 32, 33, 34, 35, 43


def forward_body(
    meta_ref, q_ref, q_come_ref, kv_ref, own_ref, other_ref, lse_ref, qs, key_pos
):
    first = meta_ref[CORE] == 0
    ctx = meta_ref[CTX_AT]
    qs[...] = jnp.zeros_like(qs)
    for run in range(2):
        rows = slice(run * RUN, run * RUN + RUN)
        qs[run * 128 : run * 128 + RUN, :] = jnp.where(
            first, q_ref[rows, :HD], q_ref[rows, HD:]
        )
        qs[256 + run * 128 : 256 + run * 128 + RUN, :] = q_come_ref[rows, :]
    down = lax.broadcasted_iota(jnp.int32, (RUN, 128), 0)
    for run in range(key_pos.shape[0] // RUN):
        key_pos[run * RUN : run * RUN + RUN, :] = down + meta_ref[run]
    lse_ref[...] = jnp.zeros_like(lse_ref)
    across = lax.broadcasted_iota(jnp.int32, (1, 128), 1)
    for part in range(4):
        owner = ctx if part < 2 else ctx + 1 - 2 * meta_ref[CORE]
        query_pos = across + meta_ref[2 * owner + part % 2]
        scores = dot(kv_ref[:, :HD], qs[part * 128 : part * 128 + 128, :], ((1,), (1,))) * SCALE
        scores = jnp.where(key_pos[...] <= query_pos, scores, NEG)
        peak = jnp.max(scores, axis=0, keepdims=True)
        weights = jnp.exp(scores - peak)
        denominator = jnp.sum(weights, axis=0, keepdims=True)
        probs = (weights * (1.0 / denominator)).astype(BF)
        result = dot(probs, kv_ref[:, HD:], ((0,), (0,))).astype(BF)
        rows = slice(part % 2 * RUN, part % 2 * RUN + RUN)
        (own_ref if part < 2 else other_ref)[rows, :] = result[:RUN, :]
        lse_ref[part : part + 1, :] = peak + jnp.log(denominator)


def embed_body(meta_ref, ids_ref, *refs):
    out_ref = refs[-1]
    rows = ids_ref.shape[0]
    lane = lax.broadcasted_iota(jnp.int32, (rows, 256), 1)
    sums = [jnp.zeros((rows, 256), F32) for _ in range(4)]
    for block in range(8):
        pick = (ids_ref[...] == lane + meta_ref[SHARDS + block] * 256).astype(F32).astype(BF)
        for quarter in range(4):
            table = refs[block][1024 + quarter * 256 : 1280 + quarter * 256, :]
            sums[quarter] += dot(pick, table, ((1,), (0,)))
    for quarter in range(4):
        out_ref[:, quarter * 256 : quarter * 256 + 256] = sums[quarter].astype(BF)


def head_body(meta_ref, base_ref, embed_ref, target_ref, cot_ref, *refs):
    tables, (unit_ref, dlogits_ref, grad_ref, loss_ref, logits_ref) = refs[:8], refs[8:]
    rows = base_ref.shape[0]
    keep = jnp.where(meta_ref[TP_AT] > 0, 1.0, 0.0)
    depth_in = base_ref[...].astype(F32) + embed_ref[...].astype(F32) * keep
    inverse_rms = lax.rsqrt(jnp.mean(depth_in * depth_in, axis=-1, keepdims=True) + EPS)
    scaled = depth_in * inverse_rms
    unit = scaled.astype(BF)
    unit_ref[...] = unit
    lane = lax.broadcasted_iota(jnp.int32, (rows, 256), 1)
    peak = jnp.full((rows, 1), NEG, F32)
    for block in range(8):
        cols = slice(block * 256, block * 256 + 256)
        logits = dot(unit, tables[block][:1024, :], ((1,), (0,)))
        logits_ref[:, cols] = logits
        peak = jnp.maximum(peak, jnp.max(logits, axis=-1, keepdims=True))
    denominator = jnp.zeros((rows, 1), F32)
    chosen = jnp.zeros((rows, 1), F32)
    for block in range(8):
        cols = slice(block * 256, block * 256 + 256)
        logits = logits_ref[:, cols]
        is_target = target_ref[...] == lane + meta_ref[SHARDS + block] * 256
        chosen += jnp.sum(jnp.where(is_target, logits, 0.0), axis=-1, keepdims=True)
        terms = jnp.exp(logits - peak)
        denominator += jnp.sum(terms, axis=-1, keepdims=True)
        logits_ref[:, cols] = terms
    loss_ref[...] = jnp.log(denominator) + peak - chosen
    inverse = 1.0 / denominator
    cot = cot_ref[...]
    unit_grad = jnp.zeros((rows, 1024), F32)
    for block in range(8):
        cols = slice(block * 256, block * 256 + 256)
        start = meta_ref[SHARDS + block] * 256
        hit = jnp.where(target_ref[...] == lane + start, 1.0, 0.0)
        dlogits = (cot * (logits_ref[:, cols] * inverse - hit)).astype(BF)
        dlogits_ref[:, pl.ds(pl.multiple_of(start, 256), 256)] = dlogits
        unit_grad += dot(dlogits, tables[block][:1024, :], ((1,), (1,)))
    centre = jnp.mean(unit_grad * scaled, axis=-1, keepdims=True)
    grad_ref[...] = (inverse_rms * (unit_grad - scaled * centre)).astype(BF)


STAT_AT, OUTER_AT, SEND = 192, 224, 352


def send_body(
    meta_ref, summed_ref, fold_ref, attended_ref, lse_ref, lse_come_ref, out_ref, stat, product
):
    first = meta_ref[CORE] == 0
    summed = summed_ref[...]
    attended = attended_ref[...]
    grad = dot(summed, fold_ref[...], ((1,), (0,))).astype(BF)
    outer = dot(summed, attended, ((0,), (0,))).astype(BF)
    for block in range(16):
        out_ref[block, OUTER_AT : OUTER_AT + 64, :] = outer[block * 64 : block * 64 + 64, :HD]
        out_ref[block, OUTER_AT + 64 :, :] = outer[block * 64 : block * 64 + 64, HD:]
    ones = jnp.ones((8, 128), F32)
    for head in range(2):
        cols = slice(head * HD, head * HD + HD)
        stat[...] = jnp.zeros_like(stat)
        product[...] = jnp.zeros_like(product)
        for run in range(2):
            rows = slice(run * RUN, run * RUN + RUN)
            product[:RUN, :] = grad[rows, cols].astype(F32) * attended[rows, cols].astype(F32)
            centre = lax.dot_general(
                ones, product[...], (((1,), (1,)), ((), ())),
                preferred_element_type=F32, precision=lax.Precision.HIGHEST,
            )[:1, :]
            mine = lse_ref[run : run + 1, :]
            come = lse_come_ref[2 + run : 3 + run, :]
            lse = jnp.where(first, mine, come) if head == 0 else jnp.where(first, come, mine)
            for at, value in ((0, lse * (-1.0 / SCALE)), (3, -centre)):
                for term in range(3):
                    part = value.astype(BF).astype(F32)
                    row = run * 16 + at + term
                    stat[row : row + 1, :] = part
                    value = value - part
        packed = stat[...].astype(BF)
        for block in range(head, 16, 2):
            out_ref[block, :STAT_AT, :] = grad[:, cols]
            out_ref[block, STAT_AT:OUTER_AT, :] = packed


def backward_body(meta_ref, q_ref, kv_ref, come_ref, grads, qs, ks, vs, gs, dq, dk, dv):
    core = meta_ref[CORE]
    first = core == 0
    total_rows = q_ref.shape[0]
    runs = total_rows // RUN
    stat_row = lax.broadcasted_iota(jnp.int32, (16, 128), 0)
    stat_lane = lax.broadcasted_iota(jnp.int32, (16, 128), 1)
    place_lse = jnp.where((stat_row == stat_lane) & (stat_lane < 3), 1.0, 0.0).astype(BF)
    place_centre = jnp.where((stat_row == stat_lane + 3) & (stat_lane < 3), 1.0, 0.0).astype(BF)
    for run in range(runs):
        src = slice(run * RUN, run * RUN + RUN)
        dst = pl.ds(pl.multiple_of(meta_ref[run], 32), RUN)
        half = slice(run % 2 * RUN, run % 2 * RUN + RUN)
        stats = come_ref[run // 2, STAT_AT + run % 2 * 16 : STAT_AT + run % 2 * 16 + 16, :]
        qs[dst, :HD] = jnp.where(first, q_ref[src, :HD], q_ref[src, HD:])
        qs[dst, HD:] = dot(stats, place_lse, ((0,), (0,))).astype(BF)[:RUN, :]
        gs[dst, :HD] = come_ref[run // 2, half, :]
        gs[dst, HD:] = dot(stats, place_centre, ((0,), (0,))).astype(BF)[:RUN, :]
        ks[dst, :HD] = kv_ref[src, :HD]
        vs[dst, :HD] = kv_ref[src, HD:]

    ks[:, HD:] = jnp.ones((total_rows, HD), BF)
    vs[:, HD:] = jnp.ones((total_rows, HD), BF)
    dk[...] = jnp.zeros_like(dk)
    dv[...] = jnp.zeros_like(dv)

    @pl.loop(0, total_rows // QB)
    def _(block):
        q_rows = pl.ds(pl.multiple_of(block * QB, QB), QB)
        q = qs[q_rows, :]
        g = gs[q_rows, :]

        def step(chunk, running, masked):
            rows = pl.ds(pl.multiple_of(chunk * KB, KB), KB)
            k = ks[rows, :]
            v = vs[rows, :]
            shifted = dot(k, q, ((1,), (1,)))
            if masked:
                key_at = lax.broadcasted_iota(jnp.int32, (KB, QB), 0) + chunk * KB
                query_at = lax.broadcasted_iota(jnp.int32, (KB, QB), 1) + block * QB
                shifted = jnp.where(key_at <= query_at, shifted, NEG)
            probs = jnp.exp(shifted * SCALE)
            score_grad = (probs * dot(v, g, ((1,), (1,)))).astype(BF)
            dv[rows, :] += dot(probs.astype(BF), g[:, :HD], ((1,), (0,)))
            dk[rows, :] += dot(score_grad, q[:, :HD], ((1,), (0,)))
            return running + dot(score_grad, k[:, :HD], ((0,), (0,)))

        last = block // (KB // QB)
        running = lax.fori_loop(
            0, last, lambda chunk, acc: step(chunk, acc, False), jnp.zeros((QB, HD), F32)
        )
        dq[q_rows, :] = step(last, running, True)

    for run in range(runs):
        src = slice(run * RUN, run * RUN + RUN)
        dst = pl.ds(pl.multiple_of(meta_ref[run], 32), RUN)
        grads[src, :HD] = (dq[dst, :] * SCALE).astype(BF)
        grads[src, HD : 2 * HD] = (dk[dst, :] * SCALE).astype(BF)
        grads[src, 2 * HD :] = dv[dst, :].astype(BF)


def weight_body(meta_ref, grads_ref, *refs):
    normed_refs, (keep_ref, send_ref) = refs[:16], refs[16:]
    core = meta_ref[CORE]
    first = core == 0
    sums = jnp.zeros((512, 3 * HD), F32)
    for hop in range(8):
        from_x = lax.rem(lax.div(meta_ref[CTX_AT], 4) + 4 - hop // 2, 4)
        from_yl = lax.rem(lax.div(meta_ref[CTX_AT], 2) + hop % 2, 2)
        for side in range(2):
            from_core = core if side == 0 else 1 - core
            start = (from_x * 2 + from_yl) * 384 + from_core * 192
            rows = pl.ds(pl.multiple_of(start, 192), 192)
            sums += dot(normed_refs[side * 8 + hop][...], grads_ref[rows, :], ((0,), (0,)))
    keep_ref[...] = jnp.where(first, sums[:256], sums[256:])
    send_ref[...] = jnp.where(first, sums[256:], sums[:256])


def cut_body(meta_ref, normed_ref, *out_refs):
    at_x = lax.div(meta_ref[CTX_AT], 4)
    at_yl = lax.rem(lax.div(meta_ref[CTX_AT], 2), 2)
    for hop, out_ref in enumerate(out_refs):
        chip = lax.rem(at_x + hop // 2, 4) * 2 + lax.rem(at_yl + hop % 2, 2)
        out_ref[...] = normed_ref[:, pl.ds(pl.multiple_of(chip * 512, 512), 512)]


def pack_body(meta_ref, head_ref, embed_ref, *refs):
    out_refs, sems = refs[:4], refs[4]
    copies = []
    for block, out_ref in enumerate(out_refs):
        level = meta_ref[LEVELS + block]
        copies.append((head_ref.at[level], out_ref.at[pl.ds(0, 1024), :]))
        for quarter in range(4):
            copies.append((
                embed_ref.at[jnp.maximum(level - 1, 0), :, pl.ds(quarter * 256, 256)],
                out_ref.at[pl.ds(1024 + quarter * 256, 256), :],
            ))
    copies = [
        pltpu.make_async_copy(src, dst, sems.at[at]) for at, (src, dst) in enumerate(copies)
    ]
    for copy in copies:
        copy.start()
    for copy in copies:
        copy.wait()


def grad_out_body(meta_ref, outer_ref, depth_ref, out_ref):
    out_ref[...] = dot(outer_ref[...].astype(BF), depth_ref[...], ((0,), (1,)))


def join_body(meta_ref, keep_ref, come_ref, *out_refs):
    first = meta_ref[CORE] == 0
    for at, out_ref in enumerate(out_refs):
        cols = slice(at * HD, at * HD + HD)
        keep, come = keep_ref[:, cols], come_ref[:, cols]
        out_ref[:, :HD] = jnp.where(first, keep, come)
        out_ref[:, HD:] = jnp.where(first, come, keep)


def sum_piece_tp(part):
    rows, cols = part.shape
    return total(exchange(part.reshape(8, rows // 8, cols), TP)).astype(BF)


def gather_wide(block, axes):
    return lax.all_gather(block, axes, axis=0, tiled=True)


def per_device(
    frames,
    frame_pos,
    codes,
    loss_grad,
    w_query,
    w_key,
    w_value,
    w_out,
    w_depth_in,
    code_embed,
    code_head,
):
    rows = frames.shape[0]
    frame_total = frame_pos.shape[0]
    x, yl, core = lax.axis_index("x"), lax.axis_index("yl"), lax.axis_index("core")
    yh, z = lax.axis_index("yh"), lax.axis_index("z")
    ctx = lax.axis_index(CTX)
    tp = lax.axis_index(TP)
    first = core == 0

    levels, shards, turns = [], [], []
    for block in range(4):
        far, near = block // 2, block % 2 * 2
        levels.append((yh + far) % 2 * 4 + (z + near + core) % 4)
    for side in range(2):
        for block in range(4):
            far, near = block // 2, block % 2 * 2
            turn = near + (core if side == 0 else 1 - core)
            shards.append((yh + far) % 2 * 4 + (z + 4 - turn) % 4)
    meta = jnp.concatenate(
        [frame_pos[::RUN], jnp.stack([core, ctx, tp] + shards + levels).astype(jnp.int32)]
    )
    packed = kernel_call(
        pack_body, (jax.ShapeDtypeStruct((2048, 256), BF),) * 4,
        [pltpu.SemaphoreType.DMA((20,))], 0, 8_000_000, 3, 2,
    )(meta, code_head, code_embed)
    own_blocks = []
    for block, operand in enumerate(packed):
        far, near = block // 2, block % 2 * 2
        moves = []
        for a in range(2):
            for k in range(2):
                for h in range(2):
                    for d in range(4):
                        to = ((a + far) % 2, k, (h + far) % 2, (d + near + k) % 4)
                        moves.append(
                            (((a * 2 + k) * 2 + h) * 4 + d, ((to[0] * 2 + to[1]) * 2 + to[2]) * 4 + to[3])
                        )
        own_blocks.append(lax.ppermute(operand, ("yl", "core", "yh", "z"), moves))
    tables = own_blocks + [swap_core(block) for block in own_blocks]

    depth_cols = lax.dynamic_slice_in_dim(w_depth_in, ctx * 64, 64, 1).T
    depth_cols = spread(depth_cols, TP, 8)
    fold_cols = lax.dot_general(
        depth_cols, w_out.reshape(256, 8, 512), (((0, 2), (1, 2)), ((), ())),
        preferred_element_type=F32,
    ).astype(BF)

    normed = rms_rows(frames.astype(F32)).astype(BF)
    key = dot(normed, w_key, ((1,), (0,))).astype(BF)
    value = dot(normed, w_value, ((1,), (0,))).astype(BF)
    query = dot(normed, w_query, ((1,), (0,))).astype(BF)

    key_value = jnp.stack(
        [jnp.concatenate([key[:, :HD], value[:, :HD]], 1),
         jnp.concatenate([key[:, HD:], value[:, HD:]], 1)]
    )
    key_value = exchange(
        after(
            jnp.broadcast_to(key_value[None], (8, 2, rows, 2 * HD)).reshape(16, rows, 2 * HD),
            depth_cols,
            *packed,
        ),
        CTX,
    ).reshape(frame_total, 2 * HD)
    query_all = lax.all_gather(after(query, key_value), CTX, axis=0, tiled=True)
    query_come = swap_core(jnp.where(first, query[:, HD:], query[:, :HD]))

    own_part, other_part, lse = kernel_call(
        forward_body,
        (
            jax.ShapeDtypeStruct((rows, HD), BF),
            jax.ShapeDtypeStruct((rows, HD), BF),
            jax.ShapeDtypeStruct((8, 128), F32),
        ),
        [pltpu.VMEM((512, HD), BF), pltpu.VMEM((frame_total, 128), jnp.int32)],
        2_000_000_000, 4_000_000, 4,
    )(meta, query, query_come, key_value)
    come_part = swap_core(other_part)
    lse_come = swap_core(lse)
    attended = jnp.where(
        first,
        jnp.concatenate([own_part, come_part], 1),
        jnp.concatenate([come_part, own_part], 1),
    )
    fold = spread(after(fold_cols, key_value, own_blocks[0]), CTX, 16).reshape(1024, 2 * HD)

    base = sum_piece_tp(dot(after(attended, own_blocks[1]), fold, ((1,), (1,))).astype(BF))
    base = spread(base, TP, 8).reshape(rows, 1024)

    level_ids = jnp.arange(8, dtype=jnp.int32)[None, :]
    target = jnp.sum(jnp.where(level_ids == tp, codes, 0), axis=1, keepdims=True)
    cotangent = jnp.sum(jnp.where(level_ids == tp, loss_grad, 0.0), axis=1, keepdims=True)
    previous = jnp.sum(jnp.where(level_ids + 1 == tp, codes, 0), axis=1, keepdims=True)
    embedded = kernel_call(
        embed_body, jax.ShapeDtypeStruct((rows, 1024), BF), [], 800_000_000, 5_000_000, 10
    )(meta, previous, *tables)
    unit, dlogits, depth_grad, loss = kernel_call(
        head_body,
        (
            jax.ShapeDtypeStruct((rows, 1024), BF),
            jax.ShapeDtypeStruct((rows, 2048), BF),
            jax.ShapeDtypeStruct((rows, 1024), BF),
            jax.ShapeDtypeStruct((rows, 1), F32),
        ),
        [pltpu.VMEM((rows, 2048), F32)],
        2_000_000_000, 6_000_000, 13,
    )(meta, base, embedded, target, cotangent, *tables)

    normed_own = []
    cuts = kernel_call(
        cut_body, (jax.ShapeDtypeStruct((rows, 512), BF),) * 8, [], 0, 3_000_000, 2
    )(meta, after(normed, depth_grad))
    for hop, piece in enumerate(cuts):
        moves = [
            (a * 2 + b, (a + hop // 2) % 4 * 2 + (b + hop % 2) % 2)
            for a in range(4) for b in range(2)
        ]
        normed_own.append(lax.ppermute(piece, CHIPS, moves) if hop else piece)
    normed_other = [swap_core(piece) for piece in normed_own]

    summed = sum_piece_tp(after(depth_grad, query_all))
    summed = spread(after(summed, *normed_own), TP, 8).reshape(rows, 1024)

    send = kernel_call(
        send_body,
        jax.ShapeDtypeStruct((16, SEND, 128), BF),
        [pltpu.VMEM((32, 128), F32), pltpu.VMEM((128, 128), F32)],
        400_000_000, 3_000_000, 6,
    )(meta, after(summed, *normed_other), fold, attended, lse, lse_come)
    come = exchange(send, CTX)

    unit, dlogits = after(unit, send), after(dlogits, send)
    unit_blocks = unit.reshape(rows, 8, 2, 64)
    unit_keep = lax.dynamic_index_in_dim(unit_blocks, core, 2, False).reshape(rows, 512)
    unit_send = lax.dynamic_index_in_dim(unit_blocks, 1 - core, 2, False).reshape(rows, 512)
    head_come = swap_core(dot(unit_send, dlogits, ((0,), (0,))).astype(BF))
    head_part = (dot(unit_keep, dlogits, ((0,), (0,))) + head_come.astype(F32)).astype(BF)
    head_parts = exchange(after(head_part, come).reshape(8, 64, 2048), CHIPS)

    outer_own = total(come[:, OUTER_AT:])
    outer_own = jnp.concatenate([outer_own[:64], outer_own[64:]], axis=1)
    outer = gather_wide(outer_own, CTX)

    grads = kernel_call(
        backward_body,
        jax.ShapeDtypeStruct((frame_total, 3 * HD), BF),
        [pltpu.VMEM((frame_total, 2 * HD), BF)] * 4 + [pltpu.VMEM((frame_total, HD), F32)] * 3,
        25_000_000_000, 8_000_000, 4,
    )(meta, query_all, key_value, after(come, outer_own, head_part))
    head_sum = total(after(head_parts, grads)).astype(BF)
    weights_keep, weights_send = kernel_call(
        weight_body,
        (jax.ShapeDtypeStruct((256, 3 * HD), F32), jax.ShapeDtypeStruct((256, 3 * HD), F32)),
        [], 1_200_000_000, 6_000_000, 18,
    )(meta, grads, *normed_own, *normed_other)
    weights_come = swap_core(weights_send)
    grad_query, grad_key, grad_value = kernel_call(
        join_body, (jax.ShapeDtypeStruct((256, 2 * HD), F32),) * 3, [], 0, 2_000_000, 3
    )(meta, weights_keep, weights_come)

    depth_half = lax.dynamic_slice_in_dim(w_depth_in, core * 256, 256, 0)
    moves = [
        (c * 8 + t, (2 * t + c % 2) * 8 + c // 2) for c in range(16) for t in range(8)
    ]
    depth_rows = lax.ppermute(after(depth_half, base), ALL, moves)
    grad_out = kernel_call(
        grad_out_body, jax.ShapeDtypeStruct((2 * HD, 256), F32), [], 100_000_000, 2_000_000, 3
    )(meta, outer, depth_rows)
    depth_part = dot(outer_own.astype(BF), w_out, ((1,), (0,))).astype(BF)
    loss_row = jnp.pad(thirds(loss[:, 0]).reshape(1, 576), ((0, 15), (0, 192)))
    tail = jnp.concatenate(
        [
            jnp.concatenate(
                [depth_part.reshape(64, 8, 512), head_sum.reshape(64, 8, 256)], axis=2
            ).transpose(1, 0, 2),
            jnp.broadcast_to(loss_row[None], (8, 16, 768)),
        ],
        axis=1,
    )
    tail = exchange(tail, TP)
    grad_depth_in = total(tail[:, :64, :512]).T
    grad_head = tail[:, :64, 512:].astype(F32)
    token_loss = total(tail[:, 64, :576].reshape(8, 3, rows).transpose(1, 2, 0))
    return (token_loss, grad_query, grad_key, grad_value, grad_out, grad_depth_in, grad_head)


def solution(mesh):
    fine = Mesh(mesh.devices.reshape(4, 2, 2, 2, 4), ALL)
    in_specs = (
        P(CTX, None),
        P(),
        P(CTX, None),
        P(CTX, None),
        P(None, TP),
        P(None, TP),
        P(None, TP),
        P(TP, None),
        P(TP, None),
        P(None, TP, None),
        P(None, None, TP),
    )
    out_specs = (
        P(CTX, None),
        P(CTX, TP),
        P(CTX, TP),
        P(CTX, TP),
        P(TP, CTX),
        P(TP, CTX),
        P(None, CTX, TP),
    )
    return jax.shard_map(
        per_device, mesh=fine, in_specs=in_specs, out_specs=out_specs, check_vma=False
    )
```

```python
import math

import jax
import jax.numpy as jnp
from jax import lax
from jax.experimental import pallas as pl
from jax.experimental.pallas import tpu as pltpu
from jax.sharding import Mesh
from jax.sharding import PartitionSpec as P

HD = 128
EPS = 1e-05
NEG = -1e30
SCALE = 1.0 / math.sqrt(HD)
CTX = ("x", "yl", "core")
CHIPS = ("x", "yl")
TP = ("yh", "z")
ALL = CTX + TP
BF = jnp.bfloat16
F32 = jnp.float32
RUN = 96
QB = 256
KB = 512


def rms_rows(values):
    return values * lax.rsqrt(jnp.mean(values * values, axis=-1, keepdims=True) + EPS)


def dot(left, right, dims):
    return lax.dot_general(left, right, (dims, ((), ())), preferred_element_type=F32)


def exchange(parts, axes):
    return lax.all_to_all(parts, axes, 0, 0, tiled=True)


def spread(block, axes, count):
    return exchange(jnp.broadcast_to(block[None], (count,) + block.shape), axes)


def total(parts):
    return jnp.sum(parts.astype(F32), axis=0)


def swap_core(block):
    return lax.ppermute(block, "core", [(0, 1), (1, 0)])


def after(value, *earlier):
    return lax.optimization_barrier((value,) + earlier)[0]


def thirds(values):
    high = lax.reduce_precision(values, 8, 7)
    rest = values - high
    middle = lax.reduce_precision(rest, 8, 7)
    return jnp.stack([high, middle, rest - middle]).astype(BF)


def kernel_call(body, out_shape, scratch, flops, byte_count, count, far_in=0):
    near, far = pl.BlockSpec(memory_space=pltpu.VMEM), pl.BlockSpec(memory_space=pl.ANY)
    return pl.pallas_call(
        body,
        out_shape=out_shape,
        in_specs=[pl.BlockSpec(memory_space=pltpu.SMEM)]
        + [near] * (count - 1 - far_in)
        + [far] * far_in,
        out_specs=jax.tree.map(lambda _: near, out_shape),
        scratch_shapes=scratch,
        compiler_params=pltpu.CompilerParams(vmem_limit_bytes=48 << 20),
        cost_estimate=pl.CostEstimate(
            flops=flops, bytes_accessed=byte_count, transcendentals=0
        ),
    )


CORE, CTX_AT, TP_AT, SHARDS, LEVELS = 32, 33, 34, 35, 43


def forward_body(
    meta_ref, q_ref, q_come_ref, kv_ref, own_ref, other_ref, lse_ref, qs, key_pos
):
    first = meta_ref[CORE] == 0
    ctx = meta_ref[CTX_AT]
    qs[...] = jnp.zeros_like(qs)
    for run in range(2):
        rows = slice(run * RUN, run * RUN + RUN)
        qs[run * 128 : run * 128 + RUN, :] = jnp.where(
            first, q_ref[rows, :HD], q_ref[rows, HD:]
        )
        qs[256 + run * 128 : 256 + run * 128 + RUN, :] = q_come_ref[rows, :]
    down = lax.broadcasted_iota(jnp.int32, (RUN, 128), 0)
    for run in range(key_pos.shape[0] // RUN):
        key_pos[run * RUN : run * RUN + RUN, :] = down + meta_ref[run]
    lse_ref[...] = jnp.zeros_like(lse_ref)
    across = lax.broadcasted_iota(jnp.int32, (1, 128), 1)
    for part in range(4):
        owner = ctx if part < 2 else ctx + 1 - 2 * meta_ref[CORE]
        query_pos = across + meta_ref[2 * owner + part % 2]
        scores = dot(kv_ref[:, :HD], qs[part * 128 : part * 128 + 128, :], ((1,), (1,))) * SCALE
        scores = jnp.where(key_pos[...] <= query_pos, scores, NEG)
        peak = jnp.max(scores, axis=0, keepdims=True)
        weights = jnp.exp(scores - peak)
        denominator = jnp.sum(weights, axis=0, keepdims=True)
        probs = (weights * (1.0 / denominator)).astype(BF)
        result = dot(probs, kv_ref[:, HD:], ((0,), (0,))).astype(BF)
        rows = slice(part % 2 * RUN, part % 2 * RUN + RUN)
        (own_ref if part < 2 else other_ref)[rows, :] = result[:RUN, :]
        lse_ref[part : part + 1, :] = peak + jnp.log(denominator)


def embed_body(meta_ref, ids_ref, *refs):
    out_ref = refs[-1]
    rows = ids_ref.shape[0]
    lane = lax.broadcasted_iota(jnp.int32, (rows, 256), 1)
    sums = jnp.zeros((rows, 1024), F32)
    for block in range(8):
        pick = (ids_ref[...] == lane + meta_ref[SHARDS + block] * 256).astype(F32).astype(BF)
        sums += dot(pick, refs[block][...], ((1,), (0,)))
    out_ref[...] = sums.astype(BF)


def head_body(meta_ref, base_ref, embed_ref, target_ref, cot_ref, *refs):
    tables, (unit_ref, dlogits_ref, grad_ref, loss_ref, logits_ref) = refs[:8], refs[8:]
    rows = base_ref.shape[0]
    keep = jnp.where(meta_ref[TP_AT] > 0, 1.0, 0.0)
    depth_in = base_ref[...].astype(F32) + embed_ref[...].astype(F32) * keep
    inverse_rms = lax.rsqrt(jnp.mean(depth_in * depth_in, axis=-1, keepdims=True) + EPS)
    scaled = depth_in * inverse_rms
    unit = scaled.astype(BF)
    unit_ref[...] = unit
    lane = lax.broadcasted_iota(jnp.int32, (rows, 256), 1)
    peak = jnp.full((rows, 1), NEG, F32)
    for block in range(8):
        cols = slice(block * 256, block * 256 + 256)
        logits = dot(unit, tables[block][...], ((1,), (0,)))
        logits_ref[:, cols] = logits
        peak = jnp.maximum(peak, jnp.max(logits, axis=-1, keepdims=True))
    denominator = jnp.zeros((rows, 1), F32)
    chosen = jnp.zeros((rows, 1), F32)
    for block in range(8):
        cols = slice(block * 256, block * 256 + 256)
        logits = logits_ref[:, cols]
        is_target = target_ref[...] == lane + meta_ref[SHARDS + block] * 256
        chosen += jnp.sum(jnp.where(is_target, logits, 0.0), axis=-1, keepdims=True)
        terms = jnp.exp(logits - peak)
        denominator += jnp.sum(terms, axis=-1, keepdims=True)
        logits_ref[:, cols] = terms
    loss_ref[...] = jnp.log(denominator) + peak - chosen
    inverse = 1.0 / denominator
    cot = cot_ref[...]
    unit_grad = jnp.zeros((rows, 1024), F32)
    for block in range(8):
        cols = slice(block * 256, block * 256 + 256)
        start = meta_ref[SHARDS + block] * 256
        hit = jnp.where(target_ref[...] == lane + start, 1.0, 0.0)
        dlogits = (cot * (logits_ref[:, cols] * inverse - hit)).astype(BF)
        dlogits_ref[:, pl.ds(pl.multiple_of(start, 256), 256)] = dlogits
        unit_grad += dot(dlogits, tables[block][...], ((1,), (1,)))
    centre = jnp.mean(unit_grad * scaled, axis=-1, keepdims=True)
    grad_ref[...] = (inverse_rms * (unit_grad - scaled * centre)).astype(BF)


STAT_AT, OUTER_AT, SEND = 192, 224, 352


def send_body(
    meta_ref, summed_ref, fold_ref, attended_ref, lse_ref, lse_come_ref, out_ref, stat, product
):
    first = meta_ref[CORE] == 0
    summed = summed_ref[...]
    attended = attended_ref[...]
    grad = dot(summed, fold_ref[...], ((1,), (0,))).astype(BF)
    outer = dot(summed, attended, ((0,), (0,))).astype(BF)
    for block in range(16):
        out_ref[block, OUTER_AT : OUTER_AT + 64, :] = outer[block * 64 : block * 64 + 64, :HD]
        out_ref[block, OUTER_AT + 64 :, :] = outer[block * 64 : block * 64 + 64, HD:]
    ones = jnp.ones((8, 128), F32)
    for head in range(2):
        cols = slice(head * HD, head * HD + HD)
        stat[...] = jnp.zeros_like(stat)
        product[...] = jnp.zeros_like(product)
        for run in range(2):
            rows = slice(run * RUN, run * RUN + RUN)
            product[:RUN, :] = grad[rows, cols].astype(F32) * attended[rows, cols].astype(F32)
            centre = lax.dot_general(
                ones, product[...], (((1,), (1,)), ((), ())),
                preferred_element_type=F32, precision=lax.Precision.HIGHEST,
            )[:1, :]
            mine = lse_ref[run : run + 1, :]
            come = lse_come_ref[2 + run : 3 + run, :]
            lse = jnp.where(first, mine, come) if head == 0 else jnp.where(first, come, mine)
            for at, value in ((0, lse * (-1.0 / SCALE)), (3, -centre)):
                for term in range(3):
                    part = value.astype(BF).astype(F32)
                    row = run * 16 + at + term
                    stat[row : row + 1, :] = part
                    value = value - part
        packed = stat[...].astype(BF)
        for block in range(head, 16, 2):
            out_ref[block, :STAT_AT, :] = grad[:, cols]
            out_ref[block, STAT_AT:OUTER_AT, :] = packed


def backward_body(
    meta_ref, come_ref, q_far, kv_far, grads, q_ref, kv_ref, qs, ks, vs, gs, dq, dk, dv, sems
):
    q_copy = pltpu.make_async_copy(q_far, q_ref, sems.at[0])
    kv_copy = pltpu.make_async_copy(kv_far, kv_ref, sems.at[1])
    q_copy.start()
    kv_copy.start()
    core = meta_ref[CORE]
    first = core == 0
    total_rows = q_far.shape[0]
    runs = total_rows // RUN
    stat_row = lax.broadcasted_iota(jnp.int32, (16, 128), 0)
    stat_lane = lax.broadcasted_iota(jnp.int32, (16, 128), 1)
    place_lse = jnp.where((stat_row == stat_lane) & (stat_lane < 3), 1.0, 0.0).astype(BF)
    place_centre = jnp.where((stat_row == stat_lane + 3) & (stat_lane < 3), 1.0, 0.0).astype(BF)
    for run in range(runs):
        src = slice(run * RUN, run * RUN + RUN)
        dst = pl.ds(pl.multiple_of(meta_ref[run], 32), RUN)
        half = slice(run % 2 * RUN, run % 2 * RUN + RUN)
        stats = come_ref[run // 2, STAT_AT + run % 2 * 16 : STAT_AT + run % 2 * 16 + 16, :]
        qs[dst, HD:] = dot(stats, place_lse, ((0,), (0,))).astype(BF)[:RUN, :]
        gs[dst, :HD] = come_ref[run // 2, half, :]
        gs[dst, HD:] = dot(stats, place_centre, ((0,), (0,))).astype(BF)[:RUN, :]

    ks[:, HD:] = jnp.ones((total_rows, HD), BF)
    vs[:, HD:] = jnp.ones((total_rows, HD), BF)
    dk[...] = jnp.zeros_like(dk)
    dv[...] = jnp.zeros_like(dv)
    q_copy.wait()
    kv_copy.wait()
    for run in range(runs):
        src = slice(run * RUN, run * RUN + RUN)
        dst = pl.ds(pl.multiple_of(meta_ref[run], 32), RUN)
        qs[dst, :HD] = jnp.where(first, q_ref[src, :HD], q_ref[src, HD:])
        ks[dst, :HD] = kv_ref[src, :HD]
        vs[dst, :HD] = kv_ref[src, HD:]

    @pl.loop(0, total_rows // QB)
    def _(block):
        q_rows = pl.ds(pl.multiple_of(block * QB, QB), QB)
        q = qs[q_rows, :]
        g = gs[q_rows, :]

        def step(chunk, running, masked):
            rows = pl.ds(pl.multiple_of(chunk * KB, KB), KB)
            k = ks[rows, :]
            v = vs[rows, :]
            shifted = dot(k, q, ((1,), (1,)))
            if masked:
                key_at = lax.broadcasted_iota(jnp.int32, (KB, QB), 0) + chunk * KB
                query_at = lax.broadcasted_iota(jnp.int32, (KB, QB), 1) + block * QB
                shifted = jnp.where(key_at <= query_at, shifted, NEG)
            probs = jnp.exp(shifted * SCALE)
            score_grad = (probs * dot(v, g, ((1,), (1,)))).astype(BF)
            dv[rows, :] += dot(probs.astype(BF), g[:, :HD], ((1,), (0,)))
            dk[rows, :] += dot(score_grad, q[:, :HD], ((1,), (0,)))
            return running + dot(score_grad, k[:, :HD], ((0,), (0,)))

        last = block // (KB // QB)
        running = lax.fori_loop(
            0, last, lambda chunk, acc: step(chunk, acc, False), jnp.zeros((QB, HD), F32)
        )
        dq[q_rows, :] = step(last, running, True)

    for run in range(runs):
        src = slice(run * RUN, run * RUN + RUN)
        dst = pl.ds(pl.multiple_of(meta_ref[run], 32), RUN)
        grads[src, :HD] = (dq[dst, :] * SCALE).astype(BF)
        grads[src, HD : 2 * HD] = (dk[dst, :] * SCALE).astype(BF)
        grads[src, 2 * HD :] = dv[dst, :].astype(BF)


def weight_body(meta_ref, grads_ref, *refs):
    normed_refs, (keep_ref, send_ref) = refs[:16], refs[16:]
    core = meta_ref[CORE]
    first = core == 0
    sums = jnp.zeros((512, 3 * HD), F32)
    for hop in range(8):
        from_x = lax.rem(lax.div(meta_ref[CTX_AT], 4) + 4 - hop // 2, 4)
        from_yl = lax.rem(lax.div(meta_ref[CTX_AT], 2) + hop % 2, 2)
        for side in range(2):
            from_core = core if side == 0 else 1 - core
            start = (from_x * 2 + from_yl) * 384 + from_core * 192
            rows = pl.ds(pl.multiple_of(start, 192), 192)
            sums += dot(normed_refs[side * 8 + hop][...], grads_ref[rows, :], ((0,), (0,)))
    keep_ref[...] = jnp.where(first, sums[:256], sums[256:])
    send_ref[...] = jnp.where(first, sums[256:], sums[:256])


def cut_body(meta_ref, normed_ref, *out_refs):
    at_x = lax.div(meta_ref[CTX_AT], 4)
    at_yl = lax.rem(lax.div(meta_ref[CTX_AT], 2), 2)
    for hop, out_ref in enumerate(out_refs):
        chip = lax.rem(at_x + hop // 2, 4) * 2 + lax.rem(at_yl + hop % 2, 2)
        out_ref[...] = normed_ref[:, pl.ds(pl.multiple_of(chip * 512, 512), 512)]


def grad_out_body(meta_ref, outer_ref, depth_ref, out_ref):
    out_ref[...] = dot(outer_ref[...].astype(BF), depth_ref[...], ((0,), (1,)))


def join_body(meta_ref, keep_ref, come_ref, *out_refs):
    first = meta_ref[CORE] == 0
    for at, out_ref in enumerate(out_refs):
        cols = slice(at * HD, at * HD + HD)
        keep, come = keep_ref[:, cols], come_ref[:, cols]
        out_ref[:, :HD] = jnp.where(first, keep, come)
        out_ref[:, HD:] = jnp.where(first, come, keep)


def sum_piece_tp(part):
    rows, cols = part.shape
    return total(exchange(part.reshape(8, rows // 8, cols), TP)).astype(BF)


def gather_wide(block, axes):
    return lax.all_gather(block, axes, axis=0, tiled=True)


def per_device(
    frames,
    frame_pos,
    codes,
    loss_grad,
    w_query,
    w_key,
    w_value,
    w_out,
    w_depth_in,
    code_embed,
    code_head,
):
    rows = frames.shape[0]
    frame_total = frame_pos.shape[0]
    x, yl, core = lax.axis_index("x"), lax.axis_index("yl"), lax.axis_index("core")
    yh, z = lax.axis_index("yh"), lax.axis_index("z")
    ctx = lax.axis_index(CTX)
    tp = lax.axis_index(TP)
    first = core == 0

    shards, head_blocks, embed_blocks = [], [], []
    for block in range(4):
        far, near = block // 2, block % 2 * 2
        level = (yh + far) % 2 * 4 + (z + near + core) % 4
        head_blocks.append(lax.dynamic_index_in_dim(code_head, level, 0, False))
        embed_blocks.append(
            lax.dynamic_index_in_dim(code_embed, jnp.maximum(level - 1, 0), 0, False)
        )
    frames, *blocks = lax.optimization_barrier((frames, *head_blocks, *embed_blocks))
    for side in range(2):
        for block in range(4):
            far, near = block // 2, block % 2 * 2
            turn = near + (core if side == 0 else 1 - core)
            shards.append((yh + far) % 2 * 4 + (z + 4 - turn) % 4)
    own_blocks = []
    for at, operand in enumerate(blocks):
        far, near = at % 4 // 2, at % 2 * 2
        moves = []
        for a in range(2):
            for k in range(2):
                for h in range(2):
                    for d in range(4):
                        to = ((a + far) % 2, k, (h + far) % 2, (d + near + k) % 4)
                        moves.append(
                            (((a * 2 + k) * 2 + h) * 4 + d, ((to[0] * 2 + to[1]) * 2 + to[2]) * 4 + to[3])
                        )
        own_blocks.append(lax.ppermute(operand, ("yl", "core", "yh", "z"), moves))
    other_blocks = [swap_core(block) for block in own_blocks]
    head_tables = own_blocks[:4] + other_blocks[:4]
    embed_tables = own_blocks[4:] + other_blocks[4:]
    meta = jnp.concatenate(
        [frame_pos[::RUN], jnp.stack([core, ctx, tp] + shards).astype(jnp.int32)]
    )

    depth_cols = lax.dynamic_slice_in_dim(w_depth_in, ctx * 64, 64, 1).T
    depth_cols = spread(depth_cols, TP, 8)
    fold_cols = lax.dot_general(
        depth_cols, w_out.reshape(256, 8, 512), (((0, 2), (1, 2)), ((), ())),
        preferred_element_type=F32,
    ).astype(BF)

    normed = rms_rows(frames.astype(F32)).astype(BF)
    key = dot(normed, w_key, ((1,), (0,))).astype(BF)
    value = dot(normed, w_value, ((1,), (0,))).astype(BF)
    query = dot(normed, w_query, ((1,), (0,))).astype(BF)

    key_value = jnp.stack(
        [jnp.concatenate([key[:, :HD], value[:, :HD]], 1),
         jnp.concatenate([key[:, HD:], value[:, HD:]], 1)]
    )
    key_value = exchange(
        after(
            jnp.broadcast_to(key_value[None], (8, 2, rows, 2 * HD)).reshape(16, rows, 2 * HD),
            depth_cols,
        ),
        CTX,
    ).reshape(frame_total, 2 * HD)
    query_all = lax.all_gather(after(query, key_value), CTX, axis=0, tiled=True)
    query_come = swap_core(
        after(jnp.where(first, query[:, HD:], query[:, :HD]), *own_blocks[4:])
    )

    own_part, other_part, lse = kernel_call(
        forward_body,
        (
            jax.ShapeDtypeStruct((rows, HD), BF),
            jax.ShapeDtypeStruct((rows, HD), BF),
            jax.ShapeDtypeStruct((8, 128), F32),
        ),
        [pltpu.VMEM((512, HD), BF), pltpu.VMEM((frame_total, 128), jnp.int32)],
        2_000_000_000, 4_000_000, 4,
    )(meta, query, query_come, key_value)
    come_part = swap_core(other_part)
    lse_come = swap_core(lse)
    attended = jnp.where(
        first,
        jnp.concatenate([own_part, come_part], 1),
        jnp.concatenate([come_part, own_part], 1),
    )
    fold = spread(after(fold_cols, key_value), CTX, 16).reshape(1024, 2 * HD)

    base = sum_piece_tp(dot(attended, fold, ((1,), (1,))).astype(BF))
    base = spread(base, TP, 8).reshape(rows, 1024)

    level_ids = jnp.arange(8, dtype=jnp.int32)[None, :]
    target = jnp.sum(jnp.where(level_ids == tp, codes, 0), axis=1, keepdims=True)
    cotangent = jnp.sum(jnp.where(level_ids == tp, loss_grad, 0.0), axis=1, keepdims=True)
    previous = jnp.sum(jnp.where(level_ids + 1 == tp, codes, 0), axis=1, keepdims=True)
    embedded = kernel_call(
        embed_body, jax.ShapeDtypeStruct((rows, 1024), BF), [], 800_000_000, 5_000_000, 10
    )(meta, previous, *embed_tables)
    unit, dlogits, depth_grad, loss = kernel_call(
        head_body,
        (
            jax.ShapeDtypeStruct((rows, 1024), BF),
            jax.ShapeDtypeStruct((rows, 2048), BF),
            jax.ShapeDtypeStruct((rows, 1024), BF),
            jax.ShapeDtypeStruct((rows, 1), F32),
        ),
        [pltpu.VMEM((rows, 2048), F32)],
        2_000_000_000, 6_000_000, 13,
    )(meta, base, embedded, target, cotangent, *head_tables)

    normed_own = []
    cuts = kernel_call(
        cut_body, (jax.ShapeDtypeStruct((rows, 512), BF),) * 8, [], 0, 3_000_000, 2
    )(meta, after(normed, depth_grad))
    for hop, piece in enumerate(cuts):
        moves = [
            (a * 2 + b, (a + hop // 2) % 4 * 2 + (b + hop % 2) % 2)
            for a in range(4) for b in range(2)
        ]
        normed_own.append(lax.ppermute(piece, CHIPS, moves) if hop else piece)
    normed_other = [swap_core(piece) for piece in normed_own]

    summed = sum_piece_tp(after(depth_grad, query_all))
    summed = spread(after(summed, *normed_own), TP, 8).reshape(rows, 1024)

    send = kernel_call(
        send_body,
        jax.ShapeDtypeStruct((16, SEND, 128), BF),
        [pltpu.VMEM((32, 128), F32), pltpu.VMEM((128, 128), F32)],
        400_000_000, 3_000_000, 6,
    )(meta, after(summed, *normed_other), fold, attended, lse, lse_come)
    come = exchange(send, CTX)

    unit, dlogits = after(unit, send), after(dlogits, send)
    unit_blocks = unit.reshape(rows, 8, 2, 64)
    unit_keep = lax.dynamic_index_in_dim(unit_blocks, core, 2, False).reshape(rows, 512)
    unit_send = lax.dynamic_index_in_dim(unit_blocks, 1 - core, 2, False).reshape(rows, 512)
    head_come = swap_core(dot(unit_send, dlogits, ((0,), (0,))).astype(BF))
    head_part = (dot(unit_keep, dlogits, ((0,), (0,))) + head_come.astype(F32)).astype(BF)
    head_parts = exchange(after(head_part, come).reshape(8, 64, 2048), CHIPS)

    outer_own = total(come[:, OUTER_AT:])
    outer_own = jnp.concatenate([outer_own[:64], outer_own[64:]], axis=1)
    outer = gather_wide(outer_own, CTX)

    depth_half = lax.dynamic_slice_in_dim(w_depth_in, core * 256, 256, 0)
    moves = [
        (c * 8 + t, (2 * t + c % 2) * 8 + c // 2) for c in range(16) for t in range(8)
    ]
    depth_rows = lax.ppermute(after(depth_half, base), ALL, moves)

    grads = kernel_call(
        backward_body,
        jax.ShapeDtypeStruct((frame_total, 3 * HD), BF),
        [pltpu.VMEM((frame_total, 2 * HD), BF)] * 6
        + [pltpu.VMEM((frame_total, HD), F32)] * 3
        + [pltpu.SemaphoreType.DMA((2,))],
        25_000_000_000, 8_000_000, 4, 2,
    )(meta, after(come, outer_own, head_part), query_all, key_value)
    head_sum = total(after(head_parts, grads)).astype(BF)
    weights_keep, weights_send = kernel_call(
        weight_body,
        (jax.ShapeDtypeStruct((256, 3 * HD), F32), jax.ShapeDtypeStruct((256, 3 * HD), F32)),
        [], 1_200_000_000, 6_000_000, 18,
    )(meta, after(grads, depth_rows), *normed_own, *normed_other)
    weights_come = swap_core(weights_send)
    grad_query, grad_key, grad_value = kernel_call(
        join_body, (jax.ShapeDtypeStruct((256, 2 * HD), F32),) * 3, [], 0, 2_000_000, 3
    )(meta, weights_keep, weights_come)

    grad_out = kernel_call(
        grad_out_body, jax.ShapeDtypeStruct((2 * HD, 256), F32), [], 100_000_000, 2_000_000, 3
    )(meta, outer, depth_rows)
    depth_part = dot(outer_own.astype(BF), w_out, ((1,), (0,))).astype(BF)
    loss_row = jnp.pad(thirds(loss[:, 0]).reshape(1, 576), ((0, 15), (0, 192)))
    tail = jnp.concatenate(
        [
            jnp.concatenate(
                [depth_part.reshape(64, 8, 512), head_sum.reshape(64, 8, 256)], axis=2
            ).transpose(1, 0, 2),
            jnp.broadcast_to(loss_row[None], (8, 16, 768)),
        ],
        axis=1,
    )
    tail = exchange(tail, TP)
    grad_depth_in = total(tail[:, :64, :512]).T
    grad_head = tail[:, :64, 512:].astype(F32)
    token_loss = total(tail[:, 64, :576].reshape(8, 3, rows).transpose(1, 2, 0))
    return (token_loss, grad_query, grad_key, grad_value, grad_out, grad_depth_in, grad_head)


def solution(mesh):
    fine = Mesh(mesh.devices.reshape(4, 2, 2, 2, 4), ALL)
    in_specs = (
        P(CTX, None),
        P(),
        P(CTX, None),
        P(CTX, None),
        P(None, TP),
        P(None, TP),
        P(None, TP),
        P(TP, None),
        P(TP, None),
        P(None, TP, None),
        P(None, None, TP),
    )
    out_specs = (
        P(CTX, None),
        P(CTX, TP),
        P(CTX, TP),
        P(CTX, TP),
        P(TP, CTX),
        P(TP, CTX),
        P(None, CTX, TP),
    )
    return jax.shard_map(
        per_device, mesh=fine, in_specs=in_specs, out_specs=out_specs, check_vma=False
    )
```

```python
import math

import jax
import jax.numpy as jnp
from jax import lax
from jax.experimental import pallas as pl
from jax.experimental.pallas import tpu as pltpu
from jax.sharding import Mesh
from jax.sharding import PartitionSpec as P

HD = 128
EPS = 1e-05
NEG = -1e30
SCALE = 1.0 / math.sqrt(HD)
CTX = ("x", "yl", "core")
CHIPS = ("x", "yl")
TP = ("yh", "z")
ALL = CTX + TP
BF = jnp.bfloat16
F32 = jnp.float32
RUN = 96
QB = 256
KB = 512


def rms_rows(values):
    return values * lax.rsqrt(jnp.mean(values * values, axis=-1, keepdims=True) + EPS)


def dot(left, right, dims):
    return lax.dot_general(left, right, (dims, ((), ())), preferred_element_type=F32)


def exchange(parts, axes):
    return lax.all_to_all(parts, axes, 0, 0, tiled=True)


def spread(block, axes, count):
    return exchange(jnp.broadcast_to(block[None], (count,) + block.shape), axes)


def total(parts):
    return jnp.sum(parts.astype(F32), axis=0)


def swap_core(block):
    return lax.ppermute(block, "core", [(0, 1), (1, 0)])


def after(value, *earlier):
    return lax.optimization_barrier((value,) + earlier)[0]


def thirds(values):
    high = lax.reduce_precision(values, 8, 7)
    rest = values - high
    middle = lax.reduce_precision(rest, 8, 7)
    return jnp.stack([high, middle, rest - middle]).astype(BF)


def kernel_call(body, out_shape, scratch, flops, byte_count, count, far_in=0):
    near, far = pl.BlockSpec(memory_space=pltpu.VMEM), pl.BlockSpec(memory_space=pl.ANY)
    return pl.pallas_call(
        body,
        out_shape=out_shape,
        in_specs=[pl.BlockSpec(memory_space=pltpu.SMEM)]
        + [near] * (count - 1 - far_in)
        + [far] * far_in,
        out_specs=jax.tree.map(lambda _: near, out_shape),
        scratch_shapes=scratch,
        compiler_params=pltpu.CompilerParams(vmem_limit_bytes=48 << 20),
        cost_estimate=pl.CostEstimate(
            flops=flops, bytes_accessed=byte_count, transcendentals=0
        ),
    )


CORE, CTX_AT, TP_AT, SHARDS, LEVELS = 32, 33, 34, 35, 43


def forward_body(
    meta_ref, q_ref, q_come_ref, kv_ref, own_ref, other_ref, lse_ref, qs, key_pos
):
    first = meta_ref[CORE] == 0
    ctx = meta_ref[CTX_AT]
    qs[...] = jnp.zeros_like(qs)
    for run in range(2):
        rows = slice(run * RUN, run * RUN + RUN)
        qs[run * 128 : run * 128 + RUN, :] = jnp.where(
            first, q_ref[rows, :HD], q_ref[rows, HD:]
        )
        qs[256 + run * 128 : 256 + run * 128 + RUN, :] = q_come_ref[rows, :]
    down = lax.broadcasted_iota(jnp.int32, (RUN, 128), 0)
    for run in range(key_pos.shape[0] // RUN):
        key_pos[run * RUN : run * RUN + RUN, :] = down + meta_ref[run]
    lse_ref[...] = jnp.zeros_like(lse_ref)
    across = lax.broadcasted_iota(jnp.int32, (1, 128), 1)
    for part in range(4):
        owner = ctx if part < 2 else ctx + 1 - 2 * meta_ref[CORE]
        query_pos = across + meta_ref[2 * owner + part % 2]
        scores = dot(kv_ref[:, :HD], qs[part * 128 : part * 128 + 128, :], ((1,), (1,))) * SCALE
        scores = jnp.where(key_pos[...] <= query_pos, scores, NEG)
        peak = jnp.max(scores, axis=0, keepdims=True)
        weights = jnp.exp(scores - peak)
        denominator = jnp.sum(weights, axis=0, keepdims=True)
        probs = (weights * (1.0 / denominator)).astype(BF)
        result = dot(probs, kv_ref[:, HD:], ((0,), (0,))).astype(BF)
        rows = slice(part % 2 * RUN, part % 2 * RUN + RUN)
        (own_ref if part < 2 else other_ref)[rows, :] = result[:RUN, :]
        lse_ref[part : part + 1, :] = peak + jnp.log(denominator)


def embed_body(meta_ref, ids_ref, *refs):
    out_ref = refs[-1]
    rows = ids_ref.shape[0]
    lane = lax.broadcasted_iota(jnp.int32, (rows, 256), 1)
    sums = jnp.zeros((rows, 1024), F32)
    for block in range(8):
        pick = (ids_ref[...] == lane + meta_ref[SHARDS + block] * 256).astype(F32).astype(BF)
        sums += dot(pick, refs[block][...], ((1,), (0,)))
    out_ref[...] = sums.astype(BF)


def head_body(meta_ref, base_ref, embed_ref, target_ref, cot_ref, *refs):
    tables, (unit_ref, dlogits_ref, grad_ref, loss_ref, logits_ref) = refs[:8], refs[8:]
    rows = base_ref.shape[0]
    keep = jnp.where(meta_ref[TP_AT] > 0, 1.0, 0.0)
    depth_in = base_ref[...].astype(F32) + embed_ref[...].astype(F32) * keep
    inverse_rms = lax.rsqrt(jnp.mean(depth_in * depth_in, axis=-1, keepdims=True) + EPS)
    scaled = depth_in * inverse_rms
    unit = scaled.astype(BF)
    unit_ref[...] = unit
    lane = lax.broadcasted_iota(jnp.int32, (rows, 256), 1)
    peak = jnp.full((rows, 1), NEG, F32)
    for block in range(8):
        cols = slice(block * 256, block * 256 + 256)
        logits = dot(unit, tables[block][...], ((1,), (0,)))
        logits_ref[:, cols] = logits
        peak = jnp.maximum(peak, jnp.max(logits, axis=-1, keepdims=True))
    denominator = jnp.zeros((rows, 1), F32)
    chosen = jnp.zeros((rows, 1), F32)
    for block in range(8):
        cols = slice(block * 256, block * 256 + 256)
        logits = logits_ref[:, cols]
        is_target = target_ref[...] == lane + meta_ref[SHARDS + block] * 256
        chosen += jnp.sum(jnp.where(is_target, logits, 0.0), axis=-1, keepdims=True)
        terms = jnp.exp(logits - peak)
        denominator += jnp.sum(terms, axis=-1, keepdims=True)
        logits_ref[:, cols] = terms
    loss_ref[...] = jnp.log(denominator) + peak - chosen
    inverse = 1.0 / denominator
    cot = cot_ref[...]
    unit_grad = jnp.zeros((rows, 1024), F32)
    for block in range(8):
        cols = slice(block * 256, block * 256 + 256)
        start = meta_ref[SHARDS + block] * 256
        hit = jnp.where(target_ref[...] == lane + start, 1.0, 0.0)
        dlogits = (cot * (logits_ref[:, cols] * inverse - hit)).astype(BF)
        dlogits_ref[:, pl.ds(pl.multiple_of(start, 256), 256)] = dlogits
        unit_grad += dot(dlogits, tables[block][...], ((1,), (1,)))
    centre = jnp.mean(unit_grad * scaled, axis=-1, keepdims=True)
    grad_ref[...] = (inverse_rms * (unit_grad - scaled * centre)).astype(BF)


STAT_AT, OUTER_AT, SEND = 192, 224, 352


def send_body(
    meta_ref, summed_ref, fold_ref, attended_ref, lse_ref, lse_come_ref, out_ref, stat, product
):
    first = meta_ref[CORE] == 0
    summed = summed_ref[...]
    attended = attended_ref[...]
    grad = dot(summed, fold_ref[...], ((1,), (0,))).astype(BF)
    outer = dot(summed, attended, ((0,), (0,))).astype(BF)
    for block in range(16):
        out_ref[block, OUTER_AT : OUTER_AT + 64, :] = outer[block * 64 : block * 64 + 64, :HD]
        out_ref[block, OUTER_AT + 64 :, :] = outer[block * 64 : block * 64 + 64, HD:]
    ones = jnp.ones((8, 128), F32)
    for head in range(2):
        cols = slice(head * HD, head * HD + HD)
        stat[...] = jnp.zeros_like(stat)
        product[...] = jnp.zeros_like(product)
        for run in range(2):
            rows = slice(run * RUN, run * RUN + RUN)
            product[:RUN, :] = grad[rows, cols].astype(F32) * attended[rows, cols].astype(F32)
            centre = lax.dot_general(
                ones, product[...], (((1,), (1,)), ((), ())),
                preferred_element_type=F32, precision=lax.Precision.HIGHEST,
            )[:1, :]
            mine = lse_ref[run : run + 1, :]
            come = lse_come_ref[2 + run : 3 + run, :]
            lse = jnp.where(first, mine, come) if head == 0 else jnp.where(first, come, mine)
            for at, value in ((0, lse * (-1.0 / SCALE)), (3, -centre)):
                for term in range(3):
                    part = value.astype(BF).astype(F32)
                    row = run * 16 + at + term
                    stat[row : row + 1, :] = part
                    value = value - part
        packed = stat[...].astype(BF)
        for block in range(head, 16, 2):
            out_ref[block, :STAT_AT, :] = grad[:, cols]
            out_ref[block, STAT_AT:OUTER_AT, :] = packed


def backward_body(
    meta_ref, come_ref, q_far, kv_far, grads, q_ref, kv_ref, qs, ks, vs, gs, dq, dk, dv, sems
):
    q_copy = pltpu.make_async_copy(q_far, q_ref, sems.at[0])
    kv_copy = pltpu.make_async_copy(kv_far, kv_ref, sems.at[1])
    q_copy.start()
    kv_copy.start()
    core = meta_ref[CORE]
    first = core == 0
    total_rows = q_far.shape[0]
    runs = total_rows // RUN
    stat_row = lax.broadcasted_iota(jnp.int32, (16, 128), 0)
    stat_lane = lax.broadcasted_iota(jnp.int32, (16, 128), 1)
    place_lse = jnp.where((stat_row == stat_lane) & (stat_lane < 3), 1.0, 0.0).astype(BF)
    place_centre = jnp.where((stat_row == stat_lane + 3) & (stat_lane < 3), 1.0, 0.0).astype(BF)
    for run in range(runs):
        src = slice(run * RUN, run * RUN + RUN)
        dst = pl.ds(pl.multiple_of(meta_ref[run], 32), RUN)
        half = slice(run % 2 * RUN, run % 2 * RUN + RUN)
        stats = come_ref[run // 2, STAT_AT + run % 2 * 16 : STAT_AT + run % 2 * 16 + 16, :]
        qs[dst, HD:] = dot(stats, place_lse, ((0,), (0,))).astype(BF)[:RUN, :]
        gs[dst, :HD] = come_ref[run // 2, half, :]
        gs[dst, HD:] = dot(stats, place_centre, ((0,), (0,))).astype(BF)[:RUN, :]

    ks[:, HD:] = jnp.ones((total_rows, HD), BF)
    vs[:, HD:] = jnp.ones((total_rows, HD), BF)
    dk[...] = jnp.zeros_like(dk)
    dv[...] = jnp.zeros_like(dv)
    q_copy.wait()
    kv_copy.wait()
    for run in range(runs):
        src = slice(run * RUN, run * RUN + RUN)
        dst = pl.ds(pl.multiple_of(meta_ref[run], 32), RUN)
        qs[dst, :HD] = jnp.where(first, q_ref[src, :HD], q_ref[src, HD:])
        ks[dst, :HD] = kv_ref[src, :HD]
        vs[dst, :HD] = kv_ref[src, HD:]

    @pl.loop(0, total_rows // QB)
    def _(block):
        q_rows = pl.ds(pl.multiple_of(block * QB, QB), QB)
        q = qs[q_rows, :]
        g = gs[q_rows, :]

        def step(chunk, running, masked):
            rows = pl.ds(pl.multiple_of(chunk * KB, KB), KB)
            k = ks[rows, :]
            v = vs[rows, :]
            shifted = dot(k, q, ((1,), (1,)))
            if masked:
                key_at = lax.broadcasted_iota(jnp.int32, (KB, QB), 0) + chunk * KB
                query_at = lax.broadcasted_iota(jnp.int32, (KB, QB), 1) + block * QB
                shifted = jnp.where(key_at <= query_at, shifted, NEG)
            probs = jnp.exp(shifted * SCALE)
            score_grad = (probs * dot(v, g, ((1,), (1,)))).astype(BF)
            dv[rows, :] += dot(probs.astype(BF), g[:, :HD], ((1,), (0,)))
            dk[rows, :] += dot(score_grad, q[:, :HD], ((1,), (0,)))
            return running + dot(score_grad, k[:, :HD], ((0,), (0,)))

        last = block // (KB // QB)
        running = lax.fori_loop(
            0, last, lambda chunk, acc: step(chunk, acc, False), jnp.zeros((QB, HD), F32)
        )
        dq[q_rows, :] = step(last, running, True)

    for run in range(runs):
        src = slice(run * RUN, run * RUN + RUN)
        dst = pl.ds(pl.multiple_of(meta_ref[run], 32), RUN)
        grads[src, :HD] = (dq[dst, :] * SCALE).astype(BF)
        grads[src, HD : 2 * HD] = (dk[dst, :] * SCALE).astype(BF)
        grads[src, 2 * HD :] = dv[dst, :].astype(BF)


def weight_body(meta_ref, grads_ref, *refs):
    normed_refs, (keep_ref, send_ref) = refs[:16], refs[16:]
    core = meta_ref[CORE]
    first = core == 0
    sums = jnp.zeros((512, 3 * HD), F32)
    for hop in range(8):
        from_x = lax.rem(lax.div(meta_ref[CTX_AT], 4) + 4 - hop // 2, 4)
        from_yl = lax.rem(lax.div(meta_ref[CTX_AT], 2) + hop % 2, 2)
        for side in range(2):
            from_core = core if side == 0 else 1 - core
            start = (from_x * 2 + from_yl) * 384 + from_core * 192
            rows = pl.ds(pl.multiple_of(start, 192), 192)
            sums += dot(normed_refs[side * 8 + hop][...], grads_ref[rows, :], ((0,), (0,)))
    keep_ref[...] = jnp.where(first, sums[:256], sums[256:])
    send_ref[...] = jnp.where(first, sums[256:], sums[:256])


def cut_body(meta_ref, normed_ref, *out_refs):
    at_x = lax.div(meta_ref[CTX_AT], 4)
    at_yl = lax.rem(lax.div(meta_ref[CTX_AT], 2), 2)
    for hop, out_ref in enumerate(out_refs):
        chip = lax.rem(at_x + hop // 2, 4) * 2 + lax.rem(at_yl + hop % 2, 2)
        out_ref[...] = normed_ref[:, pl.ds(pl.multiple_of(chip * 512, 512), 512)]


def grad_out_body(meta_ref, outer_ref, depth_ref, out_ref):
    out_ref[...] = dot(outer_ref[...].astype(BF), depth_ref[...], ((0,), (1,)))


def join_body(meta_ref, keep_ref, come_ref, *out_refs):
    first = meta_ref[CORE] == 0
    for at, out_ref in enumerate(out_refs):
        cols = slice(at * HD, at * HD + HD)
        keep, come = keep_ref[:, cols], come_ref[:, cols]
        out_ref[:, :HD] = jnp.where(first, keep, come)
        out_ref[:, HD:] = jnp.where(first, come, keep)


def sum_piece_tp(part):
    rows, cols = part.shape
    return total(exchange(part.reshape(8, rows // 8, cols), TP)).astype(BF)


def gather_wide(block, axes):
    return lax.all_gather(block, axes, axis=0, tiled=True)


def per_device(
    frames,
    frame_pos,
    codes,
    loss_grad,
    w_query,
    w_key,
    w_value,
    w_out,
    w_depth_in,
    code_embed,
    code_head,
):
    rows = frames.shape[0]
    frame_total = frame_pos.shape[0]
    x, yl, core = lax.axis_index("x"), lax.axis_index("yl"), lax.axis_index("core")
    yh, z = lax.axis_index("yh"), lax.axis_index("z")
    ctx = lax.axis_index(CTX)
    tp = lax.axis_index(TP)
    first = core == 0

    shards, head_blocks, embed_blocks = [], [], []
    for block in range(4):
        far, near = block // 2, block % 2 * 2
        level = (yh + far) % 2 * 4 + (z + near + core) % 4
        head_blocks.append(lax.dynamic_index_in_dim(code_head, level, 0, False))
        embed_blocks.append(
            lax.dynamic_index_in_dim(code_embed, jnp.maximum(level - 1, 0), 0, False)
        )
    frames, *blocks = lax.optimization_barrier((frames, *head_blocks, *embed_blocks))
    for side in range(2):
        for block in range(4):
            far, near = block // 2, block % 2 * 2
            turn = near + (core if side == 0 else 1 - core)
            shards.append((yh + far) % 2 * 4 + (z + 4 - turn) % 4)
    own_blocks = []
    for at, operand in enumerate(blocks):
        far, near = at % 4 // 2, at % 2 * 2
        moves = []
        for a in range(2):
            for k in range(2):
                for h in range(2):
                    for d in range(4):
                        to = ((a + far) % 2, k, (h + far) % 2, (d + near + k) % 4)
                        moves.append(
                            (((a * 2 + k) * 2 + h) * 4 + d, ((to[0] * 2 + to[1]) * 2 + to[2]) * 4 + to[3])
                        )
        own_blocks.append(lax.ppermute(operand, ("yl", "core", "yh", "z"), moves))
    other_blocks = [swap_core(block) for block in own_blocks]
    head_tables = own_blocks[:4] + other_blocks[:4]
    embed_tables = own_blocks[4:] + other_blocks[4:]
    meta = jnp.concatenate(
        [frame_pos[::RUN], jnp.stack([core, ctx, tp] + shards).astype(jnp.int32)]
    )

    depth_cols = lax.dynamic_slice_in_dim(w_depth_in, ctx * 64, 64, 1).T
    depth_cols = spread(depth_cols, TP, 8)
    fold_cols = lax.dot_general(
        depth_cols, w_out.reshape(256, 8, 512), (((0, 2), (1, 2)), ((), ())),
        preferred_element_type=F32,
    ).astype(BF)

    normed = rms_rows(frames.astype(F32)).astype(BF)
    key = dot(normed, w_key, ((1,), (0,))).astype(BF)
    value = dot(normed, w_value, ((1,), (0,))).astype(BF)
    query = dot(normed, w_query, ((1,), (0,))).astype(BF)

    key_value = jnp.stack(
        [jnp.concatenate([key[:, :HD], value[:, :HD]], 1),
         jnp.concatenate([key[:, HD:], value[:, HD:]], 1)]
    )
    key_value = exchange(
        after(
            jnp.broadcast_to(key_value[None], (8, 2, rows, 2 * HD)).reshape(16, rows, 2 * HD),
            depth_cols,
        ),
        CTX,
    ).reshape(frame_total, 2 * HD)
    query_all = lax.all_gather(after(query, key_value), CTX, axis=0, tiled=True)
    query_come = swap_core(jnp.where(first, query[:, HD:], query[:, :HD]))

    own_part, other_part, lse = kernel_call(
        forward_body,
        (
            jax.ShapeDtypeStruct((rows, HD), BF),
            jax.ShapeDtypeStruct((rows, HD), BF),
            jax.ShapeDtypeStruct((8, 128), F32),
        ),
        [pltpu.VMEM((512, HD), BF), pltpu.VMEM((frame_total, 128), jnp.int32)],
        2_000_000_000, 4_000_000, 4,
    )(meta, query, query_come, key_value)
    come_part = swap_core(other_part)
    lse_come = swap_core(lse)
    attended = jnp.where(
        first,
        jnp.concatenate([own_part, come_part], 1),
        jnp.concatenate([come_part, own_part], 1),
    )
    fold = spread(after(fold_cols, key_value), CTX, 16).reshape(1024, 2 * HD)

    base = sum_piece_tp(dot(attended, fold, ((1,), (1,))).astype(BF))
    base = spread(base, TP, 8).reshape(rows, 1024)

    level_ids = jnp.arange(8, dtype=jnp.int32)[None, :]
    target = jnp.sum(jnp.where(level_ids == tp, codes, 0), axis=1, keepdims=True)
    cotangent = jnp.sum(jnp.where(level_ids == tp, loss_grad, 0.0), axis=1, keepdims=True)
    previous = jnp.sum(jnp.where(level_ids + 1 == tp, codes, 0), axis=1, keepdims=True)
    embedded = kernel_call(
        embed_body, jax.ShapeDtypeStruct((rows, 1024), BF), [], 800_000_000, 5_000_000, 10
    )(meta, previous, *embed_tables)
    unit, dlogits, depth_grad, loss = kernel_call(
        head_body,
        (
            jax.ShapeDtypeStruct((rows, 1024), BF),
            jax.ShapeDtypeStruct((rows, 2048), BF),
            jax.ShapeDtypeStruct((rows, 1024), BF),
            jax.ShapeDtypeStruct((rows, 1), F32),
        ),
        [pltpu.VMEM((rows, 2048), F32)],
        2_000_000_000, 6_000_000, 13,
    )(meta, base, embedded, target, cotangent, *head_tables)

    normed_own = []
    cuts = kernel_call(
        cut_body, (jax.ShapeDtypeStruct((rows, 512), BF),) * 8, [], 0, 3_000_000, 2
    )(meta, after(normed, depth_grad))
    for hop, piece in enumerate(cuts):
        moves = [
            (a * 2 + b, (a + hop // 2) % 4 * 2 + (b + hop % 2) % 2)
            for a in range(4) for b in range(2)
        ]
        normed_own.append(lax.ppermute(piece, CHIPS, moves) if hop else piece)

    summed = sum_piece_tp(after(depth_grad, query_all))
    summed = spread(after(summed, *normed_own[:4]), TP, 8).reshape(rows, 1024)

    send = kernel_call(
        send_body,
        jax.ShapeDtypeStruct((16, SEND, 128), BF),
        [pltpu.VMEM((32, 128), F32), pltpu.VMEM((128, 128), F32)],
        400_000_000, 3_000_000, 6,
    )(meta, after(summed, *normed_own[4:]), fold, attended, lse, lse_come)
    come = exchange(send, CTX)

    unit, dlogits = after(unit, send), after(dlogits, send)
    unit_blocks = unit.reshape(rows, 8, 2, 64)
    unit_keep = lax.dynamic_index_in_dim(unit_blocks, core, 2, False).reshape(rows, 512)
    unit_send = lax.dynamic_index_in_dim(unit_blocks, 1 - core, 2, False).reshape(rows, 512)
    head_come = swap_core(dot(unit_send, dlogits, ((0,), (0,))).astype(BF))
    head_part = (dot(unit_keep, dlogits, ((0,), (0,))) + head_come.astype(F32)).astype(BF)
    head_parts = exchange(after(head_part, come).reshape(8, 64, 2048), CHIPS)

    outer_own = total(come[:, OUTER_AT:])
    outer_own = jnp.concatenate([outer_own[:64], outer_own[64:]], axis=1)
    outer = gather_wide(outer_own, CTX)

    depth_half = lax.dynamic_slice_in_dim(w_depth_in, core * 256, 256, 0)
    moves = [
        (c * 8 + t, (2 * t + c % 2) * 8 + c // 2) for c in range(16) for t in range(8)
    ]
    depth_rows = lax.ppermute(after(depth_half, come), ALL, moves)

    grads = kernel_call(
        backward_body,
        jax.ShapeDtypeStruct((frame_total, 3 * HD), BF),
        [pltpu.VMEM((frame_total, 2 * HD), BF)] * 6
        + [pltpu.VMEM((frame_total, HD), F32)] * 3
        + [pltpu.SemaphoreType.DMA((2,))],
        25_000_000_000, 8_000_000, 4, 2,
    )(meta, after(come, outer_own, head_part), query_all, key_value)
    head_sum = total(after(head_parts, grads)).astype(BF)
    normed_other = [swap_core(piece) for piece in normed_own]
    weights_keep, weights_send = kernel_call(
        weight_body,
        (jax.ShapeDtypeStruct((256, 3 * HD), F32), jax.ShapeDtypeStruct((256, 3 * HD), F32)),
        [], 1_200_000_000, 6_000_000, 18,
    )(meta, after(grads, depth_rows), *normed_own, *normed_other)
    weights_come = swap_core(weights_send)
    grad_query, grad_key, grad_value = kernel_call(
        join_body, (jax.ShapeDtypeStruct((256, 2 * HD), F32),) * 3, [], 0, 2_000_000, 3
    )(meta, weights_keep, weights_come)

    grad_out = kernel_call(
        grad_out_body, jax.ShapeDtypeStruct((2 * HD, 256), F32), [], 100_000_000, 2_000_000, 3
    )(meta, outer, depth_rows)
    depth_part = dot(outer_own.astype(BF), w_out, ((1,), (0,))).astype(BF)
    loss_row = jnp.pad(thirds(loss[:, 0]).reshape(1, 576), ((0, 15), (0, 192)))
    tail = jnp.concatenate(
        [
            jnp.concatenate(
                [depth_part.reshape(64, 8, 512), head_sum.reshape(64, 8, 256)], axis=2
            ).transpose(1, 0, 2),
            jnp.broadcast_to(loss_row[None], (8, 16, 768)),
        ],
        axis=1,
    )
    tail = exchange(tail, TP)
    grad_depth_in = total(tail[:, :64, :512]).T
    grad_head = tail[:, :64, 512:].astype(F32)
    token_loss = total(tail[:, 64, :576].reshape(8, 3, rows).transpose(1, 2, 0))
    return (token_loss, grad_query, grad_key, grad_value, grad_out, grad_depth_in, grad_head)


def solution(mesh):
    fine = Mesh(mesh.devices.reshape(4, 2, 2, 2, 4), ALL)
    in_specs = (
        P(CTX, None),
        P(),
        P(CTX, None),
        P(CTX, None),
        P(None, TP),
        P(None, TP),
        P(None, TP),
        P(TP, None),
        P(TP, None),
        P(None, TP, None),
        P(None, None, TP),
    )
    out_specs = (
        P(CTX, None),
        P(CTX, TP),
        P(CTX, TP),
        P(CTX, TP),
        P(TP, CTX),
        P(TP, CTX),
        P(None, CTX, TP),
    )
    return jax.shard_map(
        per_device, mesh=fine, in_specs=in_specs, out_specs=out_specs, check_vma=False
    )
```

```python
import math

import jax
import jax.numpy as jnp
from jax import lax
from jax.experimental import pallas as pl
from jax.experimental.pallas import tpu as pltpu
from jax.sharding import Mesh
from jax.sharding import PartitionSpec as P

HD = 128
EPS = 1e-05
NEG = -1e30
SCALE = 1.0 / math.sqrt(HD)
CTX = ("x", "yl", "core")
CHIPS = ("x", "yl")
TP = ("yh", "z")
ALL = CTX + TP
BF = jnp.bfloat16
F32 = jnp.float32
RUN = 96
QB = 256
KB = 512


def rms_rows(values):
    return values * lax.rsqrt(jnp.mean(values * values, axis=-1, keepdims=True) + EPS)


def dot(left, right, dims):
    return lax.dot_general(left, right, (dims, ((), ())), preferred_element_type=F32)


def exchange(parts, axes):
    return lax.all_to_all(parts, axes, 0, 0, tiled=True)


def spread(block, axes, count):
    return exchange(jnp.broadcast_to(block[None], (count,) + block.shape), axes)


def total(parts):
    return jnp.sum(parts.astype(F32), axis=0)


def swap_core(block):
    return lax.ppermute(block, "core", [(0, 1), (1, 0)])


def after(value, *earlier):
    return lax.optimization_barrier((value,) + earlier)[0]


def thirds(values):
    high = lax.reduce_precision(values, 8, 7)
    rest = values - high
    middle = lax.reduce_precision(rest, 8, 7)
    return jnp.stack([high, middle, rest - middle]).astype(BF)


def kernel_call(body, out_shape, scratch, flops, byte_count, count, far_in=0):
    near, far = pl.BlockSpec(memory_space=pltpu.VMEM), pl.BlockSpec(memory_space=pl.ANY)
    return pl.pallas_call(
        body,
        out_shape=out_shape,
        in_specs=[pl.BlockSpec(memory_space=pltpu.SMEM)]
        + [near] * (count - 1 - far_in)
        + [far] * far_in,
        out_specs=jax.tree.map(lambda _: near, out_shape),
        scratch_shapes=scratch,
        compiler_params=pltpu.CompilerParams(vmem_limit_bytes=48 << 20),
        cost_estimate=pl.CostEstimate(
            flops=flops, bytes_accessed=byte_count, transcendentals=0
        ),
    )


CORE, CTX_AT, TP_AT, SHARDS, LEVELS = 32, 33, 34, 35, 43


def forward_body(
    meta_ref, q_ref, q_come_ref, kv_ref, own_ref, other_ref, lse_ref, qs, key_pos
):
    first = meta_ref[CORE] == 0
    ctx = meta_ref[CTX_AT]
    qs[...] = jnp.zeros_like(qs)
    for run in range(2):
        rows = slice(run * RUN, run * RUN + RUN)
        qs[run * 128 : run * 128 + RUN, :] = jnp.where(
            first, q_ref[rows, :HD], q_ref[rows, HD:]
        )
        qs[256 + run * 128 : 256 + run * 128 + RUN, :] = q_come_ref[rows, :]
    down = lax.broadcasted_iota(jnp.int32, (RUN, 128), 0)
    for run in range(key_pos.shape[0] // RUN):
        key_pos[run * RUN : run * RUN + RUN, :] = down + meta_ref[run]
    lse_ref[...] = jnp.zeros_like(lse_ref)
    across = lax.broadcasted_iota(jnp.int32, (1, 128), 1)
    for part in range(4):
        owner = ctx if part < 2 else ctx + 1 - 2 * meta_ref[CORE]
        query_pos = across + meta_ref[2 * owner + part % 2]
        scores = dot(kv_ref[:, :HD], qs[part * 128 : part * 128 + 128, :], ((1,), (1,))) * SCALE
        scores = jnp.where(key_pos[...] <= query_pos, scores, NEG)
        peak = jnp.max(scores, axis=0, keepdims=True)
        weights = jnp.exp(scores - peak)
        denominator = jnp.sum(weights, axis=0, keepdims=True)
        probs = (weights * (1.0 / denominator)).astype(BF)
        result = dot(probs, kv_ref[:, HD:], ((0,), (0,))).astype(BF)
        rows = slice(part % 2 * RUN, part % 2 * RUN + RUN)
        (own_ref if part < 2 else other_ref)[rows, :] = result[:RUN, :]
        lse_ref[part : part + 1, :] = peak + jnp.log(denominator)


def embed_body(meta_ref, ids_ref, *refs):
    out_ref = refs[-1]
    rows = ids_ref.shape[0]
    lane = lax.broadcasted_iota(jnp.int32, (rows, 256), 1)
    sums = jnp.zeros((rows, 1024), F32)
    for block in range(8):
        pick = (ids_ref[...] == lane + meta_ref[SHARDS + block] * 256).astype(F32).astype(BF)
        sums += dot(pick, refs[block][...], ((1,), (0,)))
    out_ref[...] = sums.astype(BF)


def head_body(meta_ref, base_ref, embed_ref, target_ref, cot_ref, *refs):
    tables, (unit_ref, dlogits_ref, grad_ref, loss_ref, logits_ref) = refs[:8], refs[8:]
    rows = base_ref.shape[0]
    keep = jnp.where(meta_ref[TP_AT] > 0, 1.0, 0.0)
    depth_in = base_ref[...].astype(F32) + embed_ref[...].astype(F32) * keep
    inverse_rms = lax.rsqrt(jnp.mean(depth_in * depth_in, axis=-1, keepdims=True) + EPS)
    scaled = depth_in * inverse_rms
    unit = scaled.astype(BF)
    unit_ref[...] = unit
    lane = lax.broadcasted_iota(jnp.int32, (rows, 256), 1)
    peak = jnp.full((rows, 1), NEG, F32)
    for block in range(8):
        cols = slice(block * 256, block * 256 + 256)
        logits = dot(unit, tables[block][...], ((1,), (0,)))
        logits_ref[:, cols] = logits
        peak = jnp.maximum(peak, jnp.max(logits, axis=-1, keepdims=True))
    denominator = jnp.zeros((rows, 1), F32)
    chosen = jnp.zeros((rows, 1), F32)
    for block in range(8):
        cols = slice(block * 256, block * 256 + 256)
        logits = logits_ref[:, cols]
        is_target = target_ref[...] == lane + meta_ref[SHARDS + block] * 256
        chosen += jnp.sum(jnp.where(is_target, logits, 0.0), axis=-1, keepdims=True)
        terms = jnp.exp(logits - peak)
        denominator += jnp.sum(terms, axis=-1, keepdims=True)
        logits_ref[:, cols] = terms
    loss_ref[...] = jnp.log(denominator) + peak - chosen
    inverse = 1.0 / denominator
    cot = cot_ref[...]
    unit_grad = jnp.zeros((rows, 1024), F32)
    for block in range(8):
        cols = slice(block * 256, block * 256 + 256)
        start = meta_ref[SHARDS + block] * 256
        hit = jnp.where(target_ref[...] == lane + start, 1.0, 0.0)
        dlogits = (cot * (logits_ref[:, cols] * inverse - hit)).astype(BF)
        dlogits_ref[:, pl.ds(pl.multiple_of(start, 256), 256)] = dlogits
        unit_grad += dot(dlogits, tables[block][...], ((1,), (1,)))
    centre = jnp.mean(unit_grad * scaled, axis=-1, keepdims=True)
    grad_ref[...] = (inverse_rms * (unit_grad - scaled * centre)).astype(BF)


STAT_AT, OUTER_AT, SEND = 192, 224, 352


def send_body(
    meta_ref, summed_ref, fold_ref, attended_ref, lse_ref, lse_come_ref, out_ref, stat, product
):
    first = meta_ref[CORE] == 0
    summed = summed_ref[...]
    attended = attended_ref[...]
    grad = dot(summed, fold_ref[...], ((1,), (0,))).astype(BF)
    outer = dot(summed, attended, ((0,), (0,))).astype(BF)
    for block in range(16):
        out_ref[block, OUTER_AT : OUTER_AT + 64, :] = outer[block * 64 : block * 64 + 64, :HD]
        out_ref[block, OUTER_AT + 64 :, :] = outer[block * 64 : block * 64 + 64, HD:]
    ones = jnp.ones((8, 128), F32)
    for head in range(2):
        cols = slice(head * HD, head * HD + HD)
        stat[...] = jnp.zeros_like(stat)
        product[...] = jnp.zeros_like(product)
        for run in range(2):
            rows = slice(run * RUN, run * RUN + RUN)
            product[:RUN, :] = grad[rows, cols].astype(F32) * attended[rows, cols].astype(F32)
            centre = lax.dot_general(
                ones, product[...], (((1,), (1,)), ((), ())),
                preferred_element_type=F32, precision=lax.Precision.HIGHEST,
            )[:1, :]
            mine = lse_ref[run : run + 1, :]
            come = lse_come_ref[2 + run : 3 + run, :]
            lse = jnp.where(first, mine, come) if head == 0 else jnp.where(first, come, mine)
            for at, value in ((0, lse * (-1.0 / SCALE)), (3, -centre)):
                for term in range(3):
                    part = value.astype(BF).astype(F32)
                    row = run * 16 + at + term
                    stat[row : row + 1, :] = part
                    value = value - part
        packed = stat[...].astype(BF)
        for block in range(head, 16, 2):
            out_ref[block, :STAT_AT, :] = grad[:, cols]
            out_ref[block, STAT_AT:OUTER_AT, :] = packed


def backward_body(
    meta_ref, come_ref, q_far, kv_far, grads, q_ref, kv_ref, qs, ks, vs, gs, dq, dk, dv, sems
):
    q_copy = pltpu.make_async_copy(q_far, q_ref, sems.at[0])
    kv_copy = pltpu.make_async_copy(kv_far, kv_ref, sems.at[1])
    q_copy.start()
    kv_copy.start()
    core = meta_ref[CORE]
    first = core == 0
    total_rows = q_far.shape[0]
    runs = total_rows // RUN
    stat_row = lax.broadcasted_iota(jnp.int32, (16, 128), 0)
    stat_lane = lax.broadcasted_iota(jnp.int32, (16, 128), 1)
    place_lse = jnp.where((stat_row == stat_lane) & (stat_lane < 3), 1.0, 0.0).astype(BF)
    place_centre = jnp.where((stat_row == stat_lane + 3) & (stat_lane < 3), 1.0, 0.0).astype(BF)
    for run in range(runs):
        src = slice(run * RUN, run * RUN + RUN)
        dst = pl.ds(pl.multiple_of(meta_ref[run], 32), RUN)
        half = slice(run % 2 * RUN, run % 2 * RUN + RUN)
        stats = come_ref[run // 2, STAT_AT + run % 2 * 16 : STAT_AT + run % 2 * 16 + 16, :]
        qs[dst, HD:] = dot(stats, place_lse, ((0,), (0,))).astype(BF)[:RUN, :]
        gs[dst, :HD] = come_ref[run // 2, half, :]
        gs[dst, HD:] = dot(stats, place_centre, ((0,), (0,))).astype(BF)[:RUN, :]

    ks[:, HD:] = jnp.ones((total_rows, HD), BF)
    vs[:, HD:] = jnp.ones((total_rows, HD), BF)
    dk[...] = jnp.zeros_like(dk)
    dv[...] = jnp.zeros_like(dv)
    q_copy.wait()
    kv_copy.wait()
    for run in range(runs):
        src = slice(run * RUN, run * RUN + RUN)
        dst = pl.ds(pl.multiple_of(meta_ref[run], 32), RUN)
        qs[dst, :HD] = jnp.where(first, q_ref[src, :HD], q_ref[src, HD:])
        ks[dst, :HD] = kv_ref[src, :HD]
        vs[dst, :HD] = kv_ref[src, HD:]

    @pl.loop(0, total_rows // QB)
    def _(block):
        q_rows = pl.ds(pl.multiple_of(block * QB, QB), QB)
        q = qs[q_rows, :]
        g = gs[q_rows, :]

        def step(chunk, running, masked):
            rows = pl.ds(pl.multiple_of(chunk * KB, KB), KB)
            k = ks[rows, :]
            v = vs[rows, :]
            shifted = dot(k, q, ((1,), (1,)))
            if masked:
                key_at = lax.broadcasted_iota(jnp.int32, (KB, QB), 0) + chunk * KB
                query_at = lax.broadcasted_iota(jnp.int32, (KB, QB), 1) + block * QB
                shifted = jnp.where(key_at <= query_at, shifted, NEG)
            probs = jnp.exp(shifted * SCALE)
            score_grad = (probs * dot(v, g, ((1,), (1,)))).astype(BF)
            dv[rows, :] += dot(probs.astype(BF), g[:, :HD], ((1,), (0,)))
            dk[rows, :] += dot(score_grad, q[:, :HD], ((1,), (0,)))
            return running + dot(score_grad, k[:, :HD], ((0,), (0,)))

        last = block // (KB // QB)
        running = lax.fori_loop(
            0, last, lambda chunk, acc: step(chunk, acc, False), jnp.zeros((QB, HD), F32)
        )
        dq[q_rows, :] = step(last, running, True)

    for run in range(runs):
        src = slice(run * RUN, run * RUN + RUN)
        dst = pl.ds(pl.multiple_of(meta_ref[run], 32), RUN)
        grads[src, :HD] = (dq[dst, :] * SCALE).astype(BF)
        grads[src, HD : 2 * HD] = (dk[dst, :] * SCALE).astype(BF)
        grads[src, 2 * HD :] = dv[dst, :].astype(BF)


def weight_body(meta_ref, grads_ref, *refs):
    normed_refs, (keep_ref, send_ref) = refs[:16], refs[16:]
    core = meta_ref[CORE]
    first = core == 0
    sums = jnp.zeros((512, 3 * HD), F32)
    for hop in range(8):
        from_x = lax.rem(lax.div(meta_ref[CTX_AT], 4) + 4 - hop // 2, 4)
        from_yl = lax.rem(lax.div(meta_ref[CTX_AT], 2) + hop % 2, 2)
        for side in range(2):
            from_core = core if side == 0 else 1 - core
            start = (from_x * 2 + from_yl) * 384 + from_core * 192
            rows = pl.ds(pl.multiple_of(start, 192), 192)
            sums += dot(normed_refs[side * 8 + hop][...], grads_ref[rows, :], ((0,), (0,)))
    keep_ref[...] = jnp.where(first, sums[:256], sums[256:])
    send_ref[...] = jnp.where(first, sums[256:], sums[:256])


def cut_body(meta_ref, normed_ref, *out_refs):
    at_x = lax.div(meta_ref[CTX_AT], 4)
    at_yl = lax.rem(lax.div(meta_ref[CTX_AT], 2), 2)
    for hop, out_ref in enumerate(out_refs):
        chip = lax.rem(at_x + hop // 2, 4) * 2 + lax.rem(at_yl + hop % 2, 2)
        out_ref[...] = normed_ref[:, pl.ds(pl.multiple_of(chip * 512, 512), 512)]


def widen_body(meta_ref, piece_ref, out_ref):
    owner = lax.div(meta_ref[CTX_AT], 2)
    out_ref[:, :512] = piece_ref[owner, :32, :].astype(F32)
    out_ref[:, 512:] = piece_ref[owner, 32:, :].astype(F32)


def grad_out_body(meta_ref, outer_ref, depth_ref, out_ref):
    out_ref[...] = dot(
        outer_ref[...].astype(BF), depth_ref[...].astype(BF), ((0,), (1,))
    )


def join_body(meta_ref, keep_ref, come_ref, *out_refs):
    first = meta_ref[CORE] == 0
    for at, out_ref in enumerate(out_refs):
        cols = slice(at * HD, at * HD + HD)
        keep, come = keep_ref[:, cols], come_ref[:, cols]
        out_ref[:, :HD] = jnp.where(first, keep, come)
        out_ref[:, HD:] = jnp.where(first, come, keep)


def sum_piece_tp(part):
    rows, cols = part.shape
    return total(exchange(part.reshape(8, rows // 8, cols), TP)).astype(BF)


def gather_wide(block, axes):
    return lax.all_gather(block, axes, axis=0, tiled=True)


def per_device(
    frames,
    frame_pos,
    codes,
    loss_grad,
    w_query,
    w_key,
    w_value,
    w_out,
    w_depth_in,
    code_embed,
    code_head,
):
    rows = frames.shape[0]
    frame_total = frame_pos.shape[0]
    x, yl, core = lax.axis_index("x"), lax.axis_index("yl"), lax.axis_index("core")
    yh, z = lax.axis_index("yh"), lax.axis_index("z")
    ctx = lax.axis_index(CTX)
    tp = lax.axis_index(TP)
    first = core == 0

    shards, head_blocks, embed_blocks = [], [], []
    for block in range(4):
        far, near = block // 2, block % 2 * 2
        level = (yh + far) % 2 * 4 + (z + near + core) % 4
        head_blocks.append(lax.dynamic_index_in_dim(code_head, level, 0, False))
        embed_blocks.append(
            lax.dynamic_index_in_dim(code_embed, jnp.maximum(level - 1, 0), 0, False)
        )
    frames, *blocks = lax.optimization_barrier((frames, *head_blocks, *embed_blocks))
    for side in range(2):
        for block in range(4):
            far, near = block // 2, block % 2 * 2
            turn = near + (core if side == 0 else 1 - core)
            shards.append((yh + far) % 2 * 4 + (z + 4 - turn) % 4)
    own_blocks = []
    for at, operand in enumerate(blocks):
        far, near = at % 4 // 2, at % 2 * 2
        moves = []
        for a in range(2):
            for k in range(2):
                for h in range(2):
                    for d in range(4):
                        to = ((a + far) % 2, k, (h + far) % 2, (d + near + k) % 4)
                        moves.append(
                            (((a * 2 + k) * 2 + h) * 4 + d, ((to[0] * 2 + to[1]) * 2 + to[2]) * 4 + to[3])
                        )
        own_blocks.append(lax.ppermute(operand, ("yl", "core", "yh", "z"), moves))
    other_blocks = [swap_core(block) for block in own_blocks]
    head_tables = own_blocks[:4] + other_blocks[:4]
    embed_tables = own_blocks[4:] + other_blocks[4:]
    meta = jnp.concatenate(
        [frame_pos[::RUN], jnp.stack([core, ctx, tp] + shards).astype(jnp.int32)]
    )

    depth_cols = lax.dynamic_slice_in_dim(w_depth_in, ctx * 64, 64, 1).T
    depth_half = lax.dynamic_slice_in_dim(w_depth_in, core * 256, 256, 0)
    depth_half = depth_half.reshape(8, 32, 2, 512).transpose(0, 2, 1, 3).reshape(8, 64, 512)
    depth_cols = exchange(
        jnp.concatenate([jnp.broadcast_to(depth_cols[None], (8, 64, 512)), depth_half], axis=1), TP
    )
    depth_piece = depth_cols[:, 64:]
    depth_cols = depth_cols[:, :64]
    fold_cols = lax.dot_general(
        depth_cols, w_out.reshape(256, 8, 512), (((0, 2), (1, 2)), ((), ())),
        preferred_element_type=F32,
    ).astype(BF)

    normed = rms_rows(frames.astype(F32)).astype(BF)
    key = dot(normed, w_key, ((1,), (0,))).astype(BF)
    value = dot(normed, w_value, ((1,), (0,))).astype(BF)
    query = dot(normed, w_query, ((1,), (0,))).astype(BF)

    key_value = jnp.stack(
        [jnp.concatenate([key[:, :HD], value[:, :HD]], 1),
         jnp.concatenate([key[:, HD:], value[:, HD:]], 1)]
    )
    key_value = exchange(
        after(
            jnp.broadcast_to(key_value[None], (8, 2, rows, 2 * HD)).reshape(16, rows, 2 * HD),
            depth_cols,
        ),
        CTX,
    ).reshape(frame_total, 2 * HD)
    query_come = swap_core(jnp.where(first, query[:, HD:], query[:, :HD]))

    own_part, other_part, lse = kernel_call(
        forward_body,
        (
            jax.ShapeDtypeStruct((rows, HD), BF),
            jax.ShapeDtypeStruct((rows, HD), BF),
            jax.ShapeDtypeStruct((8, 128), F32),
        ),
        [pltpu.VMEM((512, HD), BF), pltpu.VMEM((frame_total, 128), jnp.int32)],
        2_000_000_000, 4_000_000, 4,
    )(meta, query, query_come, key_value)
    come_part = swap_core(other_part)
    lse_come = swap_core(lse)
    attended = jnp.where(
        first,
        jnp.concatenate([own_part, come_part], 1),
        jnp.concatenate([come_part, own_part], 1),
    )
    fold = spread(after(fold_cols, key_value), CTX, 16).reshape(1024, 2 * HD)

    base = sum_piece_tp(dot(attended, fold, ((1,), (1,))).astype(BF))
    base = spread(base, TP, 8).reshape(rows, 1024)

    level_ids = jnp.arange(8, dtype=jnp.int32)[None, :]
    target = jnp.sum(jnp.where(level_ids == tp, codes, 0), axis=1, keepdims=True)
    cotangent = jnp.sum(jnp.where(level_ids == tp, loss_grad, 0.0), axis=1, keepdims=True)
    previous = jnp.sum(jnp.where(level_ids + 1 == tp, codes, 0), axis=1, keepdims=True)
    embedded = kernel_call(
        embed_body, jax.ShapeDtypeStruct((rows, 1024), BF), [], 800_000_000, 5_000_000, 10
    )(meta, previous, *embed_tables)
    unit, dlogits, depth_grad, loss = kernel_call(
        head_body,
        (
            jax.ShapeDtypeStruct((rows, 1024), BF),
            jax.ShapeDtypeStruct((rows, 2048), BF),
            jax.ShapeDtypeStruct((rows, 1024), BF),
            jax.ShapeDtypeStruct((rows, 1), F32),
        ),
        [pltpu.VMEM((rows, 2048), F32)],
        2_000_000_000, 6_000_000, 13,
    )(meta, base, embedded, target, cotangent, *head_tables)

    query_all = lax.all_gather(after(query, depth_grad), CTX, axis=0, tiled=True)

    normed_own = []
    cuts = kernel_call(
        cut_body, (jax.ShapeDtypeStruct((rows, 512), BF),) * 8, [], 0, 3_000_000, 2
    )(meta, after(normed, depth_grad))
    for hop, piece in enumerate(cuts):
        moves = [
            (a * 2 + b, (a + hop // 2) % 4 * 2 + (b + hop % 2) % 2)
            for a in range(4) for b in range(2)
        ]
        normed_own.append(lax.ppermute(piece, CHIPS, moves) if hop else piece)

    summed = sum_piece_tp(depth_grad)
    depth_rows = kernel_call(
        widen_body, jax.ShapeDtypeStruct((32, 1024), F32), [], 0, 700_000, 2
    )(meta, after(depth_piece, summed))
    depth_rows = gather_wide(depth_rows, TP)
    summed = spread(after(summed, *normed_own[:4]), TP, 8).reshape(rows, 1024)

    send = kernel_call(
        send_body,
        jax.ShapeDtypeStruct((16, SEND, 128), BF),
        [pltpu.VMEM((32, 128), F32), pltpu.VMEM((128, 128), F32)],
        400_000_000, 3_000_000, 6,
    )(meta, after(summed, *normed_own[4:]), fold, attended, lse, lse_come)
    come = exchange(send, CTX)

    unit, dlogits = after(unit, send), after(dlogits, send)
    unit_blocks = unit.reshape(rows, 8, 2, 64)
    unit_keep = lax.dynamic_index_in_dim(unit_blocks, core, 2, False).reshape(rows, 512)
    unit_send = lax.dynamic_index_in_dim(unit_blocks, 1 - core, 2, False).reshape(rows, 512)
    head_come = swap_core(dot(unit_send, dlogits, ((0,), (0,))).astype(BF))
    head_part = (dot(unit_keep, dlogits, ((0,), (0,))) + head_come.astype(F32)).astype(BF)
    head_parts = exchange(after(head_part, come).reshape(8, 64, 2048), CHIPS)

    outer_own = total(come[:, OUTER_AT:])
    outer_own = jnp.concatenate([outer_own[:64], outer_own[64:]], axis=1)
    outer = gather_wide(outer_own, CTX)

    grads = kernel_call(
        backward_body,
        jax.ShapeDtypeStruct((frame_total, 3 * HD), BF),
        [pltpu.VMEM((frame_total, 2 * HD), BF)] * 6
        + [pltpu.VMEM((frame_total, HD), F32)] * 3
        + [pltpu.SemaphoreType.DMA((2,))],
        25_000_000_000, 8_000_000, 4, 2,
    )(meta, after(come, outer_own, head_part), query_all, key_value)
    head_sum = total(after(head_parts, grads)).astype(BF)
    normed_other = [swap_core(piece) for piece in normed_own]
    weights_keep, weights_send = kernel_call(
        weight_body,
        (jax.ShapeDtypeStruct((256, 3 * HD), F32), jax.ShapeDtypeStruct((256, 3 * HD), F32)),
        [], 1_200_000_000, 6_000_000, 18,
    )(meta, grads, *normed_own, *normed_other)
    weights_come = swap_core(weights_send)
    grad_query, grad_key, grad_value = kernel_call(
        join_body, (jax.ShapeDtypeStruct((256, 2 * HD), F32),) * 3, [], 0, 2_000_000, 3
    )(meta, weights_keep, weights_come)

    grad_out = kernel_call(
        grad_out_body, jax.ShapeDtypeStruct((2 * HD, 256), F32), [], 100_000_000, 2_000_000, 3
    )(meta, outer, depth_rows)
    depth_part = dot(outer_own.astype(BF), w_out, ((1,), (0,))).astype(BF)
    loss_row = jnp.pad(thirds(loss[:, 0]).reshape(1, 576), ((0, 15), (0, 192)))
    tail = jnp.concatenate(
        [
            jnp.concatenate(
                [depth_part.reshape(64, 8, 512), head_sum.reshape(64, 8, 256)], axis=2
            ).transpose(1, 0, 2),
            jnp.broadcast_to(loss_row[None], (8, 16, 768)),
        ],
        axis=1,
    )
    tail = exchange(tail, TP)
    grad_depth_in = total(tail[:, :64, :512]).T
    grad_head = tail[:, :64, 512:].astype(F32)
    token_loss = total(tail[:, 64, :576].reshape(8, 3, rows).transpose(1, 2, 0))
    return (token_loss, grad_query, grad_key, grad_value, grad_out, grad_depth_in, grad_head)


def solution(mesh):
    fine = Mesh(mesh.devices.reshape(4, 2, 2, 2, 4), ALL)
    in_specs = (
        P(CTX, None),
        P(),
        P(CTX, None),
        P(CTX, None),
        P(None, TP),
        P(None, TP),
        P(None, TP),
        P(TP, None),
        P(TP, None),
        P(None, TP, None),
        P(None, None, TP),
    )
    out_specs = (
        P(CTX, None),
        P(CTX, TP),
        P(CTX, TP),
        P(CTX, TP),
        P(TP, CTX),
        P(TP, CTX),
        P(None, CTX, TP),
    )
    return jax.shard_map(
        per_device, mesh=fine, in_specs=in_specs, out_specs=out_specs, check_vma=False
    )
```

```python
import math

import jax
import jax.numpy as jnp
from jax import lax
from jax.experimental import pallas as pl
from jax.experimental.pallas import tpu as pltpu
from jax.sharding import Mesh
from jax.sharding import PartitionSpec as P

HD = 128
EPS = 1e-05
NEG = -1e30
SCALE = 1.0 / math.sqrt(HD)
CTX = ("x", "yl", "core")
CHIPS = ("x", "yl")
TP = ("yh", "z")
ALL = CTX + TP
BF = jnp.bfloat16
F32 = jnp.float32
RUN = 96
QB = 256
KB = 512


def rms_rows(values):
    return values * lax.rsqrt(jnp.mean(values * values, axis=-1, keepdims=True) + EPS)


def dot(left, right, dims):
    return lax.dot_general(left, right, (dims, ((), ())), preferred_element_type=F32)


def exchange(parts, axes):
    return lax.all_to_all(parts, axes, 0, 0, tiled=True)


def spread(block, axes, count):
    return exchange(jnp.broadcast_to(block[None], (count,) + block.shape), axes)


def total(parts):
    return jnp.sum(parts.astype(F32), axis=0)


def swap_core(block):
    return lax.ppermute(block, "core", [(0, 1), (1, 0)])


def after(value, *earlier):
    return lax.optimization_barrier((value,) + earlier)[0]


def thirds(values):
    high = lax.reduce_precision(values, 8, 7)
    rest = values - high
    middle = lax.reduce_precision(rest, 8, 7)
    return jnp.stack([high, middle, rest - middle]).astype(BF)


def kernel_call(body, out_shape, scratch, flops, byte_count, count, far_in=0):
    near, far = pl.BlockSpec(memory_space=pltpu.VMEM), pl.BlockSpec(memory_space=pl.ANY)
    return pl.pallas_call(
        body,
        out_shape=out_shape,
        in_specs=[pl.BlockSpec(memory_space=pltpu.SMEM)]
        + [near] * (count - 1 - far_in)
        + [far] * far_in,
        out_specs=jax.tree.map(lambda _: near, out_shape),
        scratch_shapes=scratch,
        compiler_params=pltpu.CompilerParams(vmem_limit_bytes=48 << 20),
        cost_estimate=pl.CostEstimate(
            flops=flops, bytes_accessed=byte_count, transcendentals=0
        ),
    )


CORE, CTX_AT, TP_AT, SHARDS, LEVELS = 32, 33, 34, 35, 43


def forward_body(
    meta_ref, q_ref, q_come_ref, kv_ref, own_ref, other_ref, lse_ref, qs, key_pos
):
    first = meta_ref[CORE] == 0
    ctx = meta_ref[CTX_AT]
    qs[...] = jnp.zeros_like(qs)
    for run in range(2):
        rows = slice(run * RUN, run * RUN + RUN)
        qs[run * 128 : run * 128 + RUN, :] = jnp.where(
            first, q_ref[rows, :HD], q_ref[rows, HD:]
        )
        qs[256 + run * 128 : 256 + run * 128 + RUN, :] = q_come_ref[rows, :]
    down = lax.broadcasted_iota(jnp.int32, (RUN, 128), 0)
    for run in range(key_pos.shape[0] // RUN):
        key_pos[run * RUN : run * RUN + RUN, :] = down + meta_ref[run]
    lse_ref[...] = jnp.zeros_like(lse_ref)
    across = lax.broadcasted_iota(jnp.int32, (1, 128), 1)
    for part in range(4):
        owner = ctx if part < 2 else ctx + 1 - 2 * meta_ref[CORE]
        query_pos = across + meta_ref[2 * owner + part % 2]
        scores = dot(kv_ref[:, :HD], qs[part * 128 : part * 128 + 128, :], ((1,), (1,))) * SCALE
        scores = jnp.where(key_pos[...] <= query_pos, scores, NEG)
        peak = jnp.max(scores, axis=0, keepdims=True)
        weights = jnp.exp(scores - peak)
        denominator = jnp.sum(weights, axis=0, keepdims=True)
        probs = (weights * (1.0 / denominator)).astype(BF)
        result = dot(probs, kv_ref[:, HD:], ((0,), (0,))).astype(BF)
        rows = slice(part % 2 * RUN, part % 2 * RUN + RUN)
        (own_ref if part < 2 else other_ref)[rows, :] = result[:RUN, :]
        lse_ref[part : part + 1, :] = peak + jnp.log(denominator)


def embed_body(meta_ref, ids_ref, *refs):
    out_ref = refs[-1]
    rows = ids_ref.shape[0]
    lane = lax.broadcasted_iota(jnp.int32, (rows, 256), 1)
    sums = jnp.zeros((rows, 1024), F32)
    for block in range(8):
        pick = (ids_ref[...] == lane + meta_ref[SHARDS + block] * 256).astype(F32).astype(BF)
        sums += dot(pick, refs[block][...], ((1,), (0,)))
    out_ref[...] = sums.astype(BF)


def head_body(meta_ref, base_ref, embed_ref, target_ref, cot_ref, *refs):
    tables, (unit_ref, dlogits_ref, grad_ref, loss_ref, logits_ref) = refs[:8], refs[8:]
    rows = base_ref.shape[0]
    keep = jnp.where(meta_ref[TP_AT] > 0, 1.0, 0.0)
    depth_in = base_ref[...].astype(F32) + embed_ref[...].astype(F32) * keep
    inverse_rms = lax.rsqrt(jnp.mean(depth_in * depth_in, axis=-1, keepdims=True) + EPS)
    scaled = depth_in * inverse_rms
    unit = scaled.astype(BF)
    unit_ref[...] = unit
    lane = lax.broadcasted_iota(jnp.int32, (rows, 256), 1)
    peak = jnp.full((rows, 1), NEG, F32)
    for block in range(8):
        cols = slice(block * 256, block * 256 + 256)
        logits = dot(unit, tables[block][...], ((1,), (0,)))
        logits_ref[:, cols] = logits
        peak = jnp.maximum(peak, jnp.max(logits, axis=-1, keepdims=True))
    denominator = jnp.zeros((rows, 1), F32)
    chosen = jnp.zeros((rows, 1), F32)
    for block in range(8):
        cols = slice(block * 256, block * 256 + 256)
        logits = logits_ref[:, cols]
        is_target = target_ref[...] == lane + meta_ref[SHARDS + block] * 256
        chosen += jnp.sum(jnp.where(is_target, logits, 0.0), axis=-1, keepdims=True)
        terms = jnp.exp(logits - peak)
        denominator += jnp.sum(terms, axis=-1, keepdims=True)
        logits_ref[:, cols] = terms
    loss_ref[...] = jnp.log(denominator) + peak - chosen
    inverse = 1.0 / denominator
    cot = cot_ref[...]
    unit_grad = jnp.zeros((rows, 1024), F32)
    for block in range(8):
        cols = slice(block * 256, block * 256 + 256)
        start = meta_ref[SHARDS + block] * 256
        hit = jnp.where(target_ref[...] == lane + start, 1.0, 0.0)
        dlogits = (cot * (logits_ref[:, cols] * inverse - hit)).astype(BF)
        dlogits_ref[:, pl.ds(pl.multiple_of(start, 256), 256)] = dlogits
        unit_grad += dot(dlogits, tables[block][...], ((1,), (1,)))
    centre = jnp.mean(unit_grad * scaled, axis=-1, keepdims=True)
    grad_ref[...] = (inverse_rms * (unit_grad - scaled * centre)).astype(BF)


STAT_AT, OUTER_AT, SEND = 192, 224, 352


def send_body(
    meta_ref, summed_ref, fold_ref, attended_ref, lse_ref, lse_come_ref, out_ref, stat, product
):
    first = meta_ref[CORE] == 0
    summed = summed_ref[...]
    attended = attended_ref[...]
    grad = dot(summed, fold_ref[...], ((1,), (0,))).astype(BF)
    outer = dot(summed, attended, ((0,), (0,))).astype(BF)
    for block in range(16):
        out_ref[block, OUTER_AT : OUTER_AT + 64, :] = outer[block * 64 : block * 64 + 64, :HD]
        out_ref[block, OUTER_AT + 64 :, :] = outer[block * 64 : block * 64 + 64, HD:]
    ones = jnp.ones((8, 128), F32)
    for head in range(2):
        cols = slice(head * HD, head * HD + HD)
        stat[...] = jnp.zeros_like(stat)
        product[...] = jnp.zeros_like(product)
        for run in range(2):
            rows = slice(run * RUN, run * RUN + RUN)
            product[:RUN, :] = grad[rows, cols].astype(F32) * attended[rows, cols].astype(F32)
            centre = lax.dot_general(
                ones, product[...], (((1,), (1,)), ((), ())),
                preferred_element_type=F32, precision=lax.Precision.HIGHEST,
            )[:1, :]
            mine = lse_ref[run : run + 1, :]
            come = lse_come_ref[2 + run : 3 + run, :]
            lse = jnp.where(first, mine, come) if head == 0 else jnp.where(first, come, mine)
            for at, value in ((0, lse * (-1.0 / SCALE)), (3, -centre)):
                for term in range(3):
                    part = value.astype(BF).astype(F32)
                    row = run * 16 + at + term
                    stat[row : row + 1, :] = part
                    value = value - part
        packed = stat[...].astype(BF)
        for block in range(head, 16, 2):
            out_ref[block, :STAT_AT, :] = grad[:, cols]
            out_ref[block, STAT_AT:OUTER_AT, :] = packed


def backward_body(
    meta_ref, come_ref, q_far, kv_far, grads, q_ref, kv_ref, qs, ks, vs, gs, dq, dk, dv, sems
):
    q_copy = pltpu.make_async_copy(q_far, q_ref, sems.at[0])
    kv_copy = pltpu.make_async_copy(kv_far, kv_ref, sems.at[1])
    q_copy.start()
    kv_copy.start()
    core = meta_ref[CORE]
    first = core == 0
    total_rows = q_far.shape[0]
    runs = total_rows // RUN
    stat_row = lax.broadcasted_iota(jnp.int32, (16, 128), 0)
    stat_lane = lax.broadcasted_iota(jnp.int32, (16, 128), 1)
    place_lse = jnp.where((stat_row == stat_lane) & (stat_lane < 3), 1.0, 0.0).astype(BF)
    place_centre = jnp.where((stat_row == stat_lane + 3) & (stat_lane < 3), 1.0, 0.0).astype(BF)
    for run in range(runs):
        src = slice(run * RUN, run * RUN + RUN)
        dst = pl.ds(pl.multiple_of(meta_ref[run], 32), RUN)
        half = slice(run % 2 * RUN, run % 2 * RUN + RUN)
        stats = come_ref[run // 2, STAT_AT + run % 2 * 16 : STAT_AT + run % 2 * 16 + 16, :]
        qs[dst, HD:] = dot(stats, place_lse, ((0,), (0,))).astype(BF)[:RUN, :]
        gs[dst, :HD] = come_ref[run // 2, half, :]
        gs[dst, HD:] = dot(stats, place_centre, ((0,), (0,))).astype(BF)[:RUN, :]

    ks[:, HD:] = jnp.ones((total_rows, HD), BF)
    vs[:, HD:] = jnp.ones((total_rows, HD), BF)
    dk[...] = jnp.zeros_like(dk)
    dv[...] = jnp.zeros_like(dv)
    q_copy.wait()
    kv_copy.wait()
    for run in range(runs):
        src = slice(run * RUN, run * RUN + RUN)
        dst = pl.ds(pl.multiple_of(meta_ref[run], 32), RUN)
        qs[dst, :HD] = jnp.where(first, q_ref[src, :HD], q_ref[src, HD:])
        ks[dst, :HD] = kv_ref[src, :HD]
        vs[dst, :HD] = kv_ref[src, HD:]

    @pl.loop(0, total_rows // QB)
    def _(block):
        q_rows = pl.ds(pl.multiple_of(block * QB, QB), QB)
        q = qs[q_rows, :]
        g = gs[q_rows, :]

        def step(chunk, running, masked):
            rows = pl.ds(pl.multiple_of(chunk * KB, KB), KB)
            k = ks[rows, :]
            v = vs[rows, :]
            shifted = dot(k, q, ((1,), (1,)))
            if masked:
                key_at = lax.broadcasted_iota(jnp.int32, (KB, QB), 0) + chunk * KB
                query_at = lax.broadcasted_iota(jnp.int32, (KB, QB), 1) + block * QB
                shifted = jnp.where(key_at <= query_at, shifted, NEG)
            probs = jnp.exp(shifted * SCALE)
            score_grad = (probs * dot(v, g, ((1,), (1,)))).astype(BF)
            dv[rows, :] += dot(probs.astype(BF), g[:, :HD], ((1,), (0,)))
            dk[rows, :] += dot(score_grad, q[:, :HD], ((1,), (0,)))
            return running + dot(score_grad, k[:, :HD], ((0,), (0,)))

        last = block // (KB // QB)
        running = lax.fori_loop(
            0, last, lambda chunk, acc: step(chunk, acc, False), jnp.zeros((QB, HD), F32)
        )
        dq[q_rows, :] = step(last, running, True)

    for run in range(runs):
        src = slice(run * RUN, run * RUN + RUN)
        dst = pl.ds(pl.multiple_of(meta_ref[run], 32), RUN)
        grads[src, :HD] = (dq[dst, :] * SCALE).astype(BF)
        grads[src, HD : 2 * HD] = (dk[dst, :] * SCALE).astype(BF)
        grads[src, 2 * HD :] = dv[dst, :].astype(BF)


def weight_body(meta_ref, grads_ref, *refs):
    normed_refs, (keep_ref, send_ref) = refs[:16], refs[16:]
    core = meta_ref[CORE]
    first = core == 0
    sums = jnp.zeros((512, 3 * HD), F32)
    for hop in range(8):
        from_x = lax.rem(lax.div(meta_ref[CTX_AT], 4) + 4 - hop // 2, 4)
        from_yl = lax.rem(lax.div(meta_ref[CTX_AT], 2) + hop % 2, 2)
        for side in range(2):
            from_core = core if side == 0 else 1 - core
            start = (from_x * 2 + from_yl) * 384 + from_core * 192
            rows = pl.ds(pl.multiple_of(start, 192), 192)
            sums += dot(normed_refs[side * 8 + hop][...], grads_ref[rows, :], ((0,), (0,)))
    keep_ref[...] = jnp.where(first, sums[:256], sums[256:])
    send_ref[...] = jnp.where(first, sums[256:], sums[:256])


def cut_body(meta_ref, normed_ref, *out_refs):
    at_x = lax.div(meta_ref[CTX_AT], 4)
    at_yl = lax.rem(lax.div(meta_ref[CTX_AT], 2), 2)
    for hop, out_ref in enumerate(out_refs):
        chip = lax.rem(at_x + hop // 2, 4) * 2 + lax.rem(at_yl + hop % 2, 2)
        out_ref[...] = normed_ref[:, pl.ds(pl.multiple_of(chip * 512, 512), 512)]


def widen_body(meta_ref, piece_ref, out_ref):
    owner = lax.div(meta_ref[CTX_AT], 2)
    out_ref[:, :512] = piece_ref[owner, :32, :].astype(F32)
    out_ref[:, 512:] = piece_ref[owner, 32:, :].astype(F32)


def grad_out_body(meta_ref, outer_ref, depth_ref, out_ref):
    out_ref[...] = dot(
        outer_ref[...].astype(BF), depth_ref[...].astype(BF), ((0,), (1,))
    )


def join_body(meta_ref, keep_ref, come_ref, *out_refs):
    first = meta_ref[CORE] == 0
    for at, out_ref in enumerate(out_refs):
        cols = slice(at * HD, at * HD + HD)
        keep, come = keep_ref[:, cols], come_ref[:, cols]
        out_ref[:, :HD] = jnp.where(first, keep, come)
        out_ref[:, HD:] = jnp.where(first, come, keep)


def sum_piece_tp(part):
    rows, cols = part.shape
    return total(exchange(part.reshape(8, rows // 8, cols), TP)).astype(BF)


def gather_wide(block, axes):
    return lax.all_gather(block, axes, axis=0, tiled=True)


def per_device(
    frames,
    frame_pos,
    codes,
    loss_grad,
    w_query,
    w_key,
    w_value,
    w_out,
    w_depth_in,
    code_embed,
    code_head,
):
    rows = frames.shape[0]
    frame_total = frame_pos.shape[0]
    x, yl, core = lax.axis_index("x"), lax.axis_index("yl"), lax.axis_index("core")
    yh, z = lax.axis_index("yh"), lax.axis_index("z")
    ctx = lax.axis_index(CTX)
    tp = lax.axis_index(TP)
    first = core == 0

    shards, head_blocks, embed_blocks = [], [], []
    for block in range(4):
        far, near = block // 2, block % 2 * 2
        level = (yh + far) % 2 * 4 + (z + near + core) % 4
        head_blocks.append(lax.dynamic_index_in_dim(code_head, level, 0, False))
        embed_blocks.append(
            lax.dynamic_index_in_dim(code_embed, jnp.maximum(level - 1, 0), 0, False)
        )
    frames, *blocks = lax.optimization_barrier((frames, *head_blocks, *embed_blocks))
    for side in range(2):
        for block in range(4):
            far, near = block // 2, block % 2 * 2
            turn = near + (core if side == 0 else 1 - core)
            shards.append((yh + far) % 2 * 4 + (z + 4 - turn) % 4)
    own_blocks = []
    for at, operand in enumerate(blocks):
        far, near = at % 4 // 2, at % 2 * 2
        moves = []
        for a in range(2):
            for k in range(2):
                for h in range(2):
                    for d in range(4):
                        to = ((a + far) % 2, k, (h + far) % 2, (d + near + k) % 4)
                        moves.append(
                            (((a * 2 + k) * 2 + h) * 4 + d, ((to[0] * 2 + to[1]) * 2 + to[2]) * 4 + to[3])
                        )
        own_blocks.append(lax.ppermute(operand, ("yl", "core", "yh", "z"), moves))
    other_blocks = [swap_core(block) for block in own_blocks]
    head_tables = own_blocks[:4] + other_blocks[:4]
    embed_tables = own_blocks[4:] + other_blocks[4:]
    meta = jnp.concatenate(
        [frame_pos[::RUN], jnp.stack([core, ctx, tp] + shards).astype(jnp.int32)]
    )

    depth_cols = lax.dynamic_slice_in_dim(w_depth_in, ctx * 64, 64, 1).T
    depth_half = lax.dynamic_slice_in_dim(w_depth_in, core * 256, 256, 0)
    depth_half = depth_half.reshape(8, 32, 2, 512).transpose(0, 2, 1, 3).reshape(8, 64, 512)
    depth_cols = exchange(
        jnp.concatenate([jnp.broadcast_to(depth_cols[None], (8, 64, 512)), depth_half], axis=1), TP
    )
    depth_piece = depth_cols[:, 64:]
    depth_cols = depth_cols[:, :64]
    fold_cols = lax.dot_general(
        depth_cols, w_out.reshape(256, 8, 512), (((0, 2), (1, 2)), ((), ())),
        preferred_element_type=F32,
    ).astype(BF)

    normed = rms_rows(frames.astype(F32)).astype(BF)
    key = dot(normed, w_key, ((1,), (0,))).astype(BF)
    value = dot(normed, w_value, ((1,), (0,))).astype(BF)
    query = dot(normed, w_query, ((1,), (0,))).astype(BF)

    key_value = jnp.stack(
        [jnp.concatenate([key[:, :HD], value[:, :HD]], 1),
         jnp.concatenate([key[:, HD:], value[:, HD:]], 1)]
    )
    key_value = exchange(
        after(
            jnp.broadcast_to(key_value[None], (8, 2, rows, 2 * HD)).reshape(16, rows, 2 * HD),
            depth_cols,
        ),
        CTX,
    ).reshape(frame_total, 2 * HD)
    query_come = swap_core(jnp.where(first, query[:, HD:], query[:, :HD]))

    own_part, other_part, lse = kernel_call(
        forward_body,
        (
            jax.ShapeDtypeStruct((rows, HD), BF),
            jax.ShapeDtypeStruct((rows, HD), BF),
            jax.ShapeDtypeStruct((8, 128), F32),
        ),
        [pltpu.VMEM((512, HD), BF), pltpu.VMEM((frame_total, 128), jnp.int32)],
        2_000_000_000, 4_000_000, 4,
    )(meta, query, query_come, key_value)
    come_part = swap_core(other_part)
    lse_come = swap_core(lse)
    attended = jnp.where(
        first,
        jnp.concatenate([own_part, come_part], 1),
        jnp.concatenate([come_part, own_part], 1),
    )
    fold = spread(after(fold_cols, key_value), CTX, 16).reshape(1024, 2 * HD)

    base = sum_piece_tp(dot(attended, fold, ((1,), (1,))).astype(BF))
    base = spread(base, TP, 8).reshape(rows, 1024)

    level_ids = jnp.arange(8, dtype=jnp.int32)[None, :]
    target = jnp.sum(jnp.where(level_ids == tp, codes, 0), axis=1, keepdims=True)
    cotangent = jnp.sum(jnp.where(level_ids == tp, loss_grad, 0.0), axis=1, keepdims=True)
    previous = jnp.sum(jnp.where(level_ids + 1 == tp, codes, 0), axis=1, keepdims=True)
    depth_rows = kernel_call(
        widen_body, jax.ShapeDtypeStruct((32, 1024), F32), [], 0, 700_000, 2
    )(meta, depth_piece)
    previous = after(previous, depth_rows)
    embedded = kernel_call(
        embed_body, jax.ShapeDtypeStruct((rows, 1024), BF), [], 800_000_000, 5_000_000, 10
    )(meta, previous, *embed_tables)
    unit, dlogits, depth_grad, loss = kernel_call(
        head_body,
        (
            jax.ShapeDtypeStruct((rows, 1024), BF),
            jax.ShapeDtypeStruct((rows, 2048), BF),
            jax.ShapeDtypeStruct((rows, 1024), BF),
            jax.ShapeDtypeStruct((rows, 1), F32),
        ),
        [pltpu.VMEM((rows, 2048), F32)],
        2_000_000_000, 6_000_000, 13,
    )(meta, base, embedded, target, cotangent, *head_tables)

    query_all = lax.all_gather(after(query, depth_grad), CTX, axis=0, tiled=True)
    depth_rows = gather_wide(after(depth_rows, depth_grad), TP)

    normed_own = []
    cuts = kernel_call(
        cut_body, (jax.ShapeDtypeStruct((rows, 512), BF),) * 8, [], 0, 3_000_000, 2
    )(meta, after(normed, depth_grad))
    for hop, piece in enumerate(cuts):
        moves = [
            (a * 2 + b, (a + hop // 2) % 4 * 2 + (b + hop % 2) % 2)
            for a in range(4) for b in range(2)
        ]
        normed_own.append(lax.ppermute(piece, CHIPS, moves) if hop else piece)

    summed = sum_piece_tp(depth_grad)
    summed = spread(summed, TP, 8).reshape(rows, 1024)

    send = kernel_call(
        send_body,
        jax.ShapeDtypeStruct((16, SEND, 128), BF),
        [pltpu.VMEM((32, 128), F32), pltpu.VMEM((128, 128), F32)],
        400_000_000, 3_000_000, 6,
    )(meta, after(summed, *normed_own[:4]), fold, attended, lse, lse_come)
    come = exchange(send, CTX)

    unit, dlogits = after(unit, send), after(dlogits, send)
    unit_blocks = unit.reshape(rows, 8, 2, 64)
    unit_keep = lax.dynamic_index_in_dim(unit_blocks, core, 2, False).reshape(rows, 512)
    unit_send = lax.dynamic_index_in_dim(unit_blocks, 1 - core, 2, False).reshape(rows, 512)
    head_come = swap_core(dot(unit_send, dlogits, ((0,), (0,))).astype(BF))
    head_part = (dot(unit_keep, dlogits, ((0,), (0,))) + head_come.astype(F32)).astype(BF)
    head_parts = exchange(after(head_part, come).reshape(8, 64, 2048), CHIPS)

    outer_own = total(come[:, OUTER_AT:])
    outer_own = jnp.concatenate([outer_own[:64], outer_own[64:]], axis=1)
    outer = gather_wide(outer_own, CTX)

    grads = kernel_call(
        backward_body,
        jax.ShapeDtypeStruct((frame_total, 3 * HD), BF),
        [pltpu.VMEM((frame_total, 2 * HD), BF)] * 6
        + [pltpu.VMEM((frame_total, HD), F32)] * 3
        + [pltpu.SemaphoreType.DMA((2,))],
        25_000_000_000, 8_000_000, 4, 2,
    )(meta, after(come, outer_own, head_part), query_all, key_value)
    head_sum = total(after(head_parts, grads)).astype(BF)
    normed_other = [swap_core(piece) for piece in normed_own]
    weights_keep, weights_send = kernel_call(
        weight_body,
        (jax.ShapeDtypeStruct((256, 3 * HD), F32), jax.ShapeDtypeStruct((256, 3 * HD), F32)),
        [], 1_200_000_000, 6_000_000, 18,
    )(meta, grads, *normed_own, *normed_other)
    weights_come = swap_core(weights_send)
    grad_query, grad_key, grad_value = kernel_call(
        join_body, (jax.ShapeDtypeStruct((256, 2 * HD), F32),) * 3, [], 0, 2_000_000, 3
    )(meta, weights_keep, weights_come)

    grad_out = kernel_call(
        grad_out_body, jax.ShapeDtypeStruct((2 * HD, 256), F32), [], 100_000_000, 2_000_000, 3
    )(meta, outer, depth_rows)
    depth_part = dot(outer_own.astype(BF), w_out, ((1,), (0,))).astype(BF)
    loss_row = jnp.pad(thirds(loss[:, 0]).reshape(1, 576), ((0, 15), (0, 192)))
    tail = jnp.concatenate(
        [
            jnp.concatenate(
                [depth_part.reshape(64, 8, 512), head_sum.reshape(64, 8, 256)], axis=2
            ).transpose(1, 0, 2),
            jnp.broadcast_to(loss_row[None], (8, 16, 768)),
        ],
        axis=1,
    )
    tail = exchange(tail, TP)
    grad_depth_in = total(tail[:, :64, :512]).T
    grad_head = tail[:, :64, 512:].astype(F32)
    token_loss = total(tail[:, 64, :576].reshape(8, 3, rows).transpose(1, 2, 0))
    return (token_loss, grad_query, grad_key, grad_value, grad_out, grad_depth_in, grad_head)


def solution(mesh):
    fine = Mesh(mesh.devices.reshape(4, 2, 2, 2, 4), ALL)
    in_specs = (
        P(CTX, None),
        P(),
        P(CTX, None),
        P(CTX, None),
        P(None, TP),
        P(None, TP),
        P(None, TP),
        P(TP, None),
        P(TP, None),
        P(None, TP, None),
        P(None, None, TP),
    )
    out_specs = (
        P(CTX, None),
        P(CTX, TP),
        P(CTX, TP),
        P(CTX, TP),
        P(TP, CTX),
        P(TP, CTX),
        P(None, CTX, TP),
    )
    return jax.shard_map(
        per_device, mesh=fine, in_specs=in_specs, out_specs=out_specs, check_vma=False
    )
```

```python
import math

import jax
import jax.numpy as jnp
from jax import lax
from jax.experimental import pallas as pl
from jax.experimental.pallas import tpu as pltpu
from jax.sharding import Mesh
from jax.sharding import PartitionSpec as P

HD = 128
EPS = 1e-05
NEG = -1e30
SCALE = 1.0 / math.sqrt(HD)
CTX = ("x", "yl", "core")
CHIPS = ("x", "yl")
TP = ("yh", "z")
ALL = CTX + TP
BF = jnp.bfloat16
F32 = jnp.float32
RUN = 96
QB = 256
KB = 512


def rms_rows(values):
    return values * lax.rsqrt(jnp.mean(values * values, axis=-1, keepdims=True) + EPS)


def dot(left, right, dims):
    return lax.dot_general(left, right, (dims, ((), ())), preferred_element_type=F32)


def exchange(parts, axes):
    return lax.all_to_all(parts, axes, 0, 0, tiled=True)


def spread(block, axes, count):
    return exchange(jnp.broadcast_to(block[None], (count,) + block.shape), axes)


def total(parts):
    return jnp.sum(parts.astype(F32), axis=0)


def swap_core(block):
    return lax.ppermute(block, "core", [(0, 1), (1, 0)])


def after(value, *earlier):
    return lax.optimization_barrier((value,) + earlier)[0]


def thirds(values):
    high = lax.reduce_precision(values, 8, 7)
    rest = values - high
    middle = lax.reduce_precision(rest, 8, 7)
    return jnp.stack([high, middle, rest - middle]).astype(BF)


def kernel_call(body, out_shape, scratch, flops, byte_count, count, far_in=0):
    near, far = pl.BlockSpec(memory_space=pltpu.VMEM), pl.BlockSpec(memory_space=pl.ANY)
    return pl.pallas_call(
        body,
        out_shape=out_shape,
        in_specs=[pl.BlockSpec(memory_space=pltpu.SMEM)]
        + [near] * (count - 1 - far_in)
        + [far] * far_in,
        out_specs=jax.tree.map(lambda _: near, out_shape),
        scratch_shapes=scratch,
        compiler_params=pltpu.CompilerParams(vmem_limit_bytes=48 << 20),
        cost_estimate=pl.CostEstimate(
            flops=flops, bytes_accessed=byte_count, transcendentals=0
        ),
    )


CORE, CTX_AT, TP_AT, SHARDS, LEVELS = 32, 33, 34, 35, 43


def forward_body(
    meta_ref, q_ref, q_come_ref, kv_ref, own_ref, other_ref, lse_ref, qs, key_pos
):
    first = meta_ref[CORE] == 0
    ctx = meta_ref[CTX_AT]
    qs[...] = jnp.zeros_like(qs)
    for run in range(2):
        rows = slice(run * RUN, run * RUN + RUN)
        qs[run * 128 : run * 128 + RUN, :] = jnp.where(
            first, q_ref[rows, :HD], q_ref[rows, HD:]
        )
        qs[256 + run * 128 : 256 + run * 128 + RUN, :] = q_come_ref[rows, :]
    down = lax.broadcasted_iota(jnp.int32, (RUN, 128), 0)
    for run in range(key_pos.shape[0] // RUN):
        key_pos[run * RUN : run * RUN + RUN, :] = down + meta_ref[run]
    lse_ref[...] = jnp.zeros_like(lse_ref)
    across = lax.broadcasted_iota(jnp.int32, (1, 128), 1)
    for part in range(4):
        owner = ctx if part < 2 else ctx + 1 - 2 * meta_ref[CORE]
        query_pos = across + meta_ref[2 * owner + part % 2]
        scores = dot(kv_ref[:, :HD], qs[part * 128 : part * 128 + 128, :], ((1,), (1,))) * SCALE
        scores = jnp.where(key_pos[...] <= query_pos, scores, NEG)
        peak = jnp.max(scores, axis=0, keepdims=True)
        weights = jnp.exp(scores - peak)
        denominator = jnp.sum(weights, axis=0, keepdims=True)
        probs = (weights * (1.0 / denominator)).astype(BF)
        result = dot(probs, kv_ref[:, HD:], ((0,), (0,))).astype(BF)
        rows = slice(part % 2 * RUN, part % 2 * RUN + RUN)
        (own_ref if part < 2 else other_ref)[rows, :] = result[:RUN, :]
        lse_ref[part : part + 1, :] = peak + jnp.log(denominator)


def embed_body(meta_ref, ids_ref, *refs):
    out_ref = refs[-1]
    rows = ids_ref.shape[0]
    lane = lax.broadcasted_iota(jnp.int32, (rows, 256), 1)
    sums = jnp.zeros((rows, 1024), F32)
    for block in range(8):
        pick = (ids_ref[...] == lane + meta_ref[SHARDS + block] * 256).astype(F32).astype(BF)
        sums += dot(pick, refs[block][...], ((1,), (0,)))
    out_ref[...] = sums.astype(BF)


def head_body(meta_ref, base_ref, embed_ref, target_ref, cot_ref, *refs):
    tables, (unit_ref, dlogits_ref, grad_ref, loss_ref, logits_ref) = refs[:8], refs[8:]
    rows = base_ref.shape[0]
    keep = jnp.where(meta_ref[TP_AT] > 0, 1.0, 0.0)
    depth_in = base_ref[...].astype(F32) + embed_ref[...].astype(F32) * keep
    inverse_rms = lax.rsqrt(jnp.mean(depth_in * depth_in, axis=-1, keepdims=True) + EPS)
    scaled = depth_in * inverse_rms
    unit = scaled.astype(BF)
    unit_ref[...] = unit
    lane = lax.broadcasted_iota(jnp.int32, (rows, 256), 1)
    peak = jnp.full((rows, 1), NEG, F32)
    for block in range(8):
        cols = slice(block * 256, block * 256 + 256)
        logits = dot(unit, tables[block][...], ((1,), (0,)))
        logits_ref[:, cols] = logits
        peak = jnp.maximum(peak, jnp.max(logits, axis=-1, keepdims=True))
    denominator = jnp.zeros((rows, 1), F32)
    chosen = jnp.zeros((rows, 1), F32)
    for block in range(8):
        cols = slice(block * 256, block * 256 + 256)
        logits = logits_ref[:, cols]
        is_target = target_ref[...] == lane + meta_ref[SHARDS + block] * 256
        chosen += jnp.sum(jnp.where(is_target, logits, 0.0), axis=-1, keepdims=True)
        terms = jnp.exp(logits - peak)
        denominator += jnp.sum(terms, axis=-1, keepdims=True)
        logits_ref[:, cols] = terms
    loss_ref[...] = jnp.log(denominator) + peak - chosen
    inverse = 1.0 / denominator
    cot = cot_ref[...]
    unit_grad = jnp.zeros((rows, 1024), F32)
    for block in range(8):
        cols = slice(block * 256, block * 256 + 256)
        start = meta_ref[SHARDS + block] * 256
        hit = jnp.where(target_ref[...] == lane + start, 1.0, 0.0)
        dlogits = (cot * (logits_ref[:, cols] * inverse - hit)).astype(BF)
        dlogits_ref[:, pl.ds(pl.multiple_of(start, 256), 256)] = dlogits
        unit_grad += dot(dlogits, tables[block][...], ((1,), (1,)))
    centre = jnp.mean(unit_grad * scaled, axis=-1, keepdims=True)
    grad_ref[...] = (inverse_rms * (unit_grad - scaled * centre)).astype(BF)


STAT_AT, OUTER_AT, SEND = 192, 224, 352


def send_body(
    meta_ref, summed_ref, fold_ref, attended_ref, lse_ref, lse_come_ref, out_ref, stat, product
):
    first = meta_ref[CORE] == 0
    summed = summed_ref[...]
    attended = attended_ref[...]
    grad = dot(summed, fold_ref[...], ((1,), (0,))).astype(BF)
    outer = dot(summed, attended, ((0,), (0,))).astype(BF)
    for block in range(16):
        out_ref[block, OUTER_AT : OUTER_AT + 64, :] = outer[block * 64 : block * 64 + 64, :HD]
        out_ref[block, OUTER_AT + 64 :, :] = outer[block * 64 : block * 64 + 64, HD:]
    ones = jnp.ones((8, 128), F32)
    for head in range(2):
        cols = slice(head * HD, head * HD + HD)
        stat[...] = jnp.zeros_like(stat)
        product[...] = jnp.zeros_like(product)
        for run in range(2):
            rows = slice(run * RUN, run * RUN + RUN)
            product[:RUN, :] = grad[rows, cols].astype(F32) * attended[rows, cols].astype(F32)
            centre = lax.dot_general(
                ones, product[...], (((1,), (1,)), ((), ())),
                preferred_element_type=F32, precision=lax.Precision.HIGHEST,
            )[:1, :]
            mine = lse_ref[run : run + 1, :]
            come = lse_come_ref[2 + run : 3 + run, :]
            lse = jnp.where(first, mine, come) if head == 0 else jnp.where(first, come, mine)
            for at, value in ((0, lse * (-1.0 / SCALE)), (3, -centre)):
                for term in range(3):
                    part = value.astype(BF).astype(F32)
                    row = run * 16 + at + term
                    stat[row : row + 1, :] = part
                    value = value - part
        packed = stat[...].astype(BF)
        for block in range(head, 16, 2):
            out_ref[block, :STAT_AT, :] = grad[:, cols]
            out_ref[block, STAT_AT:OUTER_AT, :] = packed


def backward_body(
    meta_ref, come_ref, q_far, kv_far, grads, q_ref, kv_ref, qs, ks, vs, gs, dq, dk, dv, sems
):
    q_copy = pltpu.make_async_copy(q_far, q_ref, sems.at[0])
    kv_copy = pltpu.make_async_copy(kv_far, kv_ref, sems.at[1])
    q_copy.start()
    kv_copy.start()
    core = meta_ref[CORE]
    first = core == 0
    total_rows = q_far.shape[0]
    runs = total_rows // RUN
    stat_row = lax.broadcasted_iota(jnp.int32, (16, 128), 0)
    stat_lane = lax.broadcasted_iota(jnp.int32, (16, 128), 1)
    place_lse = jnp.where((stat_row == stat_lane) & (stat_lane < 3), 1.0, 0.0).astype(BF)
    place_centre = jnp.where((stat_row == stat_lane + 3) & (stat_lane < 3), 1.0, 0.0).astype(BF)
    for run in range(runs):
        src = slice(run * RUN, run * RUN + RUN)
        dst = pl.ds(pl.multiple_of(meta_ref[run], 32), RUN)
        half = slice(run % 2 * RUN, run % 2 * RUN + RUN)
        stats = come_ref[run // 2, STAT_AT + run % 2 * 16 : STAT_AT + run % 2 * 16 + 16, :]
        qs[dst, HD:] = dot(stats, place_lse, ((0,), (0,))).astype(BF)[:RUN, :]
        gs[dst, :HD] = come_ref[run // 2, half, :]
        gs[dst, HD:] = dot(stats, place_centre, ((0,), (0,))).astype(BF)[:RUN, :]

    ks[:, HD:] = jnp.ones((total_rows, HD), BF)
    vs[:, HD:] = jnp.ones((total_rows, HD), BF)
    dk[...] = jnp.zeros_like(dk)
    dv[...] = jnp.zeros_like(dv)
    q_copy.wait()
    kv_copy.wait()
    for run in range(runs):
        src = slice(run * RUN, run * RUN + RUN)
        dst = pl.ds(pl.multiple_of(meta_ref[run], 32), RUN)
        qs[dst, :HD] = jnp.where(first, q_ref[src, :HD], q_ref[src, HD:])
        ks[dst, :HD] = kv_ref[src, :HD]
        vs[dst, :HD] = kv_ref[src, HD:]

    @pl.loop(0, total_rows // QB)
    def _(block):
        q_rows = pl.ds(pl.multiple_of(block * QB, QB), QB)
        q = qs[q_rows, :]
        g = gs[q_rows, :]

        def step(chunk, running, masked):
            rows = pl.ds(pl.multiple_of(chunk * KB, KB), KB)
            k = ks[rows, :]
            v = vs[rows, :]
            shifted = dot(k, q, ((1,), (1,)))
            if masked:
                key_at = lax.broadcasted_iota(jnp.int32, (KB, QB), 0) + chunk * KB
                query_at = lax.broadcasted_iota(jnp.int32, (KB, QB), 1) + block * QB
                shifted = jnp.where(key_at <= query_at, shifted, NEG)
            probs = jnp.exp(shifted * SCALE)
            score_grad = (probs * dot(v, g, ((1,), (1,)))).astype(BF)
            dv[rows, :] += dot(probs.astype(BF), g[:, :HD], ((1,), (0,)))
            dk[rows, :] += dot(score_grad, q[:, :HD], ((1,), (0,)))
            return running + dot(score_grad, k[:, :HD], ((0,), (0,)))

        last = block // (KB // QB)
        running = lax.fori_loop(
            0, last, lambda chunk, acc: step(chunk, acc, False), jnp.zeros((QB, HD), F32)
        )
        dq[q_rows, :] = step(last, running, True)

    for run in range(runs):
        src = slice(run * RUN, run * RUN + RUN)
        dst = pl.ds(pl.multiple_of(meta_ref[run], 32), RUN)
        grads[src, :HD] = (dq[dst, :] * SCALE).astype(BF)
        grads[src, HD : 2 * HD] = (dk[dst, :] * SCALE).astype(BF)
        grads[src, 2 * HD :] = dv[dst, :].astype(BF)


def weight_body(meta_ref, grads_ref, *refs):
    normed_refs, (keep_ref, send_ref) = refs[:16], refs[16:]
    core = meta_ref[CORE]
    first = core == 0
    sums = jnp.zeros((512, 3 * HD), F32)
    for hop in range(8):
        from_x = lax.rem(lax.div(meta_ref[CTX_AT], 4) + 4 - hop // 2, 4)
        from_yl = lax.rem(lax.div(meta_ref[CTX_AT], 2) + hop % 2, 2)
        for side in range(2):
            from_core = core if side == 0 else 1 - core
            start = (from_x * 2 + from_yl) * 384 + from_core * 192
            rows = pl.ds(pl.multiple_of(start, 192), 192)
            sums += dot(normed_refs[side * 8 + hop][...], grads_ref[rows, :], ((0,), (0,)))
    keep_ref[...] = jnp.where(first, sums[:256], sums[256:])
    send_ref[...] = jnp.where(first, sums[256:], sums[:256])


def cut_body(meta_ref, normed_ref, *out_refs):
    at_x = lax.div(meta_ref[CTX_AT], 4)
    at_yl = lax.rem(lax.div(meta_ref[CTX_AT], 2), 2)
    for hop, out_ref in enumerate(out_refs):
        chip = lax.rem(at_x + hop // 2, 4) * 2 + lax.rem(at_yl + hop % 2, 2)
        out_ref[...] = normed_ref[:, pl.ds(pl.multiple_of(chip * 512, 512), 512)]


def grad_out_body(meta_ref, outer_ref, depth_ref, out_ref):
    out_ref[...] = dot(
        outer_ref[...].astype(BF), depth_ref[...], ((0,), (1,))
    )


def join_body(meta_ref, keep_ref, come_ref, *out_refs):
    first = meta_ref[CORE] == 0
    for at, out_ref in enumerate(out_refs):
        cols = slice(at * HD, at * HD + HD)
        keep, come = keep_ref[:, cols], come_ref[:, cols]
        out_ref[:, :HD] = jnp.where(first, keep, come)
        out_ref[:, HD:] = jnp.where(first, come, keep)


def sum_piece_tp(part):
    rows, cols = part.shape
    return total(exchange(part.reshape(8, rows // 8, cols), TP)).astype(BF)


def gather_wide(block, axes):
    return lax.all_gather(block, axes, axis=0, tiled=True)


def per_device(
    frames,
    frame_pos,
    codes,
    loss_grad,
    w_query,
    w_key,
    w_value,
    w_out,
    w_depth_in,
    code_embed,
    code_head,
):
    rows = frames.shape[0]
    frame_total = frame_pos.shape[0]
    x, yl, core = lax.axis_index("x"), lax.axis_index("yl"), lax.axis_index("core")
    yh, z = lax.axis_index("yh"), lax.axis_index("z")
    ctx = lax.axis_index(CTX)
    tp = lax.axis_index(TP)
    first = core == 0

    shards, head_blocks, embed_blocks = [], [], []
    for block in range(4):
        far, near = block // 2, block % 2 * 2
        level = (yh + far) % 2 * 4 + (z + near + core) % 4
        head_blocks.append(lax.dynamic_index_in_dim(code_head, level, 0, False))
        embed_blocks.append(
            lax.dynamic_index_in_dim(code_embed, jnp.maximum(level - 1, 0), 0, False)
        )
    frames, *blocks = lax.optimization_barrier((frames, *head_blocks, *embed_blocks))
    for side in range(2):
        for block in range(4):
            far, near = block // 2, block % 2 * 2
            turn = near + (core if side == 0 else 1 - core)
            shards.append((yh + far) % 2 * 4 + (z + 4 - turn) % 4)
    own_blocks = []
    for at, operand in enumerate(blocks):
        far, near = at % 4 // 2, at % 2 * 2
        moves = []
        for a in range(2):
            for k in range(2):
                for h in range(2):
                    for d in range(4):
                        to = ((a + far) % 2, k, (h + far) % 2, (d + near + k) % 4)
                        moves.append(
                            (((a * 2 + k) * 2 + h) * 4 + d, ((to[0] * 2 + to[1]) * 2 + to[2]) * 4 + to[3])
                        )
        own_blocks.append(lax.ppermute(operand, ("yl", "core", "yh", "z"), moves))
    other_blocks = [swap_core(block) for block in own_blocks]
    head_tables = own_blocks[:4] + other_blocks[:4]
    embed_tables = own_blocks[4:] + other_blocks[4:]
    meta = jnp.concatenate(
        [frame_pos[::RUN], jnp.stack([core, ctx, tp] + shards).astype(jnp.int32)]
    )

    depth_cols = lax.dynamic_slice_in_dim(w_depth_in, ctx * 64, 64, 1).T
    depth_half = lax.dynamic_slice_in_dim(w_depth_in, core * 256, 256, 0)
    depth_half = depth_half.reshape(8, 32, 2, 512).transpose(0, 2, 1, 3).reshape(8, 64, 512)
    depth_cols = exchange(
        jnp.concatenate([jnp.broadcast_to(depth_cols[None], (8, 64, 512)), depth_half], axis=1), TP
    )
    depth_piece = depth_cols[:, 64:]
    depth_cols = depth_cols[:, :64]
    fold_cols = lax.dot_general(
        depth_cols, w_out.reshape(256, 8, 512), (((0, 2), (1, 2)), ((), ())),
        preferred_element_type=F32,
    ).astype(BF)

    normed = rms_rows(frames.astype(F32)).astype(BF)
    key = dot(normed, w_key, ((1,), (0,))).astype(BF)
    value = dot(normed, w_value, ((1,), (0,))).astype(BF)
    query = dot(normed, w_query, ((1,), (0,))).astype(BF)

    key_value = jnp.stack(
        [jnp.concatenate([key[:, :HD], value[:, :HD]], 1),
         jnp.concatenate([key[:, HD:], value[:, HD:]], 1)]
    )
    key_value = exchange(
        after(
            jnp.broadcast_to(key_value[None], (8, 2, rows, 2 * HD)).reshape(16, rows, 2 * HD),
            depth_cols,
        ),
        CTX,
    ).reshape(frame_total, 2 * HD)
    query_come = swap_core(jnp.where(first, query[:, HD:], query[:, :HD]))

    own_part, other_part, lse = kernel_call(
        forward_body,
        (
            jax.ShapeDtypeStruct((rows, HD), BF),
            jax.ShapeDtypeStruct((rows, HD), BF),
            jax.ShapeDtypeStruct((8, 128), F32),
        ),
        [pltpu.VMEM((512, HD), BF), pltpu.VMEM((frame_total, 128), jnp.int32)],
        2_000_000_000, 4_000_000, 4,
    )(meta, query, query_come, key_value)
    come_part = swap_core(other_part)
    lse_come = swap_core(lse)
    attended = jnp.where(
        first,
        jnp.concatenate([own_part, come_part], 1),
        jnp.concatenate([come_part, own_part], 1),
    )
    fold = spread(after(fold_cols, key_value), CTX, 16).reshape(1024, 2 * HD)

    base = sum_piece_tp(dot(attended, fold, ((1,), (1,))).astype(BF))
    base = spread(base, TP, 8).reshape(rows, 1024)

    level_ids = jnp.arange(8, dtype=jnp.int32)[None, :]
    target = jnp.sum(jnp.where(level_ids == tp, codes, 0), axis=1, keepdims=True)
    cotangent = jnp.sum(jnp.where(level_ids == tp, loss_grad, 0.0), axis=1, keepdims=True)
    previous = jnp.sum(jnp.where(level_ids + 1 == tp, codes, 0), axis=1, keepdims=True)
    depth_piece = lax.dynamic_index_in_dim(depth_piece, ctx // 2, 0, False)
    depth_piece = depth_piece.reshape(2, 32, 512).transpose(1, 0, 2).reshape(32, 1024)
    previous = after(previous, depth_piece)
    embedded = kernel_call(
        embed_body, jax.ShapeDtypeStruct((rows, 1024), BF), [], 800_000_000, 5_000_000, 10
    )(meta, previous, *embed_tables)
    unit, dlogits, depth_grad, loss = kernel_call(
        head_body,
        (
            jax.ShapeDtypeStruct((rows, 1024), BF),
            jax.ShapeDtypeStruct((rows, 2048), BF),
            jax.ShapeDtypeStruct((rows, 1024), BF),
            jax.ShapeDtypeStruct((rows, 1), F32),
        ),
        [pltpu.VMEM((rows, 2048), F32)],
        2_000_000_000, 6_000_000, 13,
    )(meta, base, embedded, target, cotangent, *head_tables)

    query_all = lax.all_gather(after(query, depth_grad), CTX, axis=0, tiled=True)

    normed_own = []
    cuts = kernel_call(
        cut_body, (jax.ShapeDtypeStruct((rows, 512), BF),) * 8, [], 0, 3_000_000, 2
    )(meta, after(normed, depth_grad))
    for hop, piece in enumerate(cuts):
        moves = [
            (a * 2 + b, (a + hop // 2) % 4 * 2 + (b + hop % 2) % 2)
            for a in range(4) for b in range(2)
        ]
        normed_own.append(lax.ppermute(piece, CHIPS, moves) if hop else piece)

    summed = sum_piece_tp(depth_grad)
    summed = spread(jnp.concatenate([summed, depth_piece], axis=0), TP, 8)
    depth_rows = summed[:, 24:].reshape(256, 1024)
    summed = summed[:, :24].reshape(rows, 1024)

    send = kernel_call(
        send_body,
        jax.ShapeDtypeStruct((16, SEND, 128), BF),
        [pltpu.VMEM((32, 128), F32), pltpu.VMEM((128, 128), F32)],
        400_000_000, 3_000_000, 6,
    )(meta, after(summed, *normed_own[:4]), fold, attended, lse, lse_come)
    come = exchange(send, CTX)

    unit, dlogits = after(unit, send), after(dlogits, send)
    unit_blocks = unit.reshape(rows, 8, 2, 64)
    unit_keep = lax.dynamic_index_in_dim(unit_blocks, core, 2, False).reshape(rows, 512)
    unit_send = lax.dynamic_index_in_dim(unit_blocks, 1 - core, 2, False).reshape(rows, 512)
    head_come = swap_core(dot(unit_send, dlogits, ((0,), (0,))).astype(BF))
    head_part = (dot(unit_keep, dlogits, ((0,), (0,))) + head_come.astype(F32)).astype(BF)
    head_parts = exchange(after(head_part, come).reshape(8, 64, 2048), CHIPS)

    outer_own = total(come[:, OUTER_AT:])
    outer_own = jnp.concatenate([outer_own[:64], outer_own[64:]], axis=1)
    outer = gather_wide(outer_own, CTX)

    grads = kernel_call(
        backward_body,
        jax.ShapeDtypeStruct((frame_total, 3 * HD), BF),
        [pltpu.VMEM((frame_total, 2 * HD), BF)] * 6
        + [pltpu.VMEM((frame_total, HD), F32)] * 3
        + [pltpu.SemaphoreType.DMA((2,))],
        25_000_000_000, 8_000_000, 4, 2,
    )(meta, after(come, outer_own, head_part), query_all, key_value)
    head_sum = total(after(head_parts, grads)).astype(BF)
    normed_other = [swap_core(piece) for piece in normed_own]
    weights_keep, weights_send = kernel_call(
        weight_body,
        (jax.ShapeDtypeStruct((256, 3 * HD), F32), jax.ShapeDtypeStruct((256, 3 * HD), F32)),
        [], 1_200_000_000, 6_000_000, 18,
    )(meta, grads, *normed_own, *normed_other)
    weights_come = swap_core(weights_send)
    grad_query, grad_key, grad_value = kernel_call(
        join_body, (jax.ShapeDtypeStruct((256, 2 * HD), F32),) * 3, [], 0, 2_000_000, 3
    )(meta, weights_keep, weights_come)

    grad_out = kernel_call(
        grad_out_body, jax.ShapeDtypeStruct((2 * HD, 256), F32), [], 100_000_000, 2_000_000, 3
    )(meta, outer, depth_rows)
    depth_part = dot(outer_own.astype(BF), w_out, ((1,), (0,))).astype(BF)
    loss_row = jnp.pad(thirds(loss[:, 0]).reshape(1, 576), ((0, 15), (0, 192)))
    tail = jnp.concatenate(
        [
            jnp.concatenate(
                [depth_part.reshape(64, 8, 512), head_sum.reshape(64, 8, 256)], axis=2
            ).transpose(1, 0, 2),
            jnp.broadcast_to(loss_row[None], (8, 16, 768)),
        ],
        axis=1,
    )
    tail = exchange(tail, TP)
    grad_depth_in = total(tail[:, :64, :512]).T
    grad_head = tail[:, :64, 512:].astype(F32)
    token_loss = total(tail[:, 64, :576].reshape(8, 3, rows).transpose(1, 2, 0))
    return (token_loss, grad_query, grad_key, grad_value, grad_out, grad_depth_in, grad_head)


def solution(mesh):
    fine = Mesh(mesh.devices.reshape(4, 2, 2, 2, 4), ALL)
    in_specs = (
        P(CTX, None),
        P(),
        P(CTX, None),
        P(CTX, None),
        P(None, TP),
        P(None, TP),
        P(None, TP),
        P(TP, None),
        P(TP, None),
        P(None, TP, None),
        P(None, None, TP),
    )
    out_specs = (
        P(CTX, None),
        P(CTX, TP),
        P(CTX, TP),
        P(CTX, TP),
        P(TP, CTX),
        P(TP, CTX),
        P(None, CTX, TP),
    )
    return jax.shard_map(
        per_device, mesh=fine, in_specs=in_specs, out_specs=out_specs, check_vma=False
    )
```
